32 devices in a mesh: section: 2 (over core), dp: 16 (over z, y, x).
Axes of the slice: x: 2, y: 2, z: 4, core: 2. Of those that a mesh axis runs over, the one named last changes fastest.
Arguments:
- inputs: bfloat16 [2, 1, 128, 128, 512], P(None, None, 'dp'), may hold values from -64 to 64
- cotangent: bfloat16 [2, 1, 128, 128, 512], P(None, None, 'dp'), may hold values from -6 to 6
- shapes: int32 [2, 2], replicated, may hold values from 96 to 128, as said below
- local_to_local: bfloat16 [2, 2, 9, 128, 128], P('section'), may hold values from -0.09375 to 0.09375
- global_to_local: bfloat16 [2, 2, 9, 384, 128], P('section'), may hold values from -0.09375 to 0.09375
- local_to_global: bfloat16 [2, 2, 9, 128, 384], P('section'), may hold values from -0.1875 to 0.1875
- spec_reduce: bfloat16 [2, 2, 384, 192], P('section'), may hold values from -0.3125 to 0.3125
- spec_mix: bfloat16 [2, 2, 384, 384], P('section'), may hold values from -0.3125 to 0.3125
- spec_expand: bfloat16 [2, 2, 192, 384], P('section'), may hold values from -0.4375 to 0.4375
- norm_gains: float32 [2, 2, 1088], P('section'), may hold values from 0.1 to 1.9
- norm_biases: float32 [2, 2, 1088], P('section'), may hold values from -3 to 3
- run_means: float32 [2, 2, 1088], P('section'), may hold values from -3 to 3
- run_vars: float32 [2, 2, 1088], P('section'), may hold values from 0.5 to 2
Outputs:
- block_outputs: bfloat16 [2, 2, 1, 128, 128, 512], P('section', None, None, 'dp')
- input_grads: float32 [2, 2, 1, 128, 128, 512], P('section', None, None, 'dp')
- grad_local_to_local: float32 [2, 2, 9, 128, 128], P('section')
- grad_global_to_local: float32 [2, 2, 9, 384, 128], P('section')
- grad_local_to_global: float32 [2, 2, 9, 128, 384], P('section')
- grad_spec_reduce: float32 [2, 2, 384, 192], P('section')
- grad_spec_mix: float32 [2, 2, 384, 384], P('section')
- grad_spec_expand: float32 [2, 2, 192, 384], P('section')
- grad_gains: float32 [2, 2, 1088], P('section')
- grad_biases: float32 [2, 2, 1088], P('section')
- new_means: float32 [2, 2, 1088], P('section')
- new_vars: float32 [2, 2, 1088], P('section')
The draws below stay inside these ranges and needn't reach their ends.
Inputs may be any that keep to these rules, and one draw needn't show every extreme that they name: `shapes`: each row is (height, width) of all maps of a micro-batch, both multiples of 8; some micro-batch has height 128.
All inputs are finite; a program needn't handle non-finite values.
Results may differ from the reference program's by a relative error of at most 0.025.
Values may be sent and summed in bfloat16 or wider, within the bound.
A program may use at most 256 MiB of HBM per device.

```python
import jax
import jax.numpy as jnp
from jax import lax

CL = 128
CG = 384
CS = 192
C = 512
NORM = 1088
LONG = 128
SHORT = 96
MAPS = 1
MICRO = 2
FP = 80


def draw_inputs(key, part):
    key = jax.random.fold_in(key, 11)
    noise_key, channel_key = jax.random.split(key, 2)
    row_pos = jnp.arange(LONG, dtype=jnp.float32)
    row_scale = jnp.exp(jnp.log(3.0) * (1.0 - row_pos / (LONG - 1.0)))
    offsets = 0.4 * jax.random.normal(channel_key, (C,), jnp.float32)
    noise_vals = jax.random.normal(noise_key, (MICRO, MAPS, LONG, LONG, C), jnp.float32)
    values = (noise_vals + offsets) * row_scale[None, None, :, None, None]
    return jnp.clip(values, -64.0, 64.0).astype(jnp.bfloat16)


def draw_shapes(key, part):
    key = jax.random.fold_in(key, 23)
    height_key, width_key, pick_key = jax.random.split(key, 3)
    steps = (LONG - SHORT) // 8 + 1
    heights = SHORT + 8 * jax.random.randint(height_key, (MICRO,), 0, steps)
    widths = SHORT + 8 * jax.random.randint(width_key, (MICRO,), 0, steps)
    forced = jax.random.randint(pick_key, (), 0, MICRO)
    heights = jnp.where(jnp.arange(MICRO) == forced, LONG, heights)
    return jnp.stack([heights, widths], axis=1).astype(jnp.int32)


def shard_levels(own_key, shape, cuts, least, high):
    factor_of = 1.0
    for dim, parts in cuts:
        draws = jax.random.uniform(jax.random.fold_in(jax.random.fold_in(own_key, 6), dim), (parts,), jnp.float32, least / len(cuts), high / len(cuts))
        factor_of = factor_of * jnp.repeat(jnp.exp(draws), shape[dim] // parts).reshape((-1,) + (1,) * (len(shape) - 1 - dim))
    return factor_of


def bell_draw(own_key, dims, spread, bound, pieces=(), held_as=jnp.bfloat16):
    level = shard_levels(own_key, dims, pieces, -0.22, 0.18) if pieces else 1.0
    array = jax.random.normal(own_key, dims, jnp.float32) * spread * level
    return jnp.minimum(jnp.maximum(array, -bound), bound).astype(held_as)


def setup_inputs(seed: int = 0) -> dict:
    streams_of = jax.random.split(jax.random.key(seed), 14)
    return {
        "inputs": draw_inputs(jax.random.fold_in(streams_of[13], 71), 0),
        "cotangent": bell_draw(streams_of[1], (MICRO, MAPS, LONG, LONG, C), 1.0, 6.0, ((2, 16),)),
        "shapes": draw_shapes(jax.random.fold_in(streams_of[13], 71), 0),
        "local_to_local": bell_draw(streams_of[3], (2, 2, 9, CL, CL), (9 * C) ** -0.5, 0.09375, ((0, 2),)),
        "global_to_local": bell_draw(streams_of[4], (2, 2, 9, CG, CL), (9 * C) ** -0.5, 0.09375, ((0, 2),)),
        "local_to_global": bell_draw(streams_of[5], (2, 2, 9, CL, CG), (9 * CL) ** -0.5, 0.1875, ((0, 2),)),
        "spec_reduce": bell_draw(streams_of[6], (2, 2, CG, CS), CG ** -0.5, 0.3125, ((0, 2),)),
        "spec_mix": bell_draw(streams_of[7], (2, 2, 2 * CS, 2 * CS), (2 * CS) ** -0.5, 0.3125, ((0, 2),)),
        "spec_expand": bell_draw(streams_of[8], (2, 2, CS, CG), CS ** -0.5, 0.4375, ((0, 2),)),
        "norm_gains": jnp.clip(1.0 + 0.18 * jax.random.normal(streams_of[9], (2, 2, NORM), jnp.float32), 0.1, 1.9),
        "norm_biases": bell_draw(streams_of[10], (2, 2, NORM), 0.5, 3.0, ((0, 2),), jnp.float32),
        "run_means": bell_draw(streams_of[11], (2, 2, NORM), 0.5, 3.0, ((0, 2),), jnp.float32),
        "run_vars": jnp.clip(0.5 + 1.5 * jax.random.uniform(streams_of[12], (2, 2, NORM), jnp.float32) ** shard_levels(streams_of[12], (2, 2, NORM), ((0, 2),), -0.2, 0.2), 0.5, 2.0),
    }


EPSILON = 1e-05
MOMENTUM = 0.1
PRECISE = lax.Precision.HIGHEST

@jax.custom_vjp
def low(v):
    return lax.optimization_barrier(v.astype(jnp.bfloat16)).astype(jnp.float32)

@jax.custom_vjp
def low_back(v):
    return v

def low_keep(v):
    return (low(v), None)

def low_pass(kept, grad):
    return (grad,)

def back_keep(v):
    return (v, None)

def back_low(kept, grad):
    return (low(grad),)
low.defvjp(low_keep, low_pass)
low_back.defvjp(back_keep, back_low)

def dft_tables(height, width, long_side, freq_total):
    position = jnp.arange(long_side, dtype=jnp.int32)
    frequency = jnp.arange(freq_total, dtype=jnp.int32)
    half_width = width // 2
    width_real = width.astype(jnp.float32)
    height_real = height.astype(jnp.float32)
    width_phase = position[:, None] * frequency[None, :] % width
    width_angle = 2.0 * jnp.pi / width_real * width_phase.astype(jnp.float32)
    width_valid = ((position[:, None] < width) & (frequency[None, :] <= half_width)).astype(jnp.float32)
    width_scale = lax.rsqrt(width_real)
    fwd_cos = jnp.cos(width_angle) * width_scale * width_valid
    fwd_sin = -jnp.sin(width_angle) * width_scale * width_valid
    edge_freq = (frequency == 0) | (frequency == half_width)
    freq_weight = jnp.where(edge_freq, 1.0, 2.0).astype(jnp.float32)
    inv_cos = freq_weight[:, None] * fwd_cos.T
    inv_sin = freq_weight[:, None] * fwd_sin.T
    height_phase = position[:, None] * position[None, :] % height
    height_angle = 2.0 * jnp.pi / height_real * height_phase.astype(jnp.float32)
    height_valid = ((position[:, None] < height) & (position[None, :] < height)).astype(jnp.float32)
    height_scale = lax.rsqrt(height_real)
    row_cos = jnp.cos(height_angle) * height_scale * height_valid
    row_sin = jnp.sin(height_angle) * height_scale * height_valid
    return (fwd_cos, fwd_sin, inv_cos, inv_sin, row_cos, row_sin)

def geometry(shape_row):
    height = shape_row[0]
    width = shape_row[1]
    position = jnp.arange(LONG, dtype=jnp.int32)
    frequency = jnp.arange(FP, dtype=jnp.int32)
    rows_ok = position < height
    pix_mask = (rows_ok[:, None] & (position[None, :] < width)).astype(jnp.float32)[None, :, :, None]
    freq_mask = (rows_ok[:, None] & (frequency[None, :] <= width // 2)).astype(jnp.float32)[None, :, :, None]
    pix_count = (MAPS * height * width).astype(jnp.float32)
    spec_count = (MAPS * height * (width // 2 + 1)).astype(jnp.float32)
    return (pix_mask, freq_mask, pix_count, spec_count, dft_tables(height, width, LONG, FP))

def conv_same(entry, kernel):
    shaped = kernel.reshape(3, 3, kernel.shape[1], kernel.shape[2])
    return lax.conv_general_dilated(entry, shaped, (1, 1), ((1, 1), (1, 1)), dimension_numbers=('NHWC', 'HWIO', 'NHWC'), precision=PRECISE)

def width_forward(entry, table):
    return jnp.einsum('mrwc,wf->mrfc', entry, table, precision=PRECISE)

def width_inverse(entry, table):
    return jnp.einsum('mrfc,fw->mrwc', entry, table, precision=PRECISE)

def height_apply(table, entry):
    return jnp.einsum('kn,mnfc->mkfc', table, entry, precision=PRECISE)

def height_adjoint(table, entry):
    return jnp.einsum('kn,mkfc->mnfc', table, entry, precision=PRECISE)

def rows_forward(row_cos, row_sin, entry):
    half_ch = entry.shape[-1] // 2
    real_in = entry[..., :half_ch]
    imag_in = entry[..., half_ch:]
    real_out = height_apply(row_cos, real_in) + height_apply(row_sin, imag_in)
    imag_out = height_apply(row_cos, imag_in) - height_apply(row_sin, real_in)
    return jnp.concatenate([real_out, imag_out], axis=-1)

def rows_inverse(row_cos, row_sin, entry):
    half_ch = entry.shape[-1] // 2
    real_in = entry[..., :half_ch]
    imag_in = entry[..., half_ch:]
    real_out = height_adjoint(row_cos, real_in) - height_adjoint(row_sin, imag_in)
    imag_out = height_adjoint(row_cos, imag_in) + height_adjoint(row_sin, real_in)
    return jnp.concatenate([real_out, imag_out], axis=-1)

def norm_stats(entry, weight, count_now):
    masked = entry * weight
    mean_val = lax.optimization_barrier(jnp.sum(masked, axis=(0, 1, 2))) / count_now
    var_val = lax.optimization_barrier(jnp.sum(masked * entry, axis=(0, 1, 2))) / count_now - mean_val * mean_val
    return ((entry - mean_val) * lax.rsqrt(var_val + EPSILON), mean_val, var_val)

def ffc_layer(layer_in, geometry_now, params, gain_vec, bias_vec):
    pix_mask, freq_mask, pix_count, spec_count, tables = geometry_now
    fwd_cos, fwd_sin, inv_cos, inv_sin, row_cos, row_sin = tables
    local_kernel, lift_kernel, reduce_kernel, mix_kernel, expand_kernel = params
    acts_low = low(layer_in)
    reduced = low_back(jnp.einsum('mrwc,cd->mrwd', acts_low[..., CL:], reduce_kernel, precision=PRECISE))
    normed_one, mean_one, var_one = norm_stats(reduced, pix_mask, pix_count)
    upper_spec = jax.nn.silu(normed_one * gain_vec[:CS] + bias_vec[:CS]) * pix_mask
    spectrum = jnp.concatenate([width_forward(upper_spec, fwd_cos), width_forward(upper_spec, fwd_sin)], axis=-1)
    spectrum = low_back(low(spectrum))
    spectra = low(rows_forward(row_cos, row_sin, spectrum))
    mixed = low_back(jnp.einsum('mkfc,cd->mkfd', spectra, mix_kernel, precision=PRECISE))
    normed_two, mean_two, var_two = norm_stats(mixed, freq_mask, spec_count)
    activated = jax.nn.silu(normed_two * gain_vec[CS:3 * CS] + bias_vec[CS:3 * CS]) * freq_mask
    inverse = low_back(low(rows_inverse(row_cos, row_sin, activated)))
    half_ch = inverse.shape[-1] // 2
    restored = width_inverse(inverse[..., :half_ch], inv_cos) + width_inverse(inverse[..., half_ch:], inv_sin)
    summed = low(upper_spec + restored)
    spec_out = jnp.einsum('mrwc,cd->mrwd', summed, expand_kernel, precision=PRECISE)
    local_out = low_back(conv_same(acts_low, local_kernel))
    global_out = low_back(conv_same(acts_low[..., :CL], lift_kernel) + spec_out)
    normed_loc, mean_loc, var_loc = norm_stats(local_out, pix_mask, pix_count)
    normed_glo, mean_glo, var_glo = norm_stats(global_out, pix_mask, pix_count)
    pre_loc = normed_loc * gain_vec[3 * CS:3 * CS + CL] + bias_vec[3 * CS:3 * CS + CL]
    pre_glo = normed_glo * gain_vec[3 * CS + CL:] + bias_vec[3 * CS + CL:]
    result = jnp.concatenate([jax.nn.silu(pre_loc), jax.nn.silu(pre_glo)], axis=-1) * pix_mask
    means_layer = jnp.concatenate([mean_one, mean_two, mean_loc, mean_glo])
    vars_layer = jnp.concatenate([var_one, var_two, var_loc, var_glo])
    return (result, (means_layer, vars_layer))

def layer_params(kernel_params, layer_pos):
    local_kernel = jnp.concatenate([kernel_params[0][layer_pos], kernel_params[1][layer_pos]], axis=1)
    return (local_kernel, kernel_params[2][layer_pos], kernel_params[3][layer_pos], kernel_params[4][layer_pos], kernel_params[5][layer_pos])

def ffc_block(block_in, geometry_now, params):
    base = block_in * geometry_now[0]
    kernel_params = params[:6]
    first_out, first_stats = jax.checkpoint(ffc_layer)(base, geometry_now, layer_params(kernel_params, 0), params[6][0], params[7][0])
    second_out, second_stats = jax.checkpoint(ffc_layer)(first_out, geometry_now, layer_params(kernel_params, 1), params[6][1], params[7][1])
    return (second_out + base, (first_stats, second_stats))

def running_update(mean_now, var_now, layer_stats, geometry_now):
    pix_count = geometry_now[2]
    spec_count = geometry_now[3]
    counts = jnp.concatenate([jnp.full((CS,), pix_count, jnp.float32), jnp.full((2 * CS,), spec_count, jnp.float32), jnp.full((CL + CG,), pix_count, jnp.float32)])
    batch_means = jnp.stack([layer_stats[0][0], layer_stats[1][0]])
    batch_vars = jnp.stack([layer_stats[0][1], layer_stats[1][1]])
    new_mean = (1.0 - MOMENTUM) * mean_now + MOMENTUM * batch_means
    new_var = (1.0 - MOMENTUM) * var_now + MOMENTUM * batch_vars * counts / (counts - 1.0)
    return (new_mean, new_var)

def run_section(section_in, geometry_all, params, run_mean, run_var):

    def advance(carry_now, scan_items):
        mean_now, var_now = carry_now
        block_in, geometry_now = scan_items
        block_out, layer_stats = ffc_block(block_in, geometry_now, params)
        updated = running_update(mean_now, var_now, layer_stats, geometry_now)
        return (updated, low(block_out))
    carry_end, outputs = lax.scan(advance, (run_mean, run_var), (section_in, geometry_all))
    return (outputs, carry_end)

def reference(inputs, cotangent, shapes, local_to_local, global_to_local, local_to_global, spec_reduce, spec_mix, spec_expand, norm_gains, norm_biases, run_means, run_vars):
    geometry_all = jax.vmap(geometry)(shapes)
    every_param = (local_to_local, global_to_local, local_to_global, spec_reduce, spec_mix, spec_expand, norm_gains, norm_biases)
    first_params = tuple((array_in[0].astype(jnp.float32) for array_in in every_param))
    second_params = tuple((array_in[1].astype(jnp.float32) for array_in in every_param))

    def first_section(section_in, params):
        return run_section(section_in, geometry_all, params, run_means[0], run_vars[0])

    def second_section(section_in, params):
        return run_section(low_back(section_in), geometry_all, params, run_means[1], run_vars[1])
    hidden, first_back, first_aux = jax.vjp(first_section, inputs.astype(jnp.float32), first_params, has_aux=True)
    final, second_back, second_aux = jax.vjp(second_section, hidden, second_params, has_aux=True)
    grad_hidden, second_grads = second_back(cotangent.astype(jnp.float32))
    grad_inputs, first_grads = first_back(grad_hidden)

    def paired(position):
        return jnp.stack([first_grads[position], second_grads[position]])
    return (jnp.stack([hidden, final]).astype(jnp.bfloat16), jnp.stack([grad_inputs, grad_hidden]), paired(0), paired(1), paired(2), paired(3), paired(4), paired(5), paired(6), paired(7), jnp.stack([first_aux[0], second_aux[0]]), jnp.stack([first_aux[1], second_aux[1]]))
```

```python
import jax
import jax.numpy as jnp
from jax import lax
from jax.experimental import pallas as pl
from jax.experimental.pallas import tpu as pltpu
from jax.sharding import PartitionSpec as P

CL = 128
CG = 384
CS = 192
LONG = 128


EPSILON = 1e-05
MOMENTUM = 0.1
PRECISE = lax.Precision.HIGHEST


def with_halo(block, sides, width):
    for axis, dim in sides:
        count = lax.axis_size(axis)
        forward = [(i, i + 1) for i in range(count - 1)]
        backward = [(target, source) for source, target in forward]
        low = lax.ppermute(
            lax.slice_in_dim(block, block.shape[dim] - width, None, axis=dim), axis, forward
        )
        high = lax.ppermute(lax.slice_in_dim(block, 0, width, axis=dim), axis, backward)
        block = jnp.concatenate([low, block, high], axis=dim)
    return block


def from_behind(value, axis, steps):
    count = lax.axis_size(axis)
    first, last = (max(0, -steps), min(count, count - steps))
    return lax.ppermute(value, axis, [(source, source + steps) for source in range(first, last)])


def dft_tables(height, width, long_side, freq_total):
    position = jnp.arange(long_side, dtype=jnp.int32)
    frequency = jnp.arange(freq_total, dtype=jnp.int32)
    half_width = width // 2
    width_real = width.astype(jnp.float32)
    height_real = height.astype(jnp.float32)
    width_phase = position[:, None] * frequency[None, :] % width
    width_angle = 2.0 * jnp.pi / width_real * width_phase.astype(jnp.float32)
    width_valid = ((position[:, None] < width) & (frequency[None, :] <= half_width)).astype(
        jnp.float32
    )
    width_scale = lax.rsqrt(width_real)
    fwd_cos = jnp.cos(width_angle) * width_scale * width_valid
    fwd_sin = -jnp.sin(width_angle) * width_scale * width_valid
    edge_freq = (frequency == 0) | (frequency == half_width)
    freq_weight = jnp.where(edge_freq, 1.0, 2.0).astype(jnp.float32)
    inv_cos = freq_weight[:, None] * fwd_cos.T
    inv_sin = freq_weight[:, None] * fwd_sin.T
    height_phase = position[:, None] * position[None, :] % height
    height_angle = 2.0 * jnp.pi / height_real * height_phase.astype(jnp.float32)
    height_valid = ((position[:, None] < height) & (position[None, :] < height)).astype(jnp.float32)
    height_scale = lax.rsqrt(height_real)
    row_cos = jnp.cos(height_angle) * height_scale * height_valid
    row_sin = jnp.sin(height_angle) * height_scale * height_valid
    return (fwd_cos, fwd_sin, inv_cos, inv_sin, row_cos, row_sin)


def geometry(shape_row, band_index, band_size, freq_total, freq_local, map_count):
    height = shape_row[0]
    width = shape_row[1]
    position = jnp.arange(LONG, dtype=jnp.int32)
    band_rows = band_index * band_size + jnp.arange(band_size, dtype=jnp.int32)
    pix_mask = ((band_rows[:, None] < height) & (position[None, :] < width)).astype(jnp.float32)[
        None, :, :, None
    ]
    local_freq = band_index * freq_local + jnp.arange(freq_local, dtype=jnp.int32)
    freq_mask = ((position[:, None] < height) & (local_freq[None, :] <= width // 2)).astype(
        jnp.float32
    )[None, :, :, None]
    pix_count = (map_count * height * width).astype(jnp.float32)
    spec_count = (map_count * height * (width // 2 + 1)).astype(jnp.float32)
    return (pix_mask, freq_mask, pix_count, spec_count, dft_tables(height, width, LONG, freq_total))


def conv_rows(padded, kernel):
    shaped = kernel.reshape(3, 3, kernel.shape[1], kernel.shape[2])
    return lax.conv_general_dilated(
        padded,
        shaped,
        (1, 1),
        "VALID",
        dimension_numbers=("NHWC", "HWIO", "NHWC"),
        preferred_element_type=jnp.float32,
    )


def flipped(kernel):
    shaped = kernel.reshape(3, 3, kernel.shape[1], kernel.shape[2])[::-1, ::-1]
    return jnp.swapaxes(shaped, 2, 3).reshape(9, kernel.shape[2], kernel.shape[1])


def kernel_grad(padded, grad_out, band_size, width):
    tap_grads = []
    for row_tap in range(3):
        for col_tap in range(3):
            window = padded[:, row_tap : row_tap + band_size, col_tap : col_tap + width, :]
            tap_grads.append(
                jnp.einsum("mrwi,mrwo->io", window, grad_out, preferred_element_type=jnp.float32)
            )
    return jnp.stack(tap_grads)


def width_forward(entry, table):
    return jnp.einsum("mrwc,wf->mrfc", entry, table, precision=PRECISE)


def width_forward_adj(entry, table):
    return jnp.einsum("mrfc,wf->mrwc", entry, table, precision=PRECISE)


def width_inverse(entry, table):
    return jnp.einsum("mrfc,fw->mrwc", entry, table, precision=PRECISE)


def width_inverse_adj(entry, table):
    return jnp.einsum("mrwc,fw->mrfc", entry, table, precision=PRECISE)


def height_apply(table, entry):
    return jnp.einsum("kn,mnfc->mkfc", table, entry, precision=PRECISE)


def height_adjoint(table, entry):
    return jnp.einsum("kn,mkfc->mnfc", table, entry, precision=PRECISE)


def rows_forward(row_cos, row_sin, entry):
    half_ch = entry.shape[-1] // 2
    real_in = entry[..., :half_ch]
    imag_in = entry[..., half_ch:]
    real_out = height_apply(row_cos, real_in) + height_apply(row_sin, imag_in)
    imag_out = height_apply(row_cos, imag_in) - height_apply(row_sin, real_in)
    return jnp.concatenate([real_out, imag_out], axis=-1)


def rows_inverse(row_cos, row_sin, entry):
    half_ch = entry.shape[-1] // 2
    real_in = entry[..., :half_ch]
    imag_in = entry[..., half_ch:]
    real_out = height_adjoint(row_cos, real_in) - height_adjoint(row_sin, imag_in)
    imag_out = height_adjoint(row_cos, imag_in) + height_adjoint(row_sin, real_in)
    return jnp.concatenate([real_out, imag_out], axis=-1)


def split_pairs(totals, widths):
    pairs = []
    offset = 0
    for lead_width, tail_width in zip(widths[0::2], widths[1::2]):
        lead_part = totals[offset : offset + lead_width]
        tail_part = totals[offset + lead_width : offset + lead_width + tail_width]
        pairs.append((lead_part, tail_part))
        offset = offset + lead_width + tail_width
    return pairs


def moments(entries, weights):
    pieces = []
    for entry, weight in zip(entries, weights):
        masked = entry * weight
        pieces.append(jnp.sum(masked, axis=(0, 1, 2)))
        pieces.append(jnp.sum(masked * entry, axis=(0, 1, 2)))
    totals = lax.psum(jnp.concatenate(pieces), "dp")
    return split_pairs(totals, [piece.shape[0] for piece in pieces])


def grad_moments(grads_in, normed_in):
    pieces = []
    for grad_pre, normed in zip(grads_in, normed_in):
        pieces.append(jnp.sum(grad_pre, axis=(0, 1, 2)))
        pieces.append(jnp.sum(grad_pre * normed, axis=(0, 1, 2)))
    totals = lax.psum(jnp.concatenate(pieces), "dp")
    return split_pairs(totals, [piece.shape[0] for piece in pieces])


def normalize(entry, sum_pair, count_now):
    mean_val = sum_pair[0] / count_now
    var_val = sum_pair[1] / count_now - mean_val * mean_val
    inv_std = lax.rsqrt(var_val + EPSILON)
    return ((entry - mean_val) * inv_std, inv_std, mean_val, var_val)


def silu_slope(pre_act):
    sigmoid_val = jax.nn.sigmoid(pre_act)
    return sigmoid_val * (1.0 + pre_act * (1.0 - sigmoid_val))


def norm_backward(grad_pre, normed, inv_std, gain_part, sum_pair, count_now, weight):
    return (
        weight
        * inv_std
        * gain_part
        * (grad_pre - sum_pair[0] / count_now - normed * sum_pair[1] / count_now)
    )


def layer_forward(layer_in, geometry_now, kernels, gain_vec, bias_vec):
    pix_mask, freq_mask, pix_count, spec_count, tables = geometry_now
    fwd_cos, fwd_sin, inv_cos, inv_sin, row_cos, row_sin = tables
    local_kernel, lift_kernel, reduce_kernel, mix_kernel, expand_kernel = kernels
    acts_low = layer_in.astype(jnp.bfloat16)
    padded = with_halo(acts_low, (("dp", 1),), 1)
    padded = jnp.pad(padded, ((0, 0), (0, 0), (1, 1), (0, 0)))
    local_out = conv_rows(padded, local_kernel)
    global_conv = conv_rows(padded[..., :CL], lift_kernel)
    reduced = jnp.einsum(
        "mrwc,cd->mrwd", acts_low[..., CL:], reduce_kernel, preferred_element_type=jnp.float32
    )
    one_stats = moments([reduced], [pix_mask])[0]
    normed_one, inv_one, mean_one, var_one = normalize(reduced, one_stats, pix_count)
    pre_one = normed_one * gain_vec[:CS] + bias_vec[:CS]
    upper_spec = jax.nn.silu(pre_one) * pix_mask
    spectrum = jnp.concatenate(
        [width_forward(upper_spec, fwd_cos), width_forward(upper_spec, fwd_sin)], axis=-1
    ).astype(jnp.bfloat16)
    columns = lax.all_to_all(spectrum, "dp", split_axis=2, concat_axis=1, tiled=True).astype(
        jnp.float32
    )
    spectra = rows_forward(row_cos, row_sin, columns).astype(jnp.bfloat16)
    mixed = jnp.einsum("mkfc,cd->mkfd", spectra, mix_kernel, preferred_element_type=jnp.float32)
    two_stats = moments([mixed], [freq_mask])[0]
    normed_two, inv_two, mean_two, var_two = normalize(mixed, two_stats, spec_count)
    pre_two = normed_two * gain_vec[CS : 3 * CS] + bias_vec[CS : 3 * CS]
    activated = jax.nn.silu(pre_two) * freq_mask
    inverse = rows_inverse(row_cos, row_sin, activated).astype(jnp.bfloat16)
    returned = lax.all_to_all(inverse, "dp", split_axis=1, concat_axis=2, tiled=True).astype(
        jnp.float32
    )
    half_ch = returned.shape[-1] // 2
    restored = width_inverse(returned[..., :half_ch], inv_cos) + width_inverse(
        returned[..., half_ch:], inv_sin
    )
    summed = (upper_spec + restored).astype(jnp.bfloat16)
    spec_out = jnp.einsum(
        "mrwc,cd->mrwd", summed, expand_kernel, preferred_element_type=jnp.float32
    )
    global_out = global_conv + spec_out
    loc_stats, glo_stats = moments([local_out, global_out], [pix_mask, pix_mask])
    normed_loc, inv_loc, mean_loc, var_loc = normalize(local_out, loc_stats, pix_count)
    normed_glo, inv_glo, mean_glo, var_glo = normalize(global_out, glo_stats, pix_count)
    pre_loc = normed_loc * gain_vec[3 * CS : 3 * CS + CL] + bias_vec[3 * CS : 3 * CS + CL]
    pre_glo = normed_glo * gain_vec[3 * CS + CL :] + bias_vec[3 * CS + CL :]
    result = jnp.concatenate([jax.nn.silu(pre_loc), jax.nn.silu(pre_glo)], axis=-1) * pix_mask
    stored = (
        padded,
        pre_one,
        normed_one,
        inv_one,
        spectra,
        pre_two,
        normed_two,
        inv_two,
        summed,
        pre_loc,
        normed_loc,
        inv_loc,
        pre_glo,
        normed_glo,
        inv_glo,
    )
    means_layer = jnp.concatenate([mean_one, mean_two, mean_loc, mean_glo])
    vars_layer = jnp.concatenate([var_one, var_two, var_loc, var_glo])
    return (result, stored, (means_layer, vars_layer))


def layer_backward(grad_result, stored, geometry_now, kernels, gain_vec):
    (
        padded,
        pre_one,
        normed_one,
        inv_one,
        spectra,
        pre_two,
        normed_two,
        inv_two,
        summed,
        pre_loc,
        normed_loc,
        inv_loc,
        pre_glo,
        normed_glo,
        inv_glo,
    ) = stored
    pix_mask, freq_mask, pix_count, spec_count, tables = geometry_now
    fwd_cos, fwd_sin, inv_cos, inv_sin, row_cos, row_sin = tables
    local_kernel, lift_kernel, reduce_kernel, mix_kernel, expand_kernel = kernels
    band_size = pre_one.shape[1]
    width = pre_one.shape[2]
    grad_loc = grad_result[..., :CL] * pix_mask * silu_slope(pre_loc)
    grad_glo = grad_result[..., CL:] * pix_mask * silu_slope(pre_glo)
    loc_pair, glo_pair = grad_moments([grad_loc, grad_glo], [normed_loc, normed_glo])
    d_local = norm_backward(
        grad_loc, normed_loc, inv_loc, gain_vec[3 * CS : 3 * CS + CL], loc_pair, pix_count, pix_mask
    ).astype(jnp.bfloat16)
    d_global = norm_backward(
        grad_glo, normed_glo, inv_glo, gain_vec[3 * CS + CL :], glo_pair, pix_count, pix_mask
    ).astype(jnp.bfloat16)
    grad_expand = jnp.einsum("mrwc,mrwd->cd", summed, d_global, preferred_element_type=jnp.float32)
    d_summed = jnp.einsum(
        "mrwd,cd->mrwc", d_global, expand_kernel, preferred_element_type=jnp.float32
    )
    d_returned = jnp.concatenate(
        [width_inverse_adj(d_summed, inv_cos), width_inverse_adj(d_summed, inv_sin)], axis=-1
    ).astype(jnp.bfloat16)
    d_inverse = lax.all_to_all(d_returned, "dp", split_axis=2, concat_axis=1, tiled=True).astype(
        jnp.float32
    )
    d_activated = rows_forward(row_cos, row_sin, d_inverse)
    grad_two = d_activated * freq_mask * silu_slope(pre_two)
    two_pair = grad_moments([grad_two], [normed_two])[0]
    d_mixed = norm_backward(
        grad_two, normed_two, inv_two, gain_vec[CS : 3 * CS], two_pair, spec_count, freq_mask
    ).astype(jnp.bfloat16)
    grad_mix = jnp.einsum("mkfc,mkfd->cd", spectra, d_mixed, preferred_element_type=jnp.float32)
    d_spectra = jnp.einsum("mkfd,cd->mkfc", d_mixed, mix_kernel, preferred_element_type=jnp.float32)
    d_columns = rows_inverse(row_cos, row_sin, d_spectra).astype(jnp.bfloat16)
    d_spectrum = lax.all_to_all(d_columns, "dp", split_axis=1, concat_axis=2, tiled=True).astype(
        jnp.float32
    )
    half_ch = d_spectrum.shape[-1] // 2
    d_upper = (
        d_summed
        + width_forward_adj(d_spectrum[..., :half_ch], fwd_cos)
        + width_forward_adj(d_spectrum[..., half_ch:], fwd_sin)
    )
    grad_one = d_upper * pix_mask * silu_slope(pre_one)
    one_pair = grad_moments([grad_one], [normed_one])[0]
    d_reduced = norm_backward(
        grad_one, normed_one, inv_one, gain_vec[:CS], one_pair, pix_count, pix_mask
    ).astype(jnp.bfloat16)
    acts_low = padded[:, 1:-1, 1:-1, :]
    grad_reduce = jnp.einsum(
        "mrwc,mrwd->cd", acts_low[..., CL:], d_reduced, preferred_element_type=jnp.float32
    )
    d_global_in = jnp.einsum(
        "mrwd,cd->mrwc", d_reduced, reduce_kernel, preferred_element_type=jnp.float32
    )
    grad_outs = jnp.concatenate([d_local, d_global], axis=-1)
    grad_pad = with_halo(grad_outs, (("dp", 1),), 1)
    grad_pad = jnp.pad(grad_pad, ((0, 0), (0, 0), (1, 1), (0, 0)))
    d_acts = conv_rows(grad_pad[..., :CL], flipped(local_kernel))
    d_lift = conv_rows(grad_pad[..., CL:], flipped(lift_kernel))
    d_input = d_acts + jnp.concatenate([d_lift, d_global_in], axis=-1)
    grad_local_kernel = kernel_grad(padded, d_local, band_size, width)
    grad_lift = kernel_grad(padded[..., :CL], d_global, band_size, width)
    gains_grad = jnp.concatenate([one_pair[1], two_pair[1], loc_pair[1], glo_pair[1]])
    biases_grad = jnp.concatenate([one_pair[0], two_pair[0], loc_pair[0], glo_pair[0]])
    return (
        d_input,
        (grad_local_kernel, grad_lift, grad_reduce, grad_mix, grad_expand),
        (gains_grad, biases_grad),
    )


def block_forward(block_in, geometry_now, kernels, gain_all, bias_all):
    base = block_in.astype(jnp.float32) * geometry_now[0]
    first_out, first_stored, first_stats = layer_forward(
        base, geometry_now, kernels[0], gain_all[0], bias_all[0]
    )
    second_out, second_stored, second_stats = layer_forward(
        first_out, geometry_now, kernels[1], gain_all[1], bias_all[1]
    )
    return (
        (second_out + base).astype(jnp.bfloat16),
        (first_stored, second_stored),
        (first_stats, second_stats),
    )


def block_backward(grad_in, stored, geometry_now, kernels, gain_all):
    pix_mask = geometry_now[0]
    grad_masked = grad_in * pix_mask
    d_first, second_kernels, second_norms = layer_backward(
        grad_masked, stored[1], geometry_now, kernels[1], gain_all[1]
    )
    d_base, first_kernels, first_norms = layer_backward(
        d_first, stored[0], geometry_now, kernels[0], gain_all[0]
    )
    return (
        (grad_masked + d_base) * pix_mask,
        (first_kernels, second_kernels),
        (first_norms, second_norms),
    )


def running_update(mean_now, var_now, layer_stats, geometry_now):
    pix_count = geometry_now[2]
    spec_count = geometry_now[3]
    counts = jnp.concatenate(
        [
            jnp.full((CS,), pix_count, jnp.float32),
            jnp.full((2 * CS,), spec_count, jnp.float32),
            jnp.full((CL + CG,), pix_count, jnp.float32),
        ]
    )
    batch_means = jnp.stack([layer_stats[0][0], layer_stats[1][0]])
    batch_vars = jnp.stack([layer_stats[0][1], layer_stats[1][1]])
    new_mean = (1.0 - MOMENTUM) * mean_now + MOMENTUM * batch_means
    new_var = (1.0 - MOMENTUM) * var_now + MOMENTUM * batch_vars * counts / (counts - 1.0)
    return (new_mean, new_var)


def on_device(
    inputs,
    cotangent,
    shapes,
    local_to_local,
    global_to_local,
    local_to_global,
    spec_reduce,
    spec_mix,
    spec_expand,
    norm_gains,
    norm_biases,
    run_means,
    run_vars,
):
    section_id = lax.axis_index("section")
    band_index = lax.axis_index("dp")
    n_dp = lax.axis_size("dp")
    micro_count = inputs.shape[0]
    map_count = inputs.shape[1]
    band_size = inputs.shape[2]
    freq_total = (LONG // 2 + n_dp) // n_dp * n_dp
    freq_local = freq_total // n_dp
    kernels = []
    for layer_pos in range(2):
        local_kernel = jnp.concatenate(
            [local_to_local[0, layer_pos], global_to_local[0, layer_pos]], axis=1
        )
        kernels.append(
            (
                local_kernel,
                local_to_global[0, layer_pos],
                spec_reduce[0, layer_pos],
                spec_mix[0, layer_pos],
                spec_expand[0, layer_pos],
            )
        )
    gain_all = norm_gains[0]
    bias_all = norm_biases[0]
    received = jnp.zeros(inputs.shape[1:], jnp.bfloat16)
    run_mean = run_means[0]
    run_var = run_vars[0]
    outputs = jnp.zeros(inputs.shape, jnp.bfloat16)
    saved_inputs = []
    saved_geometry = []
    for tick_pos in range(micro_count + 1):
        micro_index = tick_pos - section_id
        is_valid = (micro_index >= 0) & (micro_index < micro_count)
        micro_slot = jnp.clip(micro_index, 0, micro_count - 1)
        own_input = lax.dynamic_index_in_dim(inputs, micro_slot, 0, keepdims=False)
        block_in = jnp.where(section_id == 0, own_input, received)
        shape_row = lax.dynamic_index_in_dim(shapes, micro_slot, 0, keepdims=False)
        geometry_now = geometry(shape_row, band_index, band_size, freq_total, freq_local, map_count)
        block_out, stored, layer_stats = block_forward(
            block_in, geometry_now, kernels, gain_all, bias_all
        )
        new_mean, new_var = running_update(run_mean, run_var, layer_stats, geometry_now)
        run_mean = jnp.where(is_valid, new_mean, run_mean)
        run_var = jnp.where(is_valid, new_var, run_var)
        updated = lax.dynamic_update_index_in_dim(outputs, block_out, micro_slot, 0)
        outputs = jnp.where(is_valid, updated, outputs)
        saved_inputs.append(block_in)
        saved_geometry.append(geometry_now)
        if tick_pos < micro_count:
            received = from_behind(block_out, "section", 1)
    kernel_acc = [jnp.zeros((2,) + part_now.shape, jnp.float32) for part_now in kernels[0]]
    gain_acc = jnp.zeros(gain_all.shape, jnp.float32)
    bias_acc = jnp.zeros(bias_all.shape, jnp.float32)
    received_grad = jnp.zeros(inputs.shape[1:], jnp.bfloat16)
    grads_out = jnp.zeros(inputs.shape, jnp.float32)
    for tick_pos in range(micro_count + 1):
        micro_index = micro_count - tick_pos - section_id
        is_valid = (micro_index >= 0) & (micro_index < micro_count)
        micro_slot = jnp.clip(micro_index, 0, micro_count - 1)
        scale_valid = is_valid.astype(jnp.float32)
        forward_tick = micro_count - tick_pos
        geometry_now = saved_geometry[forward_tick]
        recomputed = block_forward(
            saved_inputs[forward_tick], geometry_now, kernels, gain_all, bias_all
        )
        stored = recomputed[1]
        own_grad = lax.dynamic_index_in_dim(cotangent, micro_slot, 0, keepdims=False)
        grad_in = jnp.where(section_id == 1, own_grad, received_grad).astype(jnp.float32)
        grad_input, kernel_grads, norm_grads = block_backward(
            grad_in, stored, geometry_now, kernels, gain_all
        )
        sent_grad = grad_input.astype(jnp.bfloat16)
        kept_grad = jnp.where(section_id == 1, sent_grad.astype(jnp.float32), grad_input)
        updated = lax.dynamic_update_index_in_dim(grads_out, kept_grad, micro_slot, 0)
        grads_out = jnp.where(is_valid, updated, grads_out)
        stacked = [
            jnp.stack([kernel_grads[0][part_pos], kernel_grads[1][part_pos]]) * scale_valid
            for part_pos in range(5)
        ]
        gain_acc = gain_acc + jnp.stack([norm_grads[0][0], norm_grads[1][0]]) * scale_valid
        bias_acc = bias_acc + jnp.stack([norm_grads[0][1], norm_grads[1][1]]) * scale_valid
        kernel_acc = [acc_part + new_part for acc_part, new_part in zip(kernel_acc, stacked)]
        if tick_pos < micro_count:
            received_grad = from_behind(sent_grad, "section", -1)
    totals = lax.psum(
        (kernel_acc[0], kernel_acc[1], kernel_acc[2], kernel_acc[3], kernel_acc[4]), "dp"
    )
    grad_ll = totals[0][:, :, :CL, :]
    grad_gl = totals[0][:, :, CL:, :]
    return (
        outputs[None],
        grads_out[None],
        grad_ll[None],
        grad_gl[None],
        totals[1][None],
        totals[2][None],
        totals[3][None],
        totals[4][None],
        gain_acc[None],
        bias_acc[None],
        run_mean[None],
        run_var[None],
    )


F32 = jnp.float32
BF16 = jnp.bfloat16
MESH = pl.DeviceIdType.MESH
MEMBERS = 16
ROWS = 8
LAYERS = 4
PAIRS = 4
HALF = 192
FULL = 384
SLOTS = 640
GRAD_ROWS = 10752
AT_KL = 0
AT_KG = 4608
AT_E = 8064
AT_M = 8704
AT_R = 9856
SECTION_NAMES = ("one", "two", "out")


def dot(a, b):
    return lax.dot_general(a, b, (((1,), (0,)), ((), ())), preferred_element_type=F32)


def dot_nt(a, b):
    return lax.dot_general(a, b, (((1,), (1,)), ((), ())), preferred_element_type=F32)


def dot_tn(a, b):
    return lax.dot_general(a, b, (((0,), (0,)), ((), ())), preferred_element_type=F32)


def sigmoid(v):
    return 0.5 * jnp.tanh(0.5 * v) + 0.5


def fold(v):
    return jnp.sum(v.reshape(v.shape[0] // 8, 8, v.shape[1]), axis=0)


def wide(row, lanes):
    whole, rest = divmod(lanes, 128)
    parts = [row] * whole + ([row[:, :rest]] if rest else [])
    return jnp.concatenate(parts, axis=1)


def network_kernel(
    inputs, cot, shapes, ll, gl, lg, red, mix, exp, par, run, tables, counts,
    out_y, out_g, out_w, out_p,
    w_c, w_gl, w_r, w_m, w_e, pars, acts, shifted, halo, v1, u, spec, mixed, tsum, v34,
    pmask, qmask, tf, tft, tg, tgt, hf, hi, vab, e2, dq, ds, g, gblk, at, gw,
    ssum, rsum, send, recv, stats, stats_far,
    sem_w, sem_in, sem_cot, sem_halo_s, sem_halo_r, sem_ar_s, sem_ar_r, sem_aa_s, sem_aa_r,
    sem_y_s, sem_y_r, sem_g_s, sem_g_r, sem_gw, sem_st,
):
    s = lax.axis_index("section")
    d = lax.axis_index("dp")
    n_dp = lax.axis_size("dp")
    per = n_dp // 2
    grp = lax.div(d, per)
    me = 2 * lax.rem(d, per) + s
    first = (me == 0).astype(F32)

    def member(group, k):
        return (lax.rem(k, 2), group * per + lax.div(k, 2))

    barrier = pltpu.get_barrier_semaphore()
    total = 2 * n_dp
    flat = s * n_dp + d

    def greet(i, c):
        other = lax.rem(flat + 1 + i, total)
        pl.semaphore_signal(
            barrier, inc=1, device_id=(lax.div(other, n_dp), lax.rem(other, n_dp)), device_id_type=MESH
        )
        return c

    lax.fori_loop(0, total - 1, greet, 0)

    own = pl.ds(2 * s, 2)
    places = [
        (red, w_r.at[own]),
        (par, pars.at[own]),
        (ll, w_c.at[own, :, :, 0:CL]),
        (lg, w_c.at[own, :, :, CL:]),
        (gl, w_gl.at[own]),
        (mix, w_m.at[own]),
        (exp, w_e.at[own]),
    ]
    local_w = [pltpu.make_async_copy(a, b, sem_w.at[0, i]) for i, (a, b) in enumerate(places)]
    for c in local_w:
        c.start()

    pl.semaphore_wait(barrier, total - 1)

    goal = (lax.rem(d, 2), s * per + lax.div(d, 2))
    stays = (goal[0] == s) & (goal[1] == d)

    def push_in(source, target, sems):
        @pl.when(stays)
        def _():
            pltpu.make_async_copy(source, target, sems.at[0]).start()

        @pl.when(jnp.logical_not(stays))
        def _():
            pltpu.make_async_remote_copy(
                source, target, sems.at[0], sems.at[1], device_id=goal, device_id_type=MESH
            ).start()

    def wait_in(source, target, sems):
        @pl.when(stays)
        def _():
            pltpu.make_async_copy(source, target, sems.at[0]).wait()

        @pl.when(jnp.logical_not(stays))
        def _():
            pltpu.make_async_remote_copy(
                source, target, sems.at[0], sems.at[1], device_id=goal, device_id_type=MESH
            ).wait()

    push_in(inputs.at[s], acts.at[0], sem_in)
    partner = (1 - s, d)
    remote_w = [
        pltpu.make_async_remote_copy(
            a, b, sem_w.at[1, i], sem_w.at[2, i], device_id=partner, device_id_type=MESH
        )
        for i, (a, b) in enumerate(places)
    ]
    for c in remote_w:
        c.start()

    height = shapes[grp, 0]
    width = shapes[grp, 1]
    col = lax.broadcasted_iota(jnp.int32, (128, 128), 0)
    for q in range(PAIRS):
        for h in range(2):
            row_ok = (ROWS * me + 2 * q + h < height).astype(F32)
            pmask[q, h * 128 : (h + 1) * 128, :] = (col < width).astype(F32) * row_ok
    for f in range(4):
        f_ok = (4 * me + f <= lax.div(width, 2)).astype(F32)
        qmask[f * 128 : (f + 1) * 128, :] = (col < height).astype(F32) * f_ok
    qmask[512:640, :] = (col < height).astype(F32) * (64 <= lax.div(width, 2)).astype(F32) * first
    inv_n = counts[0:1, :]
    inv_ns = counts[1:2, :]

    row_a = lax.broadcasted_iota(jnp.int32, (128, 512), 0)
    col_a = lax.broadcasted_iota(jnp.int32, (128, 512), 1)
    r_of = (col_a >> 5) * 8 + ((col_a & 31) >> 3) * 2 + (col_a & 1)
    sel_r = (row_a == r_of).astype(F32).astype(BF16)
    f_of = (col_a >> 1) & 3
    row_b = lax.broadcasted_iota(jnp.int32, (512, 128), 0)
    col_b = lax.broadcasted_iota(jnp.int32, (512, 128), 1)
    r_ob = (row_b >> 5) * 8 + ((row_b & 31) >> 3) * 2 + (row_b & 1)
    sel_rt = (col_b == r_ob).astype(F32).astype(BF16)
    f_ob = (row_b >> 1) & 3
    for part in range(2):
        base = tables[part].astype(BF16)
        spread = dot(base, sel_r)
        spread_t = dot(sel_rt, base)
        for f in range(4):
            hf[f, part * 128 : (part + 1) * 128, :] = jnp.where(f_of == f, spread, 0.0).astype(BF16)
            at_col = part * 512 + f * 128
            hi[:, at_col : at_col + 128] = jnp.where(f_ob == f, spread_t, 0.0).astype(BF16)
    row_c = lax.broadcasted_iota(jnp.int32, (128, 128), 0)
    sel_f = ((row_c >> 1) == lax.broadcasted_iota(jnp.int32, (128, 128), 1)).astype(F32).astype(BF16)
    for which, (plain, flipped_table) in enumerate(((tf, tft), (tg, tgt))):
        for part in range(2):
            spread = dot(sel_f, tables[2 + 2 * which + part].astype(BF16))
            spread_t = jnp.transpose(spread)
            for h in range(2):
                rows = slice(part * 128, (part + 1) * 128)
                cols = slice(h * 128, (h + 1) * 128)
                plain[rows, cols] = jnp.where((row_c & 1) == h, spread, 0.0).astype(BF16)
                flipped_table[cols, rows] = jnp.where(
                    (lax.broadcasted_iota(jnp.int32, (128, 128), 1) & 1) == h, spread_t, 0.0
                ).astype(BF16)
    stats[...] = jnp.zeros_like(stats)
    ssum[...] = jnp.zeros_like(ssum)
    shifted[0] = jnp.zeros((128, 1536), BF16)
    shifted[9] = jnp.zeros((128, 1536), BF16)
    gw[AT_M - 64 : AT_M, :] = jnp.zeros((64, 128), BF16)
    gw[GRAD_ROWS - 128 :, :] = jnp.zeros((128, 128), BF16)

    def sums_start(slot):
        rsum[slot, me] = ssum[slot]

        def go(i, c):
            k = lax.rem(me + 1 + i, MEMBERS)
            pltpu.make_async_remote_copy(
                ssum.at[slot], rsum.at[slot, me], sem_ar_s.at[slot, k], sem_ar_r.at[slot, me],
                device_id=member(grp, k), device_id_type=MESH,
            ).start()
            return c

        lax.fori_loop(0, MEMBERS - 1, go, 0)

    def sums_wait(slot, lanes):
        def go(i, c):
            k = lax.rem(me + 1 + i, MEMBERS)
            pltpu.make_async_remote_copy(
                ssum.at[slot], rsum.at[slot, k], sem_ar_s.at[slot, k], sem_ar_r.at[slot, k],
                device_id=member(grp, k), device_id_type=MESH,
            ).wait()
            return c

        lax.fori_loop(0, MEMBERS - 1, go, 0)
        tot = jnp.sum(rsum[slot], axis=0)
        tiles = (lanes + 127) // 128
        one = jnp.concatenate([tot[i : i + 1] for i in range(tiles)], axis=1)[:, :lanes]
        two = jnp.concatenate([tot[4 + i : 5 + i] for i in range(tiles)], axis=1)[:, :lanes]
        return one, two

    def put_sums(slot, one, two):
        lanes = one.shape[1]
        for base_row, part in ((0, one), (4, two)):
            flat_part = jnp.sum(part, axis=0, keepdims=True)
            for i in range((lanes + 127) // 128):
                w = min(128, lanes - i * 128)
                ssum[slot, base_row + i : base_row + i + 1, 0:w] = flat_part[:, i * 128 : i * 128 + w]

    def swap_start(slot):
        recv[slot, me] = send[slot, me]

        def go(i, c):
            k = lax.rem(me + 1 + i, MEMBERS)
            pltpu.make_async_remote_copy(
                send.at[slot, k], recv.at[slot, me], sem_aa_s.at[slot, k], sem_aa_r.at[slot, me],
                device_id=member(grp, k), device_id_type=MESH,
            ).start()
            return c

        lax.fori_loop(0, MEMBERS - 1, go, 0)

    def swap_wait(slot):
        def go(i, c):
            k = lax.rem(me + 1 + i, MEMBERS)
            pltpu.make_async_remote_copy(
                send.at[slot, k], recv.at[slot, k], sem_aa_s.at[slot, k], sem_aa_r.at[slot, k],
                device_id=member(grp, k), device_id_type=MESH,
            ).wait()
            return c

        lax.fori_loop(0, MEMBERS - 1, go, 0)

    def halo_copies():
        up = pltpu.make_async_remote_copy(
            shifted.at[1, :, 512:1024], halo.at[1], sem_halo_s.at[0], sem_halo_r.at[1],
            device_id=member(grp, lax.rem(me + MEMBERS - 1, MEMBERS)), device_id_type=MESH,
        )
        down = pltpu.make_async_remote_copy(
            shifted.at[8, :, 512:1024], halo.at[0], sem_halo_s.at[1], sem_halo_r.at[0],
            device_id=member(grp, lax.rem(me + 1, MEMBERS)), device_id_type=MESH,
        )
        return up, down

    has_up = me > 0
    has_down = me < MEMBERS - 1

    def halo_start():
        up, down = halo_copies()

        @pl.when(has_up)
        def _():
            up.start()

        @pl.when(has_down)
        def _():
            down.start()

    def put_shifted(index, x, flip):
        at_col = lax.broadcasted_iota(jnp.int32, (128, 512), 0)
        before = jnp.where(at_col == 0, 0.0, pltpu.roll(x, 1, 0))
        after = jnp.where(at_col == 127, 0.0, pltpu.roll(x, 127, 0))
        parts = (after, x, before) if flip else (before, x, after)
        for j, part in enumerate(parts):
            shifted[index, :, j * 512 : (j + 1) * 512] = part.astype(BF16)

    def halo_wait(flip):
        up, down = halo_copies()

        @pl.when(has_up)
        def _():
            up.wait_send()
            down.wait_recv()
            put_shifted(0, halo[0].astype(F32), flip)

        @pl.when(has_down)
        def _():
            down.wait_send()
            up.wait_recv()
            put_shifted(9, halo[1].astype(F32), flip)

    lane = lax.broadcasted_iota(jnp.int32, (128, FULL), 1)
    low = lane < HALF

    def width_out(slot, h, table, get):
        parts = []
        for q in (2 * h, 2 * h + 1):
            x = dot(table[...], get(q))
            both = jnp.concatenate([x[:128], x[128:]], axis=1)
            parts.append(both.reshape(MEMBERS, 8, FULL))
        send[slot, :, pl.ds(pl.multiple_of(16 * h, 16), 16), :] = jnp.concatenate(parts, axis=1).astype(BF16)

    def width_back(slot, h, table):
        block = recv[slot, :, pl.ds(pl.multiple_of(16 * h, 16), 16), :].astype(F32)
        results = []
        for o in range(2):
            z = block[:, 8 * o : 8 * o + 8, :].reshape(128, FULL)
            zi = pltpu.roll(z, HALF, 1)
            stacked = jnp.concatenate([z[:, :HALF], zi[:, :HALF]], axis=0).astype(BF16)
            results.append(dot(table[...], stacked))
        return results

    def rows_forward_into(slot, put):
        x = recv[slot].reshape(512, FULL)
        for f in range(4):
            both = dot(hf[f], x)
            a, b = both[:128], both[128:]
            turned = pltpu.roll(b, HALF, 1)
            if f == 0:
                rest = 1.0 - first
                put(0, jnp.where(low, a + rest * turned, rest * a - turned))
                put(4, jnp.where(low, pltpu.roll(a, HALF, 1), -b) * first)
            else:
                put(f, jnp.where(low, a + turned, a - turned))

    def rows_inverse_from(slot, get):
        last = get(4)
        for f in range(4):
            v = get(f)
            turned = pltpu.roll(v, HALF, 1)
            if f == 0:
                rest = 1.0 - first
                a = jnp.where(low, v, rest * v + first * pltpu.roll(last, HALF, 1))
                b = jnp.where(low, -turned, rest * turned - first * last)
            else:
                a = v
                b = jnp.where(low, -turned, turned)
            vab[f * 128 : (f + 1) * 128, :] = a.astype(BF16)
            vab[512 + f * 128 : 640 + f * 128, :] = b.astype(BF16)

        def go(c, carry):
            z = dot(hi[pl.ds(pl.multiple_of(c * 256, 256), 256), :], vab[...])
            send[slot, pl.ds(c * 8, 8)] = z.astype(BF16).reshape(8, 32, FULL)
            return carry

        lax.fori_loop(0, 2, go, 0)

    def moments(layer, which, lanes, one, two, inv_count):
        count = wide(inv_count, lanes)
        mean = one * count
        var = two * count - mean * mean
        inv = lax.rsqrt(var + EPSILON)
        stats[layer, which : which + 1, 0:lanes] = mean
        stats[layer, 3 + which : 4 + which, 0:lanes] = inv
        stats[layer, 6 + which : 7 + which, 0:lanes] = var
        scale = pars[layer, which : which + 1, 0:lanes] * inv
        shift = pars[layer, 3 + which : 4 + which, 0:lanes] - mean * scale
        return scale, shift

    def affine(layer, which, lanes):
        mean = stats[layer, which : which + 1, 0:lanes]
        inv = stats[layer, 3 + which : 4 + which, 0:lanes]
        gain = pars[layer, which : which + 1, 0:lanes]
        return mean, inv, gain, pars[layer, 3 + which : 4 + which, 0:lanes]

    def keep_grad_sums(layer, which, lanes, one, two):
        stats[layer, 9 + which : 10 + which, 0:lanes] = one
        stats[layer, 12 + which : 13 + which, 0:lanes] = two

    zero_of = lambda lanes: jnp.zeros((8, lanes), F32)

    def conv_pair(layer, c):
        loc = jnp.zeros((256, 512), F32)
        glo = jnp.zeros((256, 128), F32)
        for i in range(3):
            a_loc = jnp.concatenate(
                [shifted[pl.ds(2 * c + i, 2), :, j * 512 : j * 512 + 128].reshape(256, 128) for j in range(3)], axis=1
            )
            a_glo = jnp.concatenate(
                [shifted[pl.ds(2 * c + i, 2), :, j * 512 + 128 : (j + 1) * 512].reshape(256, 384) for j in range(3)],
                axis=1,
            )
            loc = loc + dot(a_loc, w_c[layer, 3 * i : 3 * i + 3].reshape(384, 512))
            glo = glo + dot(a_glo, w_gl[layer, 3 * i : 3 * i + 3].reshape(1152, 128))
        v34[layer, c, :, 0:CL] = loc[:, :CL] + glo
        v34[layer, c, :, CL:] = loc[:, CL:]

    wait_in(inputs.at[s], acts.at[0], sem_in)
    push_in(cot.at[s], gblk.at[1], sem_cot)

    def start_row(r, c):
        q = lax.div(r, 2)
        pm = pmask[q, pl.ds(pl.multiple_of(lax.rem(r, 2) * 128, 128), 128), :]
        x = acts[0, r].astype(F32) * wide(pm, 512)
        acts[0, r] = x.astype(BF16)
        put_shifted(1 + r, x, False)
        return c

    lax.fori_loop(0, ROWS, start_row, 0)
    for c in local_w:
        c.wait()
    for c in remote_w:
        c.wait()

    def y_copy(block):
        source = acts.at[2 * block + 2]
        target = out_y.at[grp]
        goal_now = (block, me)
        far = pltpu.make_async_remote_copy(
            source, target, sem_y_s.at[block], sem_y_r.at[grp], device_id=goal_now, device_id_type=MESH
        )
        near = pltpu.make_async_copy(source, target, sem_y_s.at[block])
        return (block == s) & (me == d), far, near

    def g_copy(block):
        source = gblk.at[2 * block]
        target = out_g.at[grp]
        far = pltpu.make_async_remote_copy(
            source, target, sem_g_s.at[block], sem_g_r.at[grp], device_id=(block, me), device_id_type=MESH
        )
        near = pltpu.make_async_copy(source, target, sem_g_s.at[block])
        return (block == s) & (me == d), far, near

    def start_out(made):
        here, far, near = made

        @pl.when(here)
        def _():
            near.start()

        @pl.when(jnp.logical_not(here))
        def _():
            far.start()

    def wait_out(made):
        here, far, near = made

        @pl.when(here)
        def _():
            near.wait()

        @pl.when(jnp.logical_not(here))
        def _():
            far.wait_send()

    def forward(layer, carry):
        halo_start()

        def reduce_pair(q, sums):
            a = acts[layer, pl.ds(2 * q, 2), :, CL:].reshape(256, CG)
            v = dot(a, w_r[layer])
            v1[layer, q] = v
            return sums[0] + fold(v), sums[1] + fold(v * v)

        put_sums(0, *lax.fori_loop(0, PAIRS, reduce_pair, (zero_of(HALF), zero_of(HALF))))
        sums_start(0)

        def conv_go(c, carry):
            conv_pair(layer, c)
            return carry

        lax.fori_loop(1, 3, conv_go, 0)
        scale, shift = moments(layer, 0, HALF, *sums_wait(0, HALF), inv_n)

        def spectral_in(h, carry):
            def get(q):
                pre = v1[layer, q] * scale + shift
                x = pre * sigmoid(pre) * wide(pmask[q], HALF)
                u[q] = x
                return x.astype(BF16)

            width_out(0, h, tf, get)
            return carry

        lax.fori_loop(0, 2, spectral_in, 0)
        swap_start(0)
        halo_wait(False)
        lax.fori_loop(0, 2, lambda c, k: conv_go(3 * c, k), 0)
        swap_wait(0)

        def put(f, y):
            spec[layer, f * 128 : (f + 1) * 128, :] = y.astype(BF16)

        rows_forward_into(0, put)

        def mix_block(f, sums):
            at_row = pl.ds(pl.multiple_of(f * 128, 128), 128)
            v = dot(spec[layer, at_row, :], w_m[layer])
            mixed[layer, at_row, :] = v
            return sums[0] + fold(v), sums[1] + fold(v * v)

        put_sums(1, *lax.fori_loop(0, 5, mix_block, (zero_of(FULL), zero_of(FULL))))
        sums_start(1)
        scale2, shift2 = moments(layer, 1, FULL, *sums_wait(1, FULL), inv_ns)

        def get_v(f):
            rows = slice(f * 128, (f + 1) * 128)
            pre = mixed[layer, rows, :] * scale2 + shift2
            return pre * sigmoid(pre) * wide(qmask[rows, :], FULL)

        rows_inverse_from(1, get_v)
        swap_start(1)
        swap_wait(1)

        def spectral_out(h, sums):
            backs = width_back(1, h, tgt)
            one, two = sums
            for o in range(2):
                q = 2 * h + o
                t = (u[q] + backs[o]).astype(BF16)
                tsum[layer, q] = t
                pm = pmask[q]
                v_loc = v34[layer, q, :, 0:CL] * pm
                v_glo = (v34[layer, q, :, CL:] + dot(t, w_e[layer])) * wide(pm, CG)
                v34[layer, q, :, 0:CL] = v_loc
                v34[layer, q, :, CL:] = v_glo
                v = jnp.concatenate([v_loc, v_glo], axis=1)
                one = one + fold(v)
                two = two + fold(v * v)
            return one, two

        put_sums(2, *lax.fori_loop(0, 2, spectral_out, (zero_of(512), zero_of(512))))
        sums_start(2)
        scale3, shift3 = moments(layer, 2, 512, *sums_wait(2, 512), inv_n)
        odd = lax.rem(layer, 2)
        oddf = odd.astype(F32)

        def next_row(r, carry):
            q = lax.div(r, 2)
            here = pl.ds(pl.multiple_of(lax.rem(r, 2) * 128, 128), 128)
            pre = v34[layer, q, here, :] * scale3 + shift3
            x = pre * sigmoid(pre) * wide(pmask[q, here, :], 512)
            x = x + oddf * acts[layer - odd, r].astype(F32)
            acts[layer + 1, r] = x.astype(BF16)

            @pl.when(layer < LAYERS - 1)
            def _():
                put_shifted(1 + r, x, False)

            return carry

        lax.fori_loop(0, ROWS, next_row, 0)

        @pl.when(odd == 1)
        def _():
            start_out(y_copy(lax.div(layer, 2)))

        return carry

    lax.fori_loop(0, LAYERS, forward, 0)

    wait_in(cot.at[s], gblk.at[1], sem_cot)

    def cot_row(r, c):
        q = lax.div(r, 2)
        here = pl.ds(pl.multiple_of(lax.rem(r, 2) * 128, 128), 128)
        x = gblk[1, r].astype(F32) * wide(pmask[q, here, :], 512)
        gblk[1, r] = x.astype(BF16)
        g[q, here, :] = x
        return c

    lax.fori_loop(0, ROWS, cot_row, 0)

    def gw_copy(layer):
        return pltpu.make_async_copy(gw, out_w.at[layer], sem_gw)

    def backward(step, carry):
        layer = LAYERS - 1 - step
        mean3, inv3, gain3, bias3 = affine(layer, 2, 512)
        scale3 = gain3 * inv3
        shift3 = bias3 - mean3 * scale3

        def slope_row(r, sums):
            q = lax.div(r, 2)
            here = pl.ds(pl.multiple_of(lax.rem(r, 2) * 128, 128), 128)
            v = v34[layer, q, here, :]
            pre = v * scale3 + shift3
            sg = sigmoid(pre)
            e = g[q, here, :] * wide(pmask[q, here, :], 512) * (sg * (1.0 + pre * (1.0 - sg)))
            g[q, here, :] = e
            return sums[0] + fold(e), sums[1] + fold(e * ((v - mean3) * inv3))

        put_sums(3, *lax.fori_loop(0, ROWS, slope_row, (zero_of(512), zero_of(512))))
        sums_start(3)

        def turn_row(r, carry):
            at[:, pl.ds(pl.multiple_of(r * 128, 128), 128)] = jnp.transpose(acts[layer, r])
            return carry

        lax.fori_loop(0, ROWS, turn_row, 0)
        one3, two3 = sums_wait(3, 512)
        keep_grad_sums(layer, 2, 512, one3, two3)
        part_a = one3 * wide(inv_n, 512)
        part_b = two3 * wide(inv_n, 512)

        def d_row(r, carry):
            q = lax.div(r, 2)
            here = pl.ds(pl.multiple_of(lax.rem(r, 2) * 128, 128), 128)
            z = (v34[layer, q, here, :] - mean3) * inv3
            dv = wide(pmask[q, here, :], 512) * scale3 * (g[q, here, :] - part_a - z * part_b)
            put_shifted(1 + r, dv, True)
            return carry

        lax.fori_loop(0, ROWS, d_row, 0)
        halo_start()

        def grad_out(h, carry):
            def get(q):
                dg = shifted[pl.ds(1 + 2 * q, 2), :, 512 + CL : 1024].reshape(256, CG)
                dt = dot_nt(dg, w_e[layer])
                u[q] = dt
                return dt.astype(BF16)

            width_out(0, h, tg, get)
            return carry

        lax.fori_loop(0, 2, grad_out, 0)
        swap_start(0)
        halo_wait(True)

        @pl.when(step > 0)
        def _():
            gw_copy(layer + 1).wait()

        def conv_back(c, carry):
            d_loc = jnp.zeros((256, 128), F32)
            d_glo = jnp.zeros((256, 384), F32)
            for i in range(3):
                for j in range(3):
                    rows = pl.ds(2 * c + 2 - i, 2)
                    dd = shifted[rows, :, j * 512 : (j + 1) * 512].reshape(256, 512)
                    d_loc = d_loc + dot_nt(dd, w_c[layer, 3 * i + j])
                    d_glo = d_glo + dot_nt(dd[:, :CL], w_gl[layer, 3 * i + j])
            g[c, :, 0:CL] = d_loc
            g[c, :, CL:] = d_glo
            return carry

        lax.fori_loop(0, PAIRS, conv_back, 0)
        swap_wait(0)

        def put(f, y):
            e2[f * 128 : (f + 1) * 128, :] = y

        rows_forward_into(0, put)
        mean2, inv2, gain2, bias2 = affine(layer, 1, FULL)
        scale2 = gain2 * inv2
        shift2 = bias2 - mean2 * scale2

        def slope_block(f, sums):
            rows = pl.ds(pl.multiple_of(f * 128, 128), 128)
            v = mixed[layer, rows, :]
            pre = v * scale2 + shift2
            sg = sigmoid(pre)
            e = e2[rows, :] * wide(qmask[rows, :], FULL) * (sg * (1.0 + pre * (1.0 - sg)))
            e2[rows, :] = e
            return sums[0] + fold(e), sums[1] + fold(e * ((v - mean2) * inv2))

        put_sums(1, *lax.fori_loop(0, 5, slope_block, (zero_of(FULL), zero_of(FULL))))
        sums_start(1)

        for i in range(3):
            def lift_grad(i=i):
                acc = jnp.zeros((128, 1152), F32)
                for q in range(PAIRS):
                    rows = slice(2 * q + 2 - i, 2 * q + 4 - i)
                    dd = jnp.concatenate(
                        [shifted[rows, :, j * 512 + CL : (j + 1) * 512].reshape(256, CG) for j in range(3)], axis=1
                    )
                    acc = acc + dot(at[0:CL, q * 256 : (q + 1) * 256], dd)
                for n in range(9):
                    base = AT_KG + (9 * i + n) * 128
                    gw[base : base + 128, :] = acc[:, n * 128 : (n + 1) * 128].astype(BF16)
            lift_grad()
        one2, two2 = sums_wait(1, FULL)
        keep_grad_sums(layer, 1, FULL, one2, two2)
        part_a2 = one2 * wide(inv_ns, FULL)
        part_b2 = two2 * wide(inv_ns, FULL)

        def dq_block(f, carry):
            rows = pl.ds(pl.multiple_of(f * 128, 128), 128)
            z = (mixed[layer, rows, :] - mean2) * inv2
            dv = wide(qmask[rows, :], FULL) * scale2 * (e2[rows, :] - part_a2 - z * part_b2)
            low_dv = dv.astype(BF16)
            dq[rows, :] = low_dv
            e2[rows, :] = dot_nt(low_dv, w_m[layer])
            return carry

        lax.fori_loop(0, 5, dq_block, 0)
        rows_inverse_from(1, lambda f: e2[f * 128 : (f + 1) * 128, :])
        swap_start(1)

        def local_grad(c, carry):
            for i in range(3):
                acc = jnp.zeros((128, 384), F32)
                for q in range(PAIRS):
                    rows = slice(2 * q + 2 - i, 2 * q + 4 - i)
                    dd = jnp.concatenate(
                        [shifted[rows, :, j * 512 : j * 512 + CL].reshape(256, CL) for j in range(3)], axis=1
                    )
                    acc = acc + dot(at[pl.ds(pl.multiple_of(c * 128, 128), 128), q * 256 : (q + 1) * 256], dd)
                for j in range(3):
                    base = pl.multiple_of(AT_KL + (3 * i + j) * 512 + c * 128, 128)
                    gw[pl.ds(base, 128), :] = acc[:, j * 128 : (j + 1) * 128].astype(BF16)
            return carry

        lax.fori_loop(0, 4, local_grad, 0)
        acc_e = jnp.zeros((HALF, CG), F32)
        for q in range(PAIRS):
            dg = shifted[1 + 2 * q : 3 + 2 * q, :, 512 + CL : 1024].reshape(256, CG)
            acc_e = acc_e + dot_tn(tsum[layer, q], dg)
        for n in range(3):
            gw[AT_E + n * HALF : AT_E + (n + 1) * HALF, :] = acc_e[:, n * 128 : (n + 1) * 128].astype(BF16)
        acc_m = jnp.zeros((FULL, FULL), F32)
        for f in range(5):
            rows = slice(f * 128, (f + 1) * 128)
            acc_m = acc_m + dot_tn(spec[layer, rows, :], dq[rows, :])
        for n in range(3):
            gw[AT_M + n * FULL : AT_M + (n + 1) * FULL, :] = acc_m[:, n * 128 : (n + 1) * 128].astype(BF16)
        swap_wait(1)

        mean1, inv1, gain1, bias1 = affine(layer, 0, HALF)
        scale1 = gain1 * inv1
        shift1 = bias1 - mean1 * scale1

        def slope_in(h, sums):
            backs = width_back(1, h, tft)
            one, two = sums
            for o in range(2):
                q = 2 * h + o
                v = v1[layer, q]
                pre = v * scale1 + shift1
                sg = sigmoid(pre)
                e = (u[q] + backs[o]) * wide(pmask[q], HALF) * (sg * (1.0 + pre * (1.0 - sg)))
                u[q] = e
                one = one + fold(e)
                two = two + fold(e * ((v - mean1) * inv1))
            return one, two

        put_sums(0, *lax.fori_loop(0, 2, slope_in, (zero_of(HALF), zero_of(HALF))))
        sums_start(0)
        one1, two1 = sums_wait(0, HALF)
        keep_grad_sums(layer, 0, HALF, one1, two1)
        part_a1 = one1 * wide(inv_n, HALF)
        part_b1 = two1 * wide(inv_n, HALF)

        def ds_pair(q, carry):
            z = (v1[layer, q] - mean1) * inv1
            dv = wide(pmask[q], HALF) * scale1 * (u[q] - part_a1 - z * part_b1)
            low_dv = dv.astype(BF16)
            ds[q] = low_dv
            g[q, :, CL:] = g[q, :, CL:] + dot_nt(low_dv, w_r[layer])
            return carry

        lax.fori_loop(0, PAIRS, ds_pair, 0)
        acc_r = jnp.zeros((CG, HALF), F32)
        for q in range(PAIRS):
            acc_r = acc_r + dot(at[CL:, q * 256 : (q + 1) * 256], ds[q])
        gw[AT_R : AT_R + CG, :] = acc_r[:, 0:128].astype(BF16)
        gw[AT_R + CG : AT_R + 2 * CG, 0:64] = acc_r[:, 128:HALF].astype(BF16)
        gw_copy(layer).start()

        @pl.when(lax.rem(layer, 2) == 0)
        def _():
            block = lax.div(layer, 2)

            def close_row(r, carry):
                q = lax.div(r, 2)
                here = pl.ds(pl.multiple_of(lax.rem(r, 2) * 128, 128), 128)
                x = (gblk[block, r].astype(F32) + g[q, here, :]) * wide(pmask[q, here, :], 512)
                low_x = x.astype(BF16)
                gblk[2 * block, r] = low_x

                @pl.when(block == 1)
                def _():
                    gblk[0, r] = low_x
                    g[q, here, :] = low_x.astype(F32)

                return carry

            lax.fori_loop(0, ROWS, close_row, 0)
            start_out(g_copy(block))

        return carry

    gw[AT_R + CG : AT_R + 2 * CG, :] = jnp.zeros((CG, 128), BF16)
    lax.fori_loop(0, LAYERS, backward, 0)

    far = pltpu.make_async_remote_copy(
        stats, stats_far, sem_st.at[0], sem_st.at[1],
        device_id=(s, lax.rem(d + per, n_dp)), device_id_type=MESH,
    )
    far.start()
    for block in range(2):
        wait_out(y_copy(block))
        wait_out(g_copy(block))
    for m in range(2):
        from_self = (lax.rem(d, 2) == s) & (m * per + lax.div(d, 2) == d)

        @pl.when(jnp.logical_not(from_self))
        def _(m=m):
            pltpu.make_async_remote_copy(
                acts.at[0], out_y.at[m], sem_y_s.at[0], sem_y_r.at[m], device_id=partner, device_id_type=MESH
            ).wait_recv()
            pltpu.make_async_remote_copy(
                gblk.at[0], out_g.at[m], sem_g_s.at[0], sem_g_r.at[m], device_id=partner, device_id_type=MESH
            ).wait_recv()

    gw_copy(0).wait()
    far.wait()
    for lay in range(2):
        mine = stats[2 * s + lay]
        other = stats_far[2 * s + lay]
        zero_first = jnp.where(grp == 0, mine, other)
        one_next = jnp.where(grp == 0, other, mine)
        for which, (lanes, at_count) in enumerate(((HALF, 2), (FULL, 4), (512, 2))):
            mean = run[lay, which : which + 1, :]
            var = run[lay, 3 + which : 4 + which, :]
            for m, st in enumerate((zero_first, one_next)):
                mean = (1.0 - MOMENTUM) * mean + MOMENTUM * st[which : which + 1]
                fix = wide(counts[at_count + m : at_count + m + 1, :], 512)
                var = (1.0 - MOMENTUM) * var + MOMENTUM * st[6 + which : 7 + which] * fix
            out_p[lay, which : which + 1, :] = mean
            out_p[lay, 3 + which : 4 + which, :] = var
            for base in (9, 12):
                total_sum = zero_first[base + which : base + which + 1] + one_next[base + which : base + which + 1]
                out_p[lay, base - 3 + which : base - 2 + which, :] = total_sum
        out_p[lay, 12:16, :] = jnp.zeros((4, 512), F32)


def spectral_tables(height, width):
    part = lax.broadcasted_iota(jnp.int32, (6, LONG, LONG), 0)
    row = lax.broadcasted_iota(jnp.int32, (6, LONG, LONG), 1)
    col = lax.broadcasted_iota(jnp.int32, (6, LONG, LONG), 2)
    odd = part % 2 == 1
    tall = part < 2
    lifted = odd & ~tall & (row == 0)
    index = jnp.where(lifted, LONG // 2, row)
    side = jnp.where(tall, height, width)
    phase = (index * col) % side
    side_real = side.astype(jnp.float32)
    angle = 2.0 * jnp.pi / side_real * phase.astype(jnp.float32)
    wave = jnp.where(odd & ~lifted, jnp.where(tall, 1.0, -1.0) * jnp.sin(angle), jnp.cos(angle))
    valid = (col < side) & (index < jnp.where(tall, height, width // 2 + 1))
    edge = (index == 0) | (index == width // 2)
    weight = jnp.where((part >= 4) & ~edge, 2.0, 1.0)
    return jnp.where(valid, wave * weight * lax.rsqrt(side_real), 0.0)


def pack_norms(array):
    return jnp.stack(
        [
            jnp.pad(array[:, :CS], ((0, 0), (0, 512 - CS))),
            jnp.pad(array[:, CS : 3 * CS], ((0, 0), (0, 512 - 2 * CS))),
            array[:, 3 * CS :],
        ],
        axis=1,
    )


def unpack_norms(array):
    return jnp.concatenate([array[:, 0, :CS], array[:, 1, : 2 * CS], array[:, 2]], axis=1)


def tiles_of(rows, lanes, array):
    return jnp.swapaxes(array.reshape(2, lanes // 128, rows, 128), 1, 2).reshape(2, rows, lanes)


def on_band(
    inputs,
    cotangent,
    shapes,
    local_to_local,
    global_to_local,
    local_to_global,
    spec_reduce,
    spec_mix,
    spec_expand,
    norm_gains,
    norm_biases,
    run_means,
    run_vars,
):
    section_id = lax.axis_index("section")
    n_dp = lax.axis_size("dp")
    group = lax.axis_index("dp") // (n_dp // 2)
    own_shape = lax.dynamic_index_in_dim(shapes, group, 0, keepdims=False)
    tables = spectral_tables(own_shape[0], own_shape[1])
    zeros = jnp.zeros((2, 2, 512), jnp.float32)
    pars = jnp.concatenate([pack_norms(norm_gains[0]), pack_norms(norm_biases[0]), zeros], axis=1)
    run = jnp.concatenate([pack_norms(run_means[0]), pack_norms(run_vars[0]), zeros], axis=1)
    pixels = (shapes[:, 0] * shapes[:, 1]).astype(jnp.float32)
    points = (shapes[:, 0] * (shapes[:, 1] // 2 + 1)).astype(jnp.float32)
    own_pixels = lax.dynamic_index_in_dim(pixels, group, 0)
    own_points = lax.dynamic_index_in_dim(points, group, 0)
    counts = jnp.concatenate(
        [1.0 / own_pixels, 1.0 / own_points, pixels / (pixels - 1.0), points / (points - 1.0), jnp.zeros((2,))]
    )
    counts = jnp.broadcast_to(counts[:, None], (8, 128)).astype(jnp.float32)
    anywhere = pl.BlockSpec(memory_space=pl.ANY)
    vmem = pl.BlockSpec(memory_space=pltpu.VMEM)
    dma = pltpu.SemaphoreType.DMA
    band = (ROWS, LONG, 512)
    out_y, out_g, out_w, out_p = pl.pallas_call(
        network_kernel,
        out_shape=(
            jax.ShapeDtypeStruct((2,) + band, BF16),
            jax.ShapeDtypeStruct((2,) + band, BF16),
            jax.ShapeDtypeStruct((LAYERS, GRAD_ROWS, 128), BF16),
            jax.ShapeDtypeStruct((2, 16, 512), F32),
        ),
        in_specs=[anywhere, anywhere, pl.BlockSpec(memory_space=pltpu.SMEM)]
        + [anywhere] * 7
        + [vmem] * 3,
        out_specs=(anywhere, anywhere, anywhere, vmem),
        scratch_shapes=[
            pltpu.VMEM((LAYERS, 9, CL, 512), BF16),
            pltpu.VMEM((LAYERS, 9, CG, CL), BF16),
            pltpu.VMEM((LAYERS, CG, CS), BF16),
            pltpu.VMEM((LAYERS, FULL, FULL), BF16),
            pltpu.VMEM((LAYERS, CS, CG), BF16),
            pltpu.VMEM((LAYERS, 8, 512), F32),
            pltpu.VMEM((LAYERS + 1,) + band, BF16),
            pltpu.VMEM((ROWS + 2, LONG, 1536), BF16),
            pltpu.VMEM((2, LONG, 512), BF16),
            pltpu.VMEM((LAYERS, PAIRS, 256, CS), F32),
            pltpu.VMEM((PAIRS, 256, CS), F32),
            pltpu.VMEM((LAYERS, SLOTS, FULL), BF16),
            pltpu.VMEM((LAYERS, SLOTS, FULL), F32),
            pltpu.VMEM((LAYERS, PAIRS, 256, CS), BF16),
            pltpu.VMEM((LAYERS, PAIRS, 256, 512), F32),
            pltpu.VMEM((PAIRS, 256, 128), F32),
            pltpu.VMEM((SLOTS, 128), F32),
            pltpu.VMEM((256, 256), BF16),
            pltpu.VMEM((256, 256), BF16),
            pltpu.VMEM((256, 256), BF16),
            pltpu.VMEM((256, 256), BF16),
            pltpu.VMEM((4, 256, 512), BF16),
            pltpu.VMEM((512, 1024), BF16),
            pltpu.VMEM((1024, FULL), BF16),
            pltpu.VMEM((SLOTS, FULL), F32),
            pltpu.VMEM((SLOTS, FULL), BF16),
            pltpu.VMEM((PAIRS, 256, CS), BF16),
            pltpu.VMEM((PAIRS, 256, 512), F32),
            pltpu.VMEM((3,) + band, BF16),
            pltpu.VMEM((512, ROWS * LONG), BF16),
            pltpu.VMEM((GRAD_ROWS, 128), BF16),
            pltpu.VMEM((4, 8, 128), F32),
            pltpu.VMEM((4, MEMBERS, 8, 128), F32),
            pltpu.VMEM((2, MEMBERS, 32, FULL), BF16),
            pltpu.VMEM((2, MEMBERS, 32, FULL), BF16),
            pltpu.VMEM((LAYERS, 16, 512), F32),
            pltpu.VMEM((LAYERS, 16, 512), F32),
            dma((3, 8)),
            dma((2,)),
            dma((2,)),
            dma((2,)),
            dma((2,)),
            dma((4, MEMBERS)),
            dma((4, MEMBERS)),
            dma((2, MEMBERS)),
            dma((2, MEMBERS)),
            dma((2,)),
            dma((2,)),
            dma((2,)),
            dma((2,)),
            dma,
            dma((2,)),
        ],
        compiler_params=pltpu.CompilerParams(
            collective_id=0, has_side_effects=True, vmem_limit_bytes=63 << 20
        ),
        name="network",
    )(
        inputs[:, 0],
        cotangent[:, 0],
        shapes,
        local_to_local[0],
        global_to_local[0],
        local_to_global[0],
        spec_reduce[0],
        spec_mix[0],
        spec_expand[0],
        pars,
        run,
        tables,
        counts,
    )
    sent = lax.dynamic_slice_in_dim(out_w, 2 * (1 - section_id), 2, 0)
    kept = lax.dynamic_slice_in_dim(out_w, 2 * section_id, 2, 0)
    other = lax.ppermute(sent, "section", [(0, 1), (1, 0)])
    totals = lax.psum(kept.astype(F32) + other.astype(F32), "dp")
    grad_local = totals[:, AT_KL:AT_KG].reshape(2, 9, 512, 128)
    grad_lift = totals[:, AT_KG:AT_E].reshape(2, 9, 3, 128, 128)
    grad_lift = jnp.swapaxes(grad_lift, 2, 3).reshape(2, 9, CL, CG)
    grad_expand = tiles_of(CS, CG, totals[:, AT_E : AT_E + 3 * CS])
    grad_mix = tiles_of(FULL, FULL, totals[:, AT_M : AT_M + 3 * FULL])
    grad_reduce = tiles_of(CG, 256, totals[:, AT_R : AT_R + 2 * CG])[..., :CS]
    return (
        out_y[None, :, None],
        out_g.astype(F32)[None, :, None],
        grad_local[None, :, :, :CL],
        grad_local[None, :, :, CL:],
        grad_lift[None],
        grad_reduce[None],
        grad_mix[None],
        grad_expand[None],
        unpack_norms(out_p[:, 9:12])[None],
        unpack_norms(out_p[:, 6:9])[None],
        unpack_norms(out_p[:, 0:3])[None],
        unpack_norms(out_p[:, 3:6])[None],
    )


def solution(mesh):
    in_specs = (
        P(None, None, "dp", None, None),
        P(None, None, "dp", None, None),
        P(),
        P("section", None, None, None, None),
        P("section", None, None, None, None),
        P("section", None, None, None, None),
        P("section", None, None, None),
        P("section", None, None, None),
        P("section", None, None, None),
        P("section", None, None),
        P("section", None, None),
        P("section", None, None),
        P("section", None, None),
    )
    out_specs = (
        P("section", None, None, "dp", None, None),
        P("section", None, None, "dp", None, None),
        P("section", None, None, None, None),
        P("section", None, None, None, None),
        P("section", None, None, None, None),
        P("section", None, None, None),
        P("section", None, None, None),
        P("section", None, None, None),
        P("section", None, None),
        P("section", None, None),
        P("section", None, None),
        P("section", None, None),
    )
    dp_size = mesh.shape["dp"]
    banded = dp_size == MEMBERS and LONG == dp_size * ROWS
    return jax.shard_map(
        on_band if banded else on_device, mesh=mesh, in_specs=in_specs, out_specs=out_specs, check_vma=False
    )
```

```python
import jax
import jax.numpy as jnp
from jax import lax
from jax.experimental import pallas as pl
from jax.experimental.pallas import tpu as pltpu
from jax.sharding import PartitionSpec as P

CL = 128
CG = 384
CS = 192
LONG = 128


EPSILON = 1e-05
MOMENTUM = 0.1
PRECISE = lax.Precision.HIGHEST


def with_halo(block, sides, width):
    for axis, dim in sides:
        count = lax.axis_size(axis)
        forward = [(i, i + 1) for i in range(count - 1)]
        backward = [(target, source) for source, target in forward]
        low = lax.ppermute(
            lax.slice_in_dim(block, block.shape[dim] - width, None, axis=dim), axis, forward
        )
        high = lax.ppermute(lax.slice_in_dim(block, 0, width, axis=dim), axis, backward)
        block = jnp.concatenate([low, block, high], axis=dim)
    return block


def from_behind(value, axis, steps):
    count = lax.axis_size(axis)
    first, last = (max(0, -steps), min(count, count - steps))
    return lax.ppermute(value, axis, [(source, source + steps) for source in range(first, last)])


def dft_tables(height, width, long_side, freq_total):
    position = jnp.arange(long_side, dtype=jnp.int32)
    frequency = jnp.arange(freq_total, dtype=jnp.int32)
    half_width = width // 2
    width_real = width.astype(jnp.float32)
    height_real = height.astype(jnp.float32)
    width_phase = position[:, None] * frequency[None, :] % width
    width_angle = 2.0 * jnp.pi / width_real * width_phase.astype(jnp.float32)
    width_valid = ((position[:, None] < width) & (frequency[None, :] <= half_width)).astype(
        jnp.float32
    )
    width_scale = lax.rsqrt(width_real)
    fwd_cos = jnp.cos(width_angle) * width_scale * width_valid
    fwd_sin = -jnp.sin(width_angle) * width_scale * width_valid
    edge_freq = (frequency == 0) | (frequency == half_width)
    freq_weight = jnp.where(edge_freq, 1.0, 2.0).astype(jnp.float32)
    inv_cos = freq_weight[:, None] * fwd_cos.T
    inv_sin = freq_weight[:, None] * fwd_sin.T
    height_phase = position[:, None] * position[None, :] % height
    height_angle = 2.0 * jnp.pi / height_real * height_phase.astype(jnp.float32)
    height_valid = ((position[:, None] < height) & (position[None, :] < height)).astype(jnp.float32)
    height_scale = lax.rsqrt(height_real)
    row_cos = jnp.cos(height_angle) * height_scale * height_valid
    row_sin = jnp.sin(height_angle) * height_scale * height_valid
    return (fwd_cos, fwd_sin, inv_cos, inv_sin, row_cos, row_sin)


def geometry(shape_row, band_index, band_size, freq_total, freq_local, map_count):
    height = shape_row[0]
    width = shape_row[1]
    position = jnp.arange(LONG, dtype=jnp.int32)
    band_rows = band_index * band_size + jnp.arange(band_size, dtype=jnp.int32)
    pix_mask = ((band_rows[:, None] < height) & (position[None, :] < width)).astype(jnp.float32)[
        None, :, :, None
    ]
    local_freq = band_index * freq_local + jnp.arange(freq_local, dtype=jnp.int32)
    freq_mask = ((position[:, None] < height) & (local_freq[None, :] <= width // 2)).astype(
        jnp.float32
    )[None, :, :, None]
    pix_count = (map_count * height * width).astype(jnp.float32)
    spec_count = (map_count * height * (width // 2 + 1)).astype(jnp.float32)
    return (pix_mask, freq_mask, pix_count, spec_count, dft_tables(height, width, LONG, freq_total))


def conv_rows(padded, kernel):
    shaped = kernel.reshape(3, 3, kernel.shape[1], kernel.shape[2])
    return lax.conv_general_dilated(
        padded,
        shaped,
        (1, 1),
        "VALID",
        dimension_numbers=("NHWC", "HWIO", "NHWC"),
        preferred_element_type=jnp.float32,
    )


def flipped(kernel):
    shaped = kernel.reshape(3, 3, kernel.shape[1], kernel.shape[2])[::-1, ::-1]
    return jnp.swapaxes(shaped, 2, 3).reshape(9, kernel.shape[2], kernel.shape[1])


def kernel_grad(padded, grad_out, band_size, width):
    tap_grads = []
    for row_tap in range(3):
        for col_tap in range(3):
            window = padded[:, row_tap : row_tap + band_size, col_tap : col_tap + width, :]
            tap_grads.append(
                jnp.einsum("mrwi,mrwo->io", window, grad_out, preferred_element_type=jnp.float32)
            )
    return jnp.stack(tap_grads)


def width_forward(entry, table):
    return jnp.einsum("mrwc,wf->mrfc", entry, table, precision=PRECISE)


def width_forward_adj(entry, table):
    return jnp.einsum("mrfc,wf->mrwc", entry, table, precision=PRECISE)


def width_inverse(entry, table):
    return jnp.einsum("mrfc,fw->mrwc", entry, table, precision=PRECISE)


def width_inverse_adj(entry, table):
    return jnp.einsum("mrwc,fw->mrfc", entry, table, precision=PRECISE)


def height_apply(table, entry):
    return jnp.einsum("kn,mnfc->mkfc", table, entry, precision=PRECISE)


def height_adjoint(table, entry):
    return jnp.einsum("kn,mkfc->mnfc", table, entry, precision=PRECISE)


def rows_forward(row_cos, row_sin, entry):
    half_ch = entry.shape[-1] // 2
    real_in = entry[..., :half_ch]
    imag_in = entry[..., half_ch:]
    real_out = height_apply(row_cos, real_in) + height_apply(row_sin, imag_in)
    imag_out = height_apply(row_cos, imag_in) - height_apply(row_sin, real_in)
    return jnp.concatenate([real_out, imag_out], axis=-1)


def rows_inverse(row_cos, row_sin, entry):
    half_ch = entry.shape[-1] // 2
    real_in = entry[..., :half_ch]
    imag_in = entry[..., half_ch:]
    real_out = height_adjoint(row_cos, real_in) - height_adjoint(row_sin, imag_in)
    imag_out = height_adjoint(row_cos, imag_in) + height_adjoint(row_sin, real_in)
    return jnp.concatenate([real_out, imag_out], axis=-1)


def split_pairs(totals, widths):
    pairs = []
    offset = 0
    for lead_width, tail_width in zip(widths[0::2], widths[1::2]):
        lead_part = totals[offset : offset + lead_width]
        tail_part = totals[offset + lead_width : offset + lead_width + tail_width]
        pairs.append((lead_part, tail_part))
        offset = offset + lead_width + tail_width
    return pairs


def moments(entries, weights):
    pieces = []
    for entry, weight in zip(entries, weights):
        masked = entry * weight
        pieces.append(jnp.sum(masked, axis=(0, 1, 2)))
        pieces.append(jnp.sum(masked * entry, axis=(0, 1, 2)))
    totals = lax.psum(jnp.concatenate(pieces), "dp")
    return split_pairs(totals, [piece.shape[0] for piece in pieces])


def grad_moments(grads_in, normed_in):
    pieces = []
    for grad_pre, normed in zip(grads_in, normed_in):
        pieces.append(jnp.sum(grad_pre, axis=(0, 1, 2)))
        pieces.append(jnp.sum(grad_pre * normed, axis=(0, 1, 2)))
    totals = lax.psum(jnp.concatenate(pieces), "dp")
    return split_pairs(totals, [piece.shape[0] for piece in pieces])


def normalize(entry, sum_pair, count_now):
    mean_val = sum_pair[0] / count_now
    var_val = sum_pair[1] / count_now - mean_val * mean_val
    inv_std = lax.rsqrt(var_val + EPSILON)
    return ((entry - mean_val) * inv_std, inv_std, mean_val, var_val)


def silu_slope(pre_act):
    sigmoid_val = jax.nn.sigmoid(pre_act)
    return sigmoid_val * (1.0 + pre_act * (1.0 - sigmoid_val))


def norm_backward(grad_pre, normed, inv_std, gain_part, sum_pair, count_now, weight):
    return (
        weight
        * inv_std
        * gain_part
        * (grad_pre - sum_pair[0] / count_now - normed * sum_pair[1] / count_now)
    )


def layer_forward(layer_in, geometry_now, kernels, gain_vec, bias_vec):
    pix_mask, freq_mask, pix_count, spec_count, tables = geometry_now
    fwd_cos, fwd_sin, inv_cos, inv_sin, row_cos, row_sin = tables
    local_kernel, lift_kernel, reduce_kernel, mix_kernel, expand_kernel = kernels
    acts_low = layer_in.astype(jnp.bfloat16)
    padded = with_halo(acts_low, (("dp", 1),), 1)
    padded = jnp.pad(padded, ((0, 0), (0, 0), (1, 1), (0, 0)))
    local_out = conv_rows(padded, local_kernel)
    global_conv = conv_rows(padded[..., :CL], lift_kernel)
    reduced = jnp.einsum(
        "mrwc,cd->mrwd", acts_low[..., CL:], reduce_kernel, preferred_element_type=jnp.float32
    )
    one_stats = moments([reduced], [pix_mask])[0]
    normed_one, inv_one, mean_one, var_one = normalize(reduced, one_stats, pix_count)
    pre_one = normed_one * gain_vec[:CS] + bias_vec[:CS]
    upper_spec = jax.nn.silu(pre_one) * pix_mask
    spectrum = jnp.concatenate(
        [width_forward(upper_spec, fwd_cos), width_forward(upper_spec, fwd_sin)], axis=-1
    ).astype(jnp.bfloat16)
    columns = lax.all_to_all(spectrum, "dp", split_axis=2, concat_axis=1, tiled=True).astype(
        jnp.float32
    )
    spectra = rows_forward(row_cos, row_sin, columns).astype(jnp.bfloat16)
    mixed = jnp.einsum("mkfc,cd->mkfd", spectra, mix_kernel, preferred_element_type=jnp.float32)
    two_stats = moments([mixed], [freq_mask])[0]
    normed_two, inv_two, mean_two, var_two = normalize(mixed, two_stats, spec_count)
    pre_two = normed_two * gain_vec[CS : 3 * CS] + bias_vec[CS : 3 * CS]
    activated = jax.nn.silu(pre_two) * freq_mask
    inverse = rows_inverse(row_cos, row_sin, activated).astype(jnp.bfloat16)
    returned = lax.all_to_all(inverse, "dp", split_axis=1, concat_axis=2, tiled=True).astype(
        jnp.float32
    )
    half_ch = returned.shape[-1] // 2
    restored = width_inverse(returned[..., :half_ch], inv_cos) + width_inverse(
        returned[..., half_ch:], inv_sin
    )
    summed = (upper_spec + restored).astype(jnp.bfloat16)
    spec_out = jnp.einsum(
        "mrwc,cd->mrwd", summed, expand_kernel, preferred_element_type=jnp.float32
    )
    global_out = global_conv + spec_out
    loc_stats, glo_stats = moments([local_out, global_out], [pix_mask, pix_mask])
    normed_loc, inv_loc, mean_loc, var_loc = normalize(local_out, loc_stats, pix_count)
    normed_glo, inv_glo, mean_glo, var_glo = normalize(global_out, glo_stats, pix_count)
    pre_loc = normed_loc * gain_vec[3 * CS : 3 * CS + CL] + bias_vec[3 * CS : 3 * CS + CL]
    pre_glo = normed_glo * gain_vec[3 * CS + CL :] + bias_vec[3 * CS + CL :]
    result = jnp.concatenate([jax.nn.silu(pre_loc), jax.nn.silu(pre_glo)], axis=-1) * pix_mask
    stored = (
        padded,
        pre_one,
        normed_one,
        inv_one,
        spectra,
        pre_two,
        normed_two,
        inv_two,
        summed,
        pre_loc,
        normed_loc,
        inv_loc,
        pre_glo,
        normed_glo,
        inv_glo,
    )
    means_layer = jnp.concatenate([mean_one, mean_two, mean_loc, mean_glo])
    vars_layer = jnp.concatenate([var_one, var_two, var_loc, var_glo])
    return (result, stored, (means_layer, vars_layer))


def layer_backward(grad_result, stored, geometry_now, kernels, gain_vec):
    (
        padded,
        pre_one,
        normed_one,
        inv_one,
        spectra,
        pre_two,
        normed_two,
        inv_two,
        summed,
        pre_loc,
        normed_loc,
        inv_loc,
        pre_glo,
        normed_glo,
        inv_glo,
    ) = stored
    pix_mask, freq_mask, pix_count, spec_count, tables = geometry_now
    fwd_cos, fwd_sin, inv_cos, inv_sin, row_cos, row_sin = tables
    local_kernel, lift_kernel, reduce_kernel, mix_kernel, expand_kernel = kernels
    band_size = pre_one.shape[1]
    width = pre_one.shape[2]
    grad_loc = grad_result[..., :CL] * pix_mask * silu_slope(pre_loc)
    grad_glo = grad_result[..., CL:] * pix_mask * silu_slope(pre_glo)
    loc_pair, glo_pair = grad_moments([grad_loc, grad_glo], [normed_loc, normed_glo])
    d_local = norm_backward(
        grad_loc, normed_loc, inv_loc, gain_vec[3 * CS : 3 * CS + CL], loc_pair, pix_count, pix_mask
    ).astype(jnp.bfloat16)
    d_global = norm_backward(
        grad_glo, normed_glo, inv_glo, gain_vec[3 * CS + CL :], glo_pair, pix_count, pix_mask
    ).astype(jnp.bfloat16)
    grad_expand = jnp.einsum("mrwc,mrwd->cd", summed, d_global, preferred_element_type=jnp.float32)
    d_summed = jnp.einsum(
        "mrwd,cd->mrwc", d_global, expand_kernel, preferred_element_type=jnp.float32
    )
    d_returned = jnp.concatenate(
        [width_inverse_adj(d_summed, inv_cos), width_inverse_adj(d_summed, inv_sin)], axis=-1
    ).astype(jnp.bfloat16)
    d_inverse = lax.all_to_all(d_returned, "dp", split_axis=2, concat_axis=1, tiled=True).astype(
        jnp.float32
    )
    d_activated = rows_forward(row_cos, row_sin, d_inverse)
    grad_two = d_activated * freq_mask * silu_slope(pre_two)
    two_pair = grad_moments([grad_two], [normed_two])[0]
    d_mixed = norm_backward(
        grad_two, normed_two, inv_two, gain_vec[CS : 3 * CS], two_pair, spec_count, freq_mask
    ).astype(jnp.bfloat16)
    grad_mix = jnp.einsum("mkfc,mkfd->cd", spectra, d_mixed, preferred_element_type=jnp.float32)
    d_spectra = jnp.einsum("mkfd,cd->mkfc", d_mixed, mix_kernel, preferred_element_type=jnp.float32)
    d_columns = rows_inverse(row_cos, row_sin, d_spectra).astype(jnp.bfloat16)
    d_spectrum = lax.all_to_all(d_columns, "dp", split_axis=1, concat_axis=2, tiled=True).astype(
        jnp.float32
    )
    half_ch = d_spectrum.shape[-1] // 2
    d_upper = (
        d_summed
        + width_forward_adj(d_spectrum[..., :half_ch], fwd_cos)
        + width_forward_adj(d_spectrum[..., half_ch:], fwd_sin)
    )
    grad_one = d_upper * pix_mask * silu_slope(pre_one)
    one_pair = grad_moments([grad_one], [normed_one])[0]
    d_reduced = norm_backward(
        grad_one, normed_one, inv_one, gain_vec[:CS], one_pair, pix_count, pix_mask
    ).astype(jnp.bfloat16)
    acts_low = padded[:, 1:-1, 1:-1, :]
    grad_reduce = jnp.einsum(
        "mrwc,mrwd->cd", acts_low[..., CL:], d_reduced, preferred_element_type=jnp.float32
    )
    d_global_in = jnp.einsum(
        "mrwd,cd->mrwc", d_reduced, reduce_kernel, preferred_element_type=jnp.float32
    )
    grad_outs = jnp.concatenate([d_local, d_global], axis=-1)
    grad_pad = with_halo(grad_outs, (("dp", 1),), 1)
    grad_pad = jnp.pad(grad_pad, ((0, 0), (0, 0), (1, 1), (0, 0)))
    d_acts = conv_rows(grad_pad[..., :CL], flipped(local_kernel))
    d_lift = conv_rows(grad_pad[..., CL:], flipped(lift_kernel))
    d_input = d_acts + jnp.concatenate([d_lift, d_global_in], axis=-1)
    grad_local_kernel = kernel_grad(padded, d_local, band_size, width)
    grad_lift = kernel_grad(padded[..., :CL], d_global, band_size, width)
    gains_grad = jnp.concatenate([one_pair[1], two_pair[1], loc_pair[1], glo_pair[1]])
    biases_grad = jnp.concatenate([one_pair[0], two_pair[0], loc_pair[0], glo_pair[0]])
    return (
        d_input,
        (grad_local_kernel, grad_lift, grad_reduce, grad_mix, grad_expand),
        (gains_grad, biases_grad),
    )


def block_forward(block_in, geometry_now, kernels, gain_all, bias_all):
    base = block_in.astype(jnp.float32) * geometry_now[0]
    first_out, first_stored, first_stats = layer_forward(
        base, geometry_now, kernels[0], gain_all[0], bias_all[0]
    )
    second_out, second_stored, second_stats = layer_forward(
        first_out, geometry_now, kernels[1], gain_all[1], bias_all[1]
    )
    return (
        (second_out + base).astype(jnp.bfloat16),
        (first_stored, second_stored),
        (first_stats, second_stats),
    )


def block_backward(grad_in, stored, geometry_now, kernels, gain_all):
    pix_mask = geometry_now[0]
    grad_masked = grad_in * pix_mask
    d_first, second_kernels, second_norms = layer_backward(
        grad_masked, stored[1], geometry_now, kernels[1], gain_all[1]
    )
    d_base, first_kernels, first_norms = layer_backward(
        d_first, stored[0], geometry_now, kernels[0], gain_all[0]
    )
    return (
        (grad_masked + d_base) * pix_mask,
        (first_kernels, second_kernels),
        (first_norms, second_norms),
    )


def running_update(mean_now, var_now, layer_stats, geometry_now):
    pix_count = geometry_now[2]
    spec_count = geometry_now[3]
    counts = jnp.concatenate(
        [
            jnp.full((CS,), pix_count, jnp.float32),
            jnp.full((2 * CS,), spec_count, jnp.float32),
            jnp.full((CL + CG,), pix_count, jnp.float32),
        ]
    )
    batch_means = jnp.stack([layer_stats[0][0], layer_stats[1][0]])
    batch_vars = jnp.stack([layer_stats[0][1], layer_stats[1][1]])
    new_mean = (1.0 - MOMENTUM) * mean_now + MOMENTUM * batch_means
    new_var = (1.0 - MOMENTUM) * var_now + MOMENTUM * batch_vars * counts / (counts - 1.0)
    return (new_mean, new_var)


def on_device(
    inputs,
    cotangent,
    shapes,
    local_to_local,
    global_to_local,
    local_to_global,
    spec_reduce,
    spec_mix,
    spec_expand,
    norm_gains,
    norm_biases,
    run_means,
    run_vars,
):
    section_id = lax.axis_index("section")
    band_index = lax.axis_index("dp")
    n_dp = lax.axis_size("dp")
    micro_count = inputs.shape[0]
    map_count = inputs.shape[1]
    band_size = inputs.shape[2]
    freq_total = (LONG // 2 + n_dp) // n_dp * n_dp
    freq_local = freq_total // n_dp
    kernels = []
    for layer_pos in range(2):
        local_kernel = jnp.concatenate(
            [local_to_local[0, layer_pos], global_to_local[0, layer_pos]], axis=1
        )
        kernels.append(
            (
                local_kernel,
                local_to_global[0, layer_pos],
                spec_reduce[0, layer_pos],
                spec_mix[0, layer_pos],
                spec_expand[0, layer_pos],
            )
        )
    gain_all = norm_gains[0]
    bias_all = norm_biases[0]
    received = jnp.zeros(inputs.shape[1:], jnp.bfloat16)
    run_mean = run_means[0]
    run_var = run_vars[0]
    outputs = jnp.zeros(inputs.shape, jnp.bfloat16)
    saved_inputs = []
    saved_geometry = []
    for tick_pos in range(micro_count + 1):
        micro_index = tick_pos - section_id
        is_valid = (micro_index >= 0) & (micro_index < micro_count)
        micro_slot = jnp.clip(micro_index, 0, micro_count - 1)
        own_input = lax.dynamic_index_in_dim(inputs, micro_slot, 0, keepdims=False)
        block_in = jnp.where(section_id == 0, own_input, received)
        shape_row = lax.dynamic_index_in_dim(shapes, micro_slot, 0, keepdims=False)
        geometry_now = geometry(shape_row, band_index, band_size, freq_total, freq_local, map_count)
        block_out, stored, layer_stats = block_forward(
            block_in, geometry_now, kernels, gain_all, bias_all
        )
        new_mean, new_var = running_update(run_mean, run_var, layer_stats, geometry_now)
        run_mean = jnp.where(is_valid, new_mean, run_mean)
        run_var = jnp.where(is_valid, new_var, run_var)
        updated = lax.dynamic_update_index_in_dim(outputs, block_out, micro_slot, 0)
        outputs = jnp.where(is_valid, updated, outputs)
        saved_inputs.append(block_in)
        saved_geometry.append(geometry_now)
        if tick_pos < micro_count:
            received = from_behind(block_out, "section", 1)
    kernel_acc = [jnp.zeros((2,) + part_now.shape, jnp.float32) for part_now in kernels[0]]
    gain_acc = jnp.zeros(gain_all.shape, jnp.float32)
    bias_acc = jnp.zeros(bias_all.shape, jnp.float32)
    received_grad = jnp.zeros(inputs.shape[1:], jnp.bfloat16)
    grads_out = jnp.zeros(inputs.shape, jnp.float32)
    for tick_pos in range(micro_count + 1):
        micro_index = micro_count - tick_pos - section_id
        is_valid = (micro_index >= 0) & (micro_index < micro_count)
        micro_slot = jnp.clip(micro_index, 0, micro_count - 1)
        scale_valid = is_valid.astype(jnp.float32)
        forward_tick = micro_count - tick_pos
        geometry_now = saved_geometry[forward_tick]
        recomputed = block_forward(
            saved_inputs[forward_tick], geometry_now, kernels, gain_all, bias_all
        )
        stored = recomputed[1]
        own_grad = lax.dynamic_index_in_dim(cotangent, micro_slot, 0, keepdims=False)
        grad_in = jnp.where(section_id == 1, own_grad, received_grad).astype(jnp.float32)
        grad_input, kernel_grads, norm_grads = block_backward(
            grad_in, stored, geometry_now, kernels, gain_all
        )
        sent_grad = grad_input.astype(jnp.bfloat16)
        kept_grad = jnp.where(section_id == 1, sent_grad.astype(jnp.float32), grad_input)
        updated = lax.dynamic_update_index_in_dim(grads_out, kept_grad, micro_slot, 0)
        grads_out = jnp.where(is_valid, updated, grads_out)
        stacked = [
            jnp.stack([kernel_grads[0][part_pos], kernel_grads[1][part_pos]]) * scale_valid
            for part_pos in range(5)
        ]
        gain_acc = gain_acc + jnp.stack([norm_grads[0][0], norm_grads[1][0]]) * scale_valid
        bias_acc = bias_acc + jnp.stack([norm_grads[0][1], norm_grads[1][1]]) * scale_valid
        kernel_acc = [acc_part + new_part for acc_part, new_part in zip(kernel_acc, stacked)]
        if tick_pos < micro_count:
            received_grad = from_behind(sent_grad, "section", -1)
    totals = lax.psum(
        (kernel_acc[0], kernel_acc[1], kernel_acc[2], kernel_acc[3], kernel_acc[4]), "dp"
    )
    grad_ll = totals[0][:, :, :CL, :]
    grad_gl = totals[0][:, :, CL:, :]
    return (
        outputs[None],
        grads_out[None],
        grad_ll[None],
        grad_gl[None],
        totals[1][None],
        totals[2][None],
        totals[3][None],
        totals[4][None],
        gain_acc[None],
        bias_acc[None],
        run_mean[None],
        run_var[None],
    )


F32 = jnp.float32
BF16 = jnp.bfloat16
MESH = pl.DeviceIdType.MESH
MEMBERS = 16
ROWS = 8
LAYERS = 4
PAIRS = 4
HALF = 192
FULL = 384
SLOTS = 640
PIECES = 32
EARLY = 272
LATE = 64
AT_KL = 0
AT_KG = 4608
AT_E = 8064
AT_M = 0
AT_R = 1152
SECTION_NAMES = ("one", "two", "out")


def dot(a, b):
    return lax.dot_general(a, b, (((1,), (0,)), ((), ())), preferred_element_type=F32)


def dot_nt(a, b):
    return lax.dot_general(a, b, (((1,), (1,)), ((), ())), preferred_element_type=F32)


def dot_tn(a, b):
    return lax.dot_general(a, b, (((0,), (0,)), ((), ())), preferred_element_type=F32)


def sigmoid(v):
    return 0.5 * jnp.tanh(0.5 * v) + 0.5


def fold(v):
    return jnp.sum(v.reshape(v.shape[0] // 8, 8, v.shape[1]), axis=0)


def wide(row, lanes):
    whole, rest = divmod(lanes, 128)
    parts = [row] * whole + ([row[:, :rest]] if rest else [])
    return jnp.concatenate(parts, axis=1)


def network_kernel(
    inputs, cot, shapes, ll, gl, lg, red, mix, exp, gains, biases, run_m, run_v,
    out_y, out_g, out_we, out_wl, out_gains, out_biases, out_m, out_v,
    w_c, w_gl, w_r, w_m, w_e, raw_g, raw_b, pars, acts, shifted, halo, v1, u, spec, mixed, tsum, v34,
    pmask, qmask, tf, tft, tg, tgt, hf, hi, vab, e2, dq, ds, g, gblk, at,
    gwe, gwl, rbe, rbl, fine, finl,
    ssum, rsum, send, recv, stats, stats_far,
    sem_w, sem_in, sem_cot, sem_halo_s, sem_halo_r, sem_ar_s, sem_ar_r, sem_aa_s, sem_aa_r,
    sem_y_s, sem_y_r, sem_g_s, sem_g_r, sem_rs, sem_rr, sem_st,
):
    s = lax.axis_index("section")
    d = lax.axis_index("dp")
    n_dp = lax.axis_size("dp")
    per = n_dp // 2
    grp = lax.div(d, per)

    def differ(a, b):
        return a + b - 2 * a * b

    half = differ(s, grp)
    me = lax.rem(d, per) + per * half
    first = (me == 0).astype(F32)

    def member(group, k):
        return (differ(lax.div(k, per), group), group * per + lax.rem(k, per))

    barrier = pltpu.get_barrier_semaphore()
    total = 2 * n_dp
    flat = s * n_dp + d

    def greet(i, c):
        other = lax.rem(flat + 1 + i, total)
        pl.semaphore_signal(
            barrier, inc=1, device_id=(lax.div(other, n_dp), lax.rem(other, n_dp)), device_id_type=MESH
        )
        return c

    lax.fori_loop(0, total - 1, greet, 0)

    own = pl.ds(2 * s, 2)
    places = [
        (red, w_r.at[own]),
        (gains, raw_g.at[s]),
        (biases, raw_b.at[s]),
        (ll, w_c.at[own, :, :, 0:CL]),
        (lg, w_c.at[own, :, :, CL:]),
        (gl, w_gl.at[own]),
        (mix, w_m.at[own]),
        (exp, w_e.at[own]),
    ]
    local_w = [pltpu.make_async_copy(a, b, sem_w.at[0, i]) for i, (a, b) in enumerate(places)]
    for c in local_w:
        c.start()

    pl.semaphore_wait(barrier, total - 1)

    across = (s, lax.rem(d + per, n_dp))
    stays = s == 0

    def across_copy(source, target, sems):
        return pltpu.make_async_remote_copy(
            source, target, sems.at[0], sems.at[1], device_id=across, device_id_type=MESH
        )

    def when_far(do):
        pl.when(jnp.logical_not(stays))(do)

    input_near = lambda: pltpu.make_async_copy(inputs.at[half], acts.at[0], sem_in.at[0])
    input_far = lambda: across_copy(inputs.at[half], acts.at[0], sem_in)
    cot_near = lambda: pltpu.make_async_copy(cot.at[half], gblk.at[1], sem_cot.at[0, 0])

    def cot_far(row):
        return across_copy(cot.at[half, row], gblk.at[1, row], sem_cot.at[row])

    def rows_in_pieces(parity, window, do):
        row = 5 * parity + window
        pl.when(row < ROWS)(lambda: do(row))

    pl.when(stays)(lambda: input_near().start())
    when_far(lambda: input_far().start())
    partner = (1 - s, d)
    remote_w = [
        pltpu.make_async_remote_copy(
            a, b, sem_w.at[1, i], sem_w.at[2, i], device_id=partner, device_id_type=MESH
        )
        for i, (a, b) in enumerate(places)
    ]
    for c in remote_w:
        c.start()

    height = shapes[grp, 0]
    width = shapes[grp, 1]
    col = lax.broadcasted_iota(jnp.int32, (128, 128), 0)
    for q in range(PAIRS):
        for h in range(2):
            row_ok = (ROWS * me + 2 * q + h < height).astype(F32)
            pmask[q, h * 128 : (h + 1) * 128, :] = (col < width).astype(F32) * row_ok
    for f in range(4):
        f_ok = (4 * me + f <= lax.div(width, 2)).astype(F32)
        qmask[f * 128 : (f + 1) * 128, :] = (col < height).astype(F32) * f_ok
    qmask[512:640, :] = (col < height).astype(F32) * (64 <= lax.div(width, 2)).astype(F32) * first

    def inverse(count, less=0):
        return 1.0 / jnp.full((1, 128), (count - less).astype(F32))

    inv_n = inverse(height * width)
    inv_ns = inverse(height * (lax.div(width, 2) + 1))

    row_a = lax.broadcasted_iota(jnp.int32, (128, 512), 0)
    col_a = lax.broadcasted_iota(jnp.int32, (128, 512), 1)
    r_of = (col_a >> 5) * 8 + ((col_a & 31) >> 3) * 2 + (col_a & 1)
    sel_r = (row_a == r_of).astype(F32).astype(BF16)
    f_of = (col_a >> 1) & 3
    row_b = lax.broadcasted_iota(jnp.int32, (512, 128), 0)
    col_b = lax.broadcasted_iota(jnp.int32, (512, 128), 1)
    r_ob = (row_b >> 5) * 8 + ((row_b & 31) >> 3) * 2 + (row_b & 1)
    sel_rt = (col_b == r_ob).astype(F32).astype(BF16)
    f_ob = (row_b >> 1) & 3
    position = lax.broadcasted_iota(jnp.int32, (128, 128), 0)
    other_axis = lax.broadcasted_iota(jnp.int32, (128, 128), 1)

    def wave(index, side, limit, turn):
        side_real = jnp.full((128, 128), side.astype(F32))
        product = (index * other_axis).astype(F32)
        phase = product - side_real * jnp.floor((product + 0.5) / side_real)
        value = jnp.cos(phase * (2.0 * jnp.pi / side_real) + turn) * lax.rsqrt(side_real)
        return jnp.where((index < limit) & (other_axis < side), value, 0.0)

    half_turn = 0.5 * jnp.pi
    for part in range(2):
        base = wave(position, height, height, -half_turn * part).astype(BF16)
        spread = dot(base, sel_r)
        spread_t = dot(sel_rt, base)
        for f in range(4):
            hf[f, part * 128 : (part + 1) * 128, :] = jnp.where(f_of == f, spread, 0.0).astype(BF16)
            at_col = part * 512 + f * 128
            hi[:, at_col : at_col + 128] = jnp.where(f_ob == f, spread_t, 0.0).astype(BF16)
    row_c = lax.broadcasted_iota(jnp.int32, (128, 128), 0)
    sel_f = ((row_c >> 1) == lax.broadcasted_iota(jnp.int32, (128, 128), 1)).astype(F32).astype(BF16)
    half_width = lax.div(width, 2)
    lifted = jnp.where(position == 0, 64, position)
    waves = (
        wave(position, width, half_width + 1, 0.0),
        wave(lifted, width, half_width + 1, jnp.where(position == 0, 0.0, half_turn)),
    )
    weight = jnp.where((position == 0) | (position == half_width), 1.0, 2.0)
    for which, (plain, flipped_table) in enumerate(((tf, tft), (tg, tgt))):
        for part in range(2):
            spread = dot(sel_f, (waves[part] * weight if which else waves[part]).astype(BF16))
            spread_t = jnp.transpose(spread)
            for h in range(2):
                rows = slice(part * 128, (part + 1) * 128)
                cols = slice(h * 128, (h + 1) * 128)
                plain[rows, cols] = jnp.where((row_c & 1) == h, spread, 0.0).astype(BF16)
                flipped_table[cols, rows] = jnp.where(
                    (lax.broadcasted_iota(jnp.int32, (128, 128), 1) & 1) == h, spread_t, 0.0
                ).astype(BF16)
    stats[...] = jnp.zeros_like(stats)
    ssum[...] = jnp.zeros_like(ssum)
    shifted[0] = jnp.zeros((128, 1536), BF16)
    shifted[9] = jnp.zeros((128, 1536), BF16)
    gwe[...] = jnp.zeros_like(gwe)
    gwl[...] = jnp.zeros_like(gwl)

    def sums_start(slot):
        rsum[slot, me] = ssum[slot]

        def go(i, c):
            k = lax.rem(me + 1 + i, MEMBERS)
            pltpu.make_async_remote_copy(
                ssum.at[slot], rsum.at[slot, me], sem_ar_s.at[slot, k], sem_ar_r.at[slot, me],
                device_id=member(grp, k), device_id_type=MESH,
            ).start()
            return c

        lax.fori_loop(0, MEMBERS - 1, go, 0)

    def sums_wait(slot, lanes):
        def go(i, c):
            k = lax.rem(me + 1 + i, MEMBERS)
            pltpu.make_async_remote_copy(
                ssum.at[slot], rsum.at[slot, k], sem_ar_s.at[slot, k], sem_ar_r.at[slot, k],
                device_id=member(grp, k), device_id_type=MESH,
            ).wait()
            return c

        lax.fori_loop(0, MEMBERS - 1, go, 0)
        tot = jnp.sum(rsum[slot], axis=0)
        tiles = (lanes + 127) // 128
        one = jnp.concatenate([tot[i : i + 1] for i in range(tiles)], axis=1)[:, :lanes]
        two = jnp.concatenate([tot[4 + i : 5 + i] for i in range(tiles)], axis=1)[:, :lanes]
        return one, two

    def put_sums(slot, one, two):
        lanes = one.shape[1]
        for base_row, part in ((0, one), (4, two)):
            flat_part = jnp.sum(part, axis=0, keepdims=True)
            for i in range((lanes + 127) // 128):
                w = min(128, lanes - i * 128)
                ssum[slot, base_row + i : base_row + i + 1, 0:w] = flat_part[:, i * 128 : i * 128 + w]

    def swap_start(slot):
        recv[slot, me] = send[slot, me]

        def go(i, c):
            k = lax.rem(me + 1 + i, MEMBERS)
            pltpu.make_async_remote_copy(
                send.at[slot, k], recv.at[slot, me], sem_aa_s.at[slot, k], sem_aa_r.at[slot, me],
                device_id=member(grp, k), device_id_type=MESH,
            ).start()
            return c

        lax.fori_loop(0, MEMBERS - 1, go, 0)

    def swap_wait(slot):
        def go(i, c):
            k = lax.rem(me + 1 + i, MEMBERS)
            pltpu.make_async_remote_copy(
                send.at[slot, k], recv.at[slot, k], sem_aa_s.at[slot, k], sem_aa_r.at[slot, k],
                device_id=member(grp, k), device_id_type=MESH,
            ).wait()
            return c

        lax.fori_loop(0, MEMBERS - 1, go, 0)

    def halo_copies():
        up = lambda: pltpu.make_async_remote_copy(
            shifted.at[1, :, 512:1024], halo.at[1], sem_halo_s.at[0], sem_halo_r.at[1],
            device_id=member(grp, lax.rem(me + MEMBERS - 1, MEMBERS)), device_id_type=MESH,
        )
        down = lambda: pltpu.make_async_remote_copy(
            shifted.at[8, :, 512:1024], halo.at[0], sem_halo_s.at[1], sem_halo_r.at[0],
            device_id=member(grp, lax.rem(me + 1, MEMBERS)), device_id_type=MESH,
        )
        return up, down

    has_up = me > 0
    has_down = me < MEMBERS - 1

    def halo_start():
        up, down = halo_copies()

        @pl.when(has_up)
        def _():
            up().start()

        @pl.when(has_down)
        def _():
            down().start()

    def put_shifted(index, x, flip):
        at_col = lax.broadcasted_iota(jnp.int32, (128, 512), 0)
        before = jnp.where(at_col == 0, 0.0, pltpu.roll(x, 1, 0))
        after = jnp.where(at_col == 127, 0.0, pltpu.roll(x, 127, 0))
        parts = (after, x, before) if flip else (before, x, after)
        for j, part in enumerate(parts):
            shifted[index, :, j * 512 : (j + 1) * 512] = part.astype(BF16)

    def halo_wait(flip):
        up, down = halo_copies()

        @pl.when(has_up)
        def _():
            up().wait_send()
            down().wait_recv()
            put_shifted(0, halo[0].astype(F32), flip)

        @pl.when(has_down)
        def _():
            down().wait_send()
            up().wait_recv()
            put_shifted(9, halo[1].astype(F32), flip)

    lane = lax.broadcasted_iota(jnp.int32, (128, FULL), 1)
    low = lane < HALF

    def width_out(slot, h, table, get):
        parts = []
        for q in (2 * h, 2 * h + 1):
            x = dot(table[...], get(q))
            both = jnp.concatenate([x[:128], x[128:]], axis=1)
            parts.append(both.reshape(MEMBERS, 8, FULL))
        send[slot, :, pl.ds(pl.multiple_of(16 * h, 16), 16), :] = jnp.concatenate(parts, axis=1).astype(BF16)

    def width_back(slot, h, table):
        block = recv[slot, :, pl.ds(pl.multiple_of(16 * h, 16), 16), :].astype(F32)
        results = []
        for o in range(2):
            z = block[:, 8 * o : 8 * o + 8, :].reshape(128, FULL)
            zi = pltpu.roll(z, HALF, 1)
            stacked = jnp.concatenate([z[:, :HALF], zi[:, :HALF]], axis=0).astype(BF16)
            results.append(dot(table[...], stacked))
        return results

    def rows_forward_into(slot, put):
        x = recv[slot].reshape(512, FULL)
        for f in range(4):
            both = dot(hf[f], x)
            a, b = both[:128], both[128:]
            turned = pltpu.roll(b, HALF, 1)
            if f == 0:
                rest = 1.0 - first
                put(0, jnp.where(low, a + rest * turned, rest * a - turned))
                put(4, jnp.where(low, pltpu.roll(a, HALF, 1), -b) * first)
            else:
                put(f, jnp.where(low, a + turned, a - turned))

    def rows_inverse_from(slot, get):
        last = get(4)
        for f in range(4):
            v = get(f)
            turned = pltpu.roll(v, HALF, 1)
            if f == 0:
                rest = 1.0 - first
                a = jnp.where(low, v, rest * v + first * pltpu.roll(last, HALF, 1))
                b = jnp.where(low, -turned, rest * turned - first * last)
            else:
                a = v
                b = jnp.where(low, -turned, turned)
            vab[f * 128 : (f + 1) * 128, :] = a.astype(BF16)
            vab[512 + f * 128 : 640 + f * 128, :] = b.astype(BF16)

        def go(c, carry):
            z = dot(hi[pl.ds(pl.multiple_of(c * 256, 256), 256), :], vab[...])
            send[slot, pl.ds(c * 8, 8)] = z.astype(BF16).reshape(8, 32, FULL)
            return carry

        lax.fori_loop(0, 2, go, 0)

    def moments(layer, which, lanes, one, two, inv_count):
        count = wide(inv_count, lanes)
        mean = one * count
        var = two * count - mean * mean
        inv = lax.rsqrt(var + EPSILON)
        stats[layer, which : which + 1, 0:lanes] = mean
        stats[layer, 3 + which : 4 + which, 0:lanes] = inv
        stats[layer, 6 + which : 7 + which, 0:lanes] = var
        scale = pars[layer, which : which + 1, 0:lanes] * inv
        shift = pars[layer, 3 + which : 4 + which, 0:lanes] - mean * scale
        return scale, shift

    def affine(layer, which, lanes):
        mean = stats[layer, which : which + 1, 0:lanes]
        inv = stats[layer, 3 + which : 4 + which, 0:lanes]
        gain = pars[layer, which : which + 1, 0:lanes]
        return mean, inv, gain, pars[layer, 3 + which : 4 + which, 0:lanes]

    def keep_grad_sums(layer, which, lanes, one, two):
        stats[layer, 9 + which : 10 + which, 0:lanes] = one
        stats[layer, 12 + which : 13 + which, 0:lanes] = two

    zero_of = lambda lanes: jnp.zeros((8, lanes), F32)

    def conv_pair(layer, c):
        loc = jnp.zeros((256, 512), F32)
        glo = jnp.zeros((256, 128), F32)
        for i in range(3):
            a_loc = jnp.concatenate(
                [shifted[pl.ds(2 * c + i, 2), :, j * 512 : j * 512 + 128].reshape(256, 128) for j in range(3)], axis=1
            )
            a_glo = jnp.concatenate(
                [shifted[pl.ds(2 * c + i, 2), :, j * 512 + 128 : (j + 1) * 512].reshape(256, 384) for j in range(3)],
                axis=1,
            )
            loc = loc + dot(a_loc, w_c[layer, 3 * i : 3 * i + 3].reshape(384, 512))
            glo = glo + dot(a_glo, w_gl[layer, 3 * i : 3 * i + 3].reshape(1152, 128))
        v34[layer, c, :, 0:CL] = loc[:, :CL] + glo
        v34[layer, c, :, CL:] = loc[:, CL:]

    pl.when(stays)(lambda: input_near().wait())
    when_far(lambda: input_far().wait())
    pl.when(stays)(lambda: cot_near().start())

    def start_row(r, c):
        q = lax.div(r, 2)
        pm = pmask[q, pl.ds(pl.multiple_of(lax.rem(r, 2) * 128, 128), 128), :]
        x = acts[0, r].astype(F32) * wide(pm, 512)
        acts[0, r] = x.astype(BF16)
        put_shifted(1 + r, x, False)
        return c

    lax.fori_loop(0, ROWS, start_row, 0)
    for c in local_w:
        c.wait()
    for c in remote_w:
        c.wait()
    for lay in range(LAYERS):
        for base_row, raw in ((0, raw_g), (3, raw_b)):
            row = raw[lay // 2, lay % 2 : lay % 2 + 1, :]
            pars[lay, base_row : base_row + 1, 0:CS] = row[:, :CS]
            pars[lay, base_row + 1 : base_row + 2, 0:FULL] = row[:, CS : 3 * CS]
            pars[lay, base_row + 2 : base_row + 3, :] = row[:, 3 * CS :]

    def out_copies(source, target, sems, block, row):
        send_sem, arrive_sem = sems
        far = lambda: pltpu.make_async_remote_copy(
            source.at[row], target.at[grp, row], send_sem.at[block, row], arrive_sem.at[grp, row],
            device_id=(block, me), device_id_type=MESH,
        )
        near = lambda: pltpu.make_async_copy(source.at[row], target.at[grp, row], send_sem.at[block, row])
        return (block == s) & (me == d), far, near

    def y_copies(block, row):
        return out_copies(acts.at[2 * block + 2], out_y, (sem_y_s, sem_y_r), block, row)

    def g_copies(block, row):
        return out_copies(gblk.at[1 - block], out_g, (sem_g_s, sem_g_r), block, row)

    def start_out(made):
        here, far, near = made
        pl.when(here)(lambda: near().start())
        pl.when(jnp.logical_not(here))(lambda: far().start())

    def wait_out(made):
        here, far, near = made
        pl.when(here)(lambda: near().wait())
        pl.when(jnp.logical_not(here))(lambda: far().wait_send())

    def forward_window(layer, window):
        parity = lax.rem(layer, 2)

        @pl.when(layer < 2)
        def _():
            rows_in_pieces(parity, window, lambda row: when_far(lambda: cot_far(row).start()))

        @pl.when(layer >= 2)
        def _():
            rows_in_pieces(parity, window, lambda row: start_out(y_copies(0, row)))

    def backward_window(step, window):
        parity = lax.rem(step, 2)

        @pl.when(step < 2)
        def _():
            rows_in_pieces(parity, window, lambda row: start_out(y_copies(1, row)))

        @pl.when(step >= 2)
        def _():
            rows_in_pieces(parity, window, lambda row: start_out(g_copies(1, row)))

    def forward(layer, carry):
        halo_start()

        def reduce_pair(q, sums):
            a = acts[layer, pl.ds(2 * q, 2), :, CL:].reshape(256, CG)
            v = dot_nt(a, w_r[layer])
            v1[layer, q] = v
            return sums[0] + fold(v), sums[1] + fold(v * v)

        put_sums(0, *lax.fori_loop(0, PAIRS, reduce_pair, (zero_of(HALF), zero_of(HALF))))
        sums_start(0)
        forward_window(layer, 0)

        def conv_go(c, carry):
            conv_pair(layer, c)
            return carry

        lax.fori_loop(1, 3, conv_go, 0)
        scale, shift = moments(layer, 0, HALF, *sums_wait(0, HALF), inv_n)

        def spectral_in(h, carry):
            def get(q):
                pre = v1[layer, q] * scale + shift
                x = pre * sigmoid(pre) * wide(pmask[q], HALF)
                u[q] = x
                return x.astype(BF16)

            width_out(0, h, tf, get)
            return carry

        lax.fori_loop(0, 2, spectral_in, 0)
        swap_start(0)
        forward_window(layer, 1)
        halo_wait(False)
        lax.fori_loop(0, 2, lambda c, k: conv_go(3 * c, k), 0)
        swap_wait(0)

        def put(f, y):
            spec[layer, f * 128 : (f + 1) * 128, :] = y.astype(BF16)

        rows_forward_into(0, put)

        def mix_block(f, sums):
            at_row = pl.ds(pl.multiple_of(f * 128, 128), 128)
            v = dot(spec[layer, at_row, :], w_m[layer])
            mixed[layer, at_row, :] = v
            return sums[0] + fold(v), sums[1] + fold(v * v)

        put_sums(1, *lax.fori_loop(0, 5, mix_block, (zero_of(FULL), zero_of(FULL))))
        sums_start(1)
        forward_window(layer, 2)
        scale2, shift2 = moments(layer, 1, FULL, *sums_wait(1, FULL), inv_ns)

        def get_v(f):
            rows = slice(f * 128, (f + 1) * 128)
            pre = mixed[layer, rows, :] * scale2 + shift2
            return pre * sigmoid(pre) * wide(qmask[rows, :], FULL)

        rows_inverse_from(1, get_v)
        swap_start(1)
        forward_window(layer, 3)
        swap_wait(1)

        def spectral_out(h, sums):
            backs = width_back(1, h, tgt)
            one, two = sums
            for o in range(2):
                q = 2 * h + o
                t = (u[q] + backs[o]).astype(BF16)
                tsum[layer, q] = t
                pm = pmask[q]
                v_loc = v34[layer, q, :, 0:CL] * pm
                v_glo = (v34[layer, q, :, CL:] + dot(t, w_e[layer])) * wide(pm, CG)
                v34[layer, q, :, 0:CL] = v_loc
                v34[layer, q, :, CL:] = v_glo
                v = jnp.concatenate([v_loc, v_glo], axis=1)
                one = one + fold(v)
                two = two + fold(v * v)
            return one, two

        put_sums(2, *lax.fori_loop(0, 2, spectral_out, (zero_of(512), zero_of(512))))
        sums_start(2)
        forward_window(layer, 4)
        scale3, shift3 = moments(layer, 2, 512, *sums_wait(2, 512), inv_n)
        odd = lax.rem(layer, 2)
        oddf = odd.astype(F32)

        def next_row(r, carry):
            q = lax.div(r, 2)
            here = pl.ds(pl.multiple_of(lax.rem(r, 2) * 128, 128), 128)
            pre = v34[layer, q, here, :] * scale3 + shift3
            x = pre * sigmoid(pre) * wide(pmask[q, here, :], 512)
            x = x + oddf * acts[layer - odd, r].astype(F32)
            acts[layer + 1, r] = x.astype(BF16)

            @pl.when(layer < LAYERS - 1)
            def _():
                put_shifted(1 + r, x, False)

            return carry

        lax.fori_loop(0, ROWS, next_row, 0)

        return carry

    lax.fori_loop(0, LAYERS, forward, 0)

    pl.when(stays)(lambda: cot_near().wait())

    def cot_wait(row, c):
        when_far(lambda: cot_far(row).wait())
        return c

    lax.fori_loop(0, ROWS, cot_wait, 0)

    def cot_row(r, c):
        q = lax.div(r, 2)
        here = pl.ds(pl.multiple_of(lax.rem(r, 2) * 128, 128), 128)
        x = gblk[1, r].astype(F32) * wide(pmask[q, here, :], 512)
        gblk[1, r] = x.astype(BF16)
        g[q, here, :] = x
        return c

    lax.fori_loop(0, ROWS, cot_row, 0)

    x_bit = lax.rem(d, 2)
    y_bit = lax.rem(lax.div(d, 2), 2)
    at_x = jnp.where(s == 0, x_bit, y_bit)
    at_y = jnp.where(s == 0, y_bit, x_bit)
    at_z = lax.div(d, 4)
    step_x = jnp.where(s == 0, 1, 2)
    step_y = 3 - step_x
    in_core = s * 16
    in_x = in_core + at_x * 8
    in_y = in_x + at_y * 4
    near_x = (s, d + step_x * (1 - 2 * at_x))
    near_y = (s, d + step_y * (1 - 2 * at_y))

    def sum_part(p, layer):
        gw, rb, fin, out, rows = ((gwe, rbe, fine, out_we, EARLY), (gwl, rbl, finl, out_wl, LATE))[p]
        block = lax.div(layer, 2)
        odd = lax.rem(layer, 2)
        slot = jnp.where(block == s, 2, 0) + odd

        def remote(stage, source, target, other, n=0):
            return pltpu.make_async_remote_copy(
                source, target, sem_rs.at[p, odd, stage, n], sem_rr.at[p, odd, stage, n], device_id=other, device_id_type=MESH
            )

        def rows_of(first_piece, pieces):
            return pl.ds(pl.multiple_of(first_piece * rows, rows), pieces * rows)

        one = lambda: remote(0, gw.at[rows_of((1 - s) * 16, 16)], rb.at[rows_of(0, 16)], partner)
        far_x = in_core + (1 - at_x) * 8

        def two(n):
            first_four = (1 - at_y) * 4 if n == 0 else at_y * 4
            return remote(1, gw.at[rows_of(far_x + first_four, 4)], rb.at[rows_of(16 + first_four, 4)], near_x, n)

        three = lambda: remote(2, gw.at[rows_of(in_x + (1 - at_y) * 4, 4)], rb.at[rows_of(24, 4)], near_y)

        def add(first_piece, from_piece, pieces):
            def go(i, carry):
                here = rows_of(first_piece + i, 1)
                there = rows_of(from_piece + i, 1)
                gw[here, :] = (gw[here, :].astype(F32) + rb[there, :].astype(F32)).astype(BF16)
                return carry

            lax.fori_loop(0, pieces, go, 0)

        def along_z(i):
            other = lax.rem(at_z + 1 + i, 4)
            return other, (s, d + 4 * (other - at_z))

        def four(i, arriving):
            other, device = along_z(i)
            return pltpu.make_async_remote_copy(
                gw.at[rows_of(in_y + other, 1)],
                rb.at[rows_of(28 + (other if arriving else at_z), 1)],
                sem_rs.at[p, odd, 3, i], sem_rr.at[p, odd, 3, other if arriving else at_z],
                device_id=device, device_id_type=MESH,
            )

        def five(i, arriving):
            other, device = along_z(i)
            return pltpu.make_async_remote_copy(
                fin, out.at[slot, rows_of(in_y + (other if arriving else at_z), 1)],
                sem_rs.at[p, odd, 4, i], sem_rr.at[p, odd, 4, other if arriving else at_z],
                device_id=device, device_id_type=MESH,
            )

        five_own = lambda: pltpu.make_async_copy(fin, out.at[slot, rows_of(in_y + at_z, 1)], sem_rs.at[p, odd, 4, 3])

        def spread_copy(stage, first_piece, other, n=0):
            here = out.at[slot, rows_of(first_piece, 4)]
            return remote(stage, here, here, other, n)

        six = lambda: spread_copy(5, in_y, near_y)
        seven = lambda n: spread_copy(6, in_y if n == 0 else in_x + (1 - at_y) * 4, near_x, n)
        eight = lambda: remote(
            7, out.at[odd, rows_of(in_core, 16)],
            out.at[2 + odd, rows_of(in_core, 16)], partner,
        )
        starts = s != block

        def begin_one():
            one().start()

        def begin_two():
            one().wait()
            add(in_core, 0, 16)
            two(0).start()

        def begin_three():
            two(0).wait()
            add(in_x + (1 - at_y) * 4, 16 + (1 - at_y) * 4, 4)
            two(1).start()
            three().start()

        def begin_four():
            two(1).wait()
            three().wait()
            add(in_y, 16 + at_y * 4, 4)
            add(in_y, 24, 4)
            for i in range(3):
                four(i, False).start()

        def begin_five():
            total_now = gw[rows_of(in_y + at_z, 1), :].astype(F32)
            for i in range(3):
                four(i, False).wait_send()
                four(i, True).wait_recv()
                total_now = total_now + rb[rows_of(28 + lax.rem(at_z + 1 + i, 4), 1), :].astype(F32)
            fin[...] = total_now.astype(BF16)
            five_own().start()
            for i in range(3):
                five(i, False).start()

        def begin_six():
            five_own().wait()
            for i in range(3):
                five(i, False).wait_send()
                five(i, True).wait_recv()
            six().start()
            seven(0).start()

        def begin_seven():
            six().wait()
            seven(0).wait()
            seven(1).start()

        def begin_eight():
            seven(1).wait()
            pl.when(starts)(lambda: eight().start())

        def end():
            pl.when(starts)(lambda: eight().wait_send())
            pl.when(jnp.logical_not(starts))(lambda: eight().wait_recv())

        return (
            begin_one, begin_two, begin_three, begin_four, begin_five,
            begin_six, begin_seven, begin_eight, end,
        )

    def stage(p, layer, which):
        pl.when(layer < LAYERS)(lambda: sum_part(p, layer)[which]())

    def backward(step, carry):
        layer = LAYERS - 1 - step
        mean3, inv3, gain3, bias3 = affine(layer, 2, 512)
        scale3 = gain3 * inv3
        shift3 = bias3 - mean3 * scale3

        def slope_row(r, sums):
            q = lax.div(r, 2)
            here = pl.ds(pl.multiple_of(lax.rem(r, 2) * 128, 128), 128)
            v = v34[layer, q, here, :]
            pre = v * scale3 + shift3
            sg = sigmoid(pre)
            e = g[q, here, :] * wide(pmask[q, here, :], 512) * (sg * (1.0 + pre * (1.0 - sg)))
            g[q, here, :] = e
            return sums[0] + fold(e), sums[1] + fold(e * ((v - mean3) * inv3))

        put_sums(3, *lax.fori_loop(0, ROWS, slope_row, (zero_of(512), zero_of(512))))
        sums_start(3)
        backward_window(step, 0)

        def turn_row(r, carry):
            at[:, pl.ds(pl.multiple_of(r * 128, 128), 128)] = jnp.transpose(acts[layer, r])
            return carry

        lax.fori_loop(0, ROWS, turn_row, 0)
        stage(0, layer + 1, 4)
        stage(1, layer + 1, 1)
        stage(1, layer + 2, 6)
        one3, two3 = sums_wait(3, 512)
        keep_grad_sums(layer, 2, 512, one3, two3)
        part_a = one3 * wide(inv_n, 512)
        part_b = two3 * wide(inv_n, 512)

        def d_row(r, carry):
            q = lax.div(r, 2)
            here = pl.ds(pl.multiple_of(lax.rem(r, 2) * 128, 128), 128)
            z = (v34[layer, q, here, :] - mean3) * inv3
            dv = wide(pmask[q, here, :], 512) * scale3 * (g[q, here, :] - part_a - z * part_b)
            put_shifted(1 + r, dv, True)
            return carry

        lax.fori_loop(0, ROWS, d_row, 0)
        halo_start()

        def grad_out(h, carry):
            def get(q):
                dg = shifted[pl.ds(1 + 2 * q, 2), :, 512 + CL : 1024].reshape(256, CG)
                dt = dot_nt(dg, w_e[layer])
                u[q] = dt
                return dt.astype(BF16)

            width_out(0, h, tg, get)
            return carry

        lax.fori_loop(0, 2, grad_out, 0)
        swap_start(0)
        backward_window(step, 1)
        halo_wait(True)
        stage(1, layer + 2, 7)

        for i in range(3):
            def lift_grad(i=i):
                acc = jnp.zeros((128, 1152), F32)
                for q in range(PAIRS):
                    rows = slice(2 * q + 2 - i, 2 * q + 4 - i)
                    dd = jnp.concatenate(
                        [shifted[rows, :, j * 512 + CL : (j + 1) * 512].reshape(256, CG) for j in range(3)], axis=1
                    )
                    acc = acc + dot(at[0:CL, q * 256 : (q + 1) * 256], dd)
                for n in range(9):
                    base = AT_KG + (9 * i + n) * 128
                    gwe[base : base + 128, :] = acc[:, n * 128 : (n + 1) * 128].astype(BF16)
            lift_grad()
        def local_grad(c, carry):
            for i in range(3):
                acc = jnp.zeros((128, 384), F32)
                for q in range(PAIRS):
                    rows = slice(2 * q + 2 - i, 2 * q + 4 - i)
                    dd = jnp.concatenate(
                        [shifted[rows, :, j * 512 : j * 512 + CL].reshape(256, CL) for j in range(3)], axis=1
                    )
                    acc = acc + dot(at[pl.ds(pl.multiple_of(c * 128, 128), 128), q * 256 : (q + 1) * 256], dd)
                for j in range(3):
                    base = pl.multiple_of(AT_KL + (3 * i + j) * 512 + c * 128, 128)
                    gwe[pl.ds(base, 128), :] = acc[:, j * 128 : (j + 1) * 128].astype(BF16)
            return carry

        lax.fori_loop(0, 4, local_grad, 0)
        acc_e = jnp.zeros((HALF, CG), F32)
        for q in range(PAIRS):
            dg = shifted[1 + 2 * q : 3 + 2 * q, :, 512 + CL : 1024].reshape(256, CG)
            acc_e = acc_e + dot_tn(tsum[layer, q], dg)
        for n in range(3):
            gwe[AT_E + n * HALF : AT_E + (n + 1) * HALF, :] = acc_e[:, n * 128 : (n + 1) * 128].astype(BF16)
        stage(0, layer, 0)
        stage(0, layer + 1, 5)
        stage(1, layer + 1, 2)

        def conv_back(c, carry):
            d_loc = jnp.zeros((256, 128), F32)
            d_glo = jnp.zeros((256, 384), F32)
            for i in range(3):
                for j in range(3):
                    rows = pl.ds(2 * c + 2 - i, 2)
                    dd = shifted[rows, :, j * 512 : (j + 1) * 512].reshape(256, 512)
                    d_loc = d_loc + dot_nt(dd, w_c[layer, 3 * i + j])
                    d_glo = d_glo + dot_nt(dd[:, :CL], w_gl[layer, 3 * i + j])
            g[c, :, 0:CL] = d_loc
            g[c, :, CL:] = d_glo
            return carry

        swap_wait(0)

        def put(f, y):
            e2[f * 128 : (f + 1) * 128, :] = y

        rows_forward_into(0, put)
        mean2, inv2, gain2, bias2 = affine(layer, 1, FULL)
        scale2 = gain2 * inv2
        shift2 = bias2 - mean2 * scale2

        def slope_block(f, sums):
            rows = pl.ds(pl.multiple_of(f * 128, 128), 128)
            v = mixed[layer, rows, :]
            pre = v * scale2 + shift2
            sg = sigmoid(pre)
            e = e2[rows, :] * wide(qmask[rows, :], FULL) * (sg * (1.0 + pre * (1.0 - sg)))
            e2[rows, :] = e
            return sums[0] + fold(e), sums[1] + fold(e * ((v - mean2) * inv2))

        put_sums(1, *lax.fori_loop(0, 5, slope_block, (zero_of(FULL), zero_of(FULL))))
        sums_start(1)
        backward_window(step, 2)


        stage(0, layer, 1)
        stage(1, layer + 2, 8)
        stage(0, layer + 1, 6)
        stage(1, layer + 1, 3)
        lax.fori_loop(0, 2, conv_back, 0)
        one2, two2 = sums_wait(1, FULL)
        keep_grad_sums(layer, 1, FULL, one2, two2)
        part_a2 = one2 * wide(inv_ns, FULL)
        part_b2 = two2 * wide(inv_ns, FULL)

        def dq_block(f, carry):
            rows = pl.ds(pl.multiple_of(f * 128, 128), 128)
            z = (mixed[layer, rows, :] - mean2) * inv2
            dv = wide(qmask[rows, :], FULL) * scale2 * (e2[rows, :] - part_a2 - z * part_b2)
            low_dv = dv.astype(BF16)
            dq[rows, :] = low_dv
            e2[rows, :] = dot_nt(low_dv, w_m[layer])
            return carry

        lax.fori_loop(0, 5, dq_block, 0)
        rows_inverse_from(1, lambda f: e2[f * 128 : (f + 1) * 128, :])
        swap_start(1)
        backward_window(step, 3)

        stage(0, layer, 2)
        stage(0, layer + 1, 7)
        stage(1, layer + 1, 4)
        lax.fori_loop(2, PAIRS, conv_back, 0)
        acc_m = jnp.zeros((FULL, FULL), F32)
        for f in range(5):
            rows = slice(f * 128, (f + 1) * 128)
            acc_m = acc_m + dot_tn(spec[layer, rows, :], dq[rows, :])
        for n in range(3):
            gwl[AT_M + n * FULL : AT_M + (n + 1) * FULL, :] = acc_m[:, n * 128 : (n + 1) * 128].astype(BF16)
        swap_wait(1)

        mean1, inv1, gain1, bias1 = affine(layer, 0, HALF)
        scale1 = gain1 * inv1
        shift1 = bias1 - mean1 * scale1

        def slope_in(h, sums):
            backs = width_back(1, h, tft)
            one, two = sums
            for o in range(2):
                q = 2 * h + o
                v = v1[layer, q]
                pre = v * scale1 + shift1
                sg = sigmoid(pre)
                e = (u[q] + backs[o]) * wide(pmask[q], HALF) * (sg * (1.0 + pre * (1.0 - sg)))
                u[q] = e
                one = one + fold(e)
                two = two + fold(e * ((v - mean1) * inv1))
            return one, two

        put_sums(0, *lax.fori_loop(0, 2, slope_in, (zero_of(HALF), zero_of(HALF))))
        sums_start(0)
        backward_window(step, 4)
        stage(0, layer, 3)
        stage(0, layer + 1, 8)
        stage(1, layer + 1, 5)
        one1, two1 = sums_wait(0, HALF)
        keep_grad_sums(layer, 0, HALF, one1, two1)
        part_a1 = one1 * wide(inv_n, HALF)
        part_b1 = two1 * wide(inv_n, HALF)

        def ds_pair(q, carry):
            z = (v1[layer, q] - mean1) * inv1
            dv = wide(pmask[q], HALF) * scale1 * (u[q] - part_a1 - z * part_b1)
            low_dv = dv.astype(BF16)
            ds[q] = low_dv
            g[q, :, CL:] = g[q, :, CL:] + dot(low_dv, w_r[layer])
            return carry

        lax.fori_loop(0, PAIRS, ds_pair, 0)
        acc_r = jnp.zeros((HALF, CG), F32)
        for q in range(PAIRS):
            a = acts[layer, 2 * q : 2 * q + 2, :, CL:].reshape(256, CG)
            acc_r = acc_r + dot_tn(ds[q], a)
        for n in range(3):
            gwl[AT_R + n * HALF : AT_R + (n + 1) * HALF, :] = acc_r[:, n * 128 : (n + 1) * 128].astype(BF16)

        stage(1, layer, 0)

        @pl.when(lax.rem(layer, 2) == 0)
        def _():
            block = lax.div(layer, 2)

            def close_row(r, carry):
                q = lax.div(r, 2)
                here = pl.ds(pl.multiple_of(lax.rem(r, 2) * 128, 128), 128)
                x = (gblk[block, r].astype(F32) + g[q, here, :]) * wide(pmask[q, here, :], 512)
                low_x = x.astype(BF16)
                gblk[1 - block, r] = low_x
                g[q, here, :] = low_x.astype(F32)

                return carry

            lax.fori_loop(0, ROWS, close_row, 0)

        @pl.when(layer == 0)
        def _():
            def close(row, carry):
                start_out(g_copies(0, row))
                return carry

            lax.fori_loop(0, ROWS, close, 0)

        return carry

    lax.fori_loop(0, LAYERS, backward, 0)

    for which in range(1, 9):
        if which < 6:
            stage(0, 0, which + 3)
        if which < 4:
            stage(1, 1, which + 5)
        stage(1, 0, which)

    far = pltpu.make_async_remote_copy(
        stats, stats_far, sem_st.at[0], sem_st.at[1],
        device_id=across, device_id_type=MESH,
    )
    far.start()
    for block in range(2):
        def sent(row, carry, block=block):
            wait_out(y_copies(block, row))
            wait_out(g_copies(block, row))
            return carry

        lax.fori_loop(0, ROWS, sent, 0)
    for m in range(2):
        sender = member(m, d)
        from_self = (sender[0] == s) & (sender[1] == d)

        def arrived(row, carry, m=m):
            for source, target, sems in ((acts, out_y, (sem_y_s, sem_y_r)), (gblk, out_g, (sem_g_s, sem_g_r))):
                pltpu.make_async_remote_copy(
                    source.at[0, row], target.at[m, row], sems[0].at[0, row], sems[1].at[m, row],
                    device_id=partner, device_id_type=MESH,
                ).wait_recv()
            return carry

        @pl.when(jnp.logical_not(from_self))
        def _(arrived=arrived):
            lax.fori_loop(0, ROWS, arrived, 0)

    far.wait()
    for lay in range(2):
        mine = stats[2 * s + lay]
        other = stats_far[2 * s + lay]
        zero_first = jnp.where(grp == 0, mine, other)
        one_next = jnp.where(grp == 0, other, mine)
        row = slice(lay, lay + 1)

        def joined(st, base):
            return jnp.concatenate(
                [st[base : base + 1, :HALF], st[base + 1 : base + 2, :FULL], st[base + 2 : base + 3]], axis=1
            )

        mean = run_m[row, :]
        var = run_v[row, :]
        for m, st in enumerate((zero_first, one_next)):
            pixels = shapes[m, 0] * shapes[m, 1]
            points = shapes[m, 0] * (lax.div(shapes[m, 1], 2) + 1)
            fix = [
                wide(jnp.full((1, 128), count.astype(F32)) * inverse(count, 1), lanes)
                for count, lanes in ((pixels, HALF), (points, FULL), (pixels, 512))
            ]
            mean = (1.0 - MOMENTUM) * mean + MOMENTUM * joined(st, 0)
            var = (1.0 - MOMENTUM) * var + MOMENTUM * joined(st, 6) * jnp.concatenate(fix, axis=1)
        out_m[row, :] = mean
        out_v[row, :] = var
        out_biases[row, :] = joined(zero_first, 9) + joined(one_next, 9)
        out_gains[row, :] = joined(zero_first, 12) + joined(one_next, 12)


def tiles_of(rows, array):
    return jnp.concatenate([array[:, n * rows : (n + 1) * rows].astype(F32) for n in range(3)], axis=-1)


def on_band(
    inputs,
    cotangent,
    shapes,
    local_to_local,
    global_to_local,
    local_to_global,
    spec_reduce,
    spec_mix,
    spec_expand,
    norm_gains,
    norm_biases,
    run_means,
    run_vars,
):
    anywhere = pl.BlockSpec(memory_space=pl.ANY)
    vmem = pl.BlockSpec(memory_space=pltpu.VMEM)
    dma = pltpu.SemaphoreType.DMA
    band = (ROWS, LONG, 512)
    out_y, out_g, out_we, out_wl, *out_norms = pl.pallas_call(
        network_kernel,
        out_shape=(
            jax.ShapeDtypeStruct((2,) + band, BF16),
            jax.ShapeDtypeStruct((2,) + band, BF16),
            jax.ShapeDtypeStruct((4, PIECES * EARLY, 128), BF16),
            jax.ShapeDtypeStruct((4, PIECES * LATE, 128), BF16),
            *[jax.ShapeDtypeStruct((2, 3 * CS + 512), F32)] * 4,
        ),
        in_specs=[anywhere, anywhere, pl.BlockSpec(memory_space=pltpu.SMEM)]
        + [anywhere] * 8
        + [vmem] * 2,
        out_specs=(anywhere,) * 4 + (vmem,) * 4,
        scratch_shapes=[
            pltpu.VMEM((LAYERS, 9, CL, 512), BF16),
            pltpu.VMEM((LAYERS, 9, CG, CL), BF16),
            pltpu.VMEM((LAYERS, CS, CG), BF16),
            pltpu.VMEM((LAYERS, FULL, FULL), BF16),
            pltpu.VMEM((LAYERS, CS, CG), BF16),
            pltpu.VMEM((2, 2, 3 * CS + 512), F32),
            pltpu.VMEM((2, 2, 3 * CS + 512), F32),
            pltpu.VMEM((LAYERS, 8, 512), F32),
            pltpu.VMEM((LAYERS + 1,) + band, BF16),
            pltpu.VMEM((ROWS + 2, LONG, 1536), BF16),
            pltpu.VMEM((2, LONG, 512), BF16),
            pltpu.VMEM((LAYERS, PAIRS, 256, CS), F32),
            pltpu.VMEM((PAIRS, 256, CS), F32),
            pltpu.VMEM((LAYERS, SLOTS, FULL), BF16),
            pltpu.VMEM((LAYERS, SLOTS, FULL), F32),
            pltpu.VMEM((LAYERS, PAIRS, 256, CS), BF16),
            pltpu.VMEM((LAYERS, PAIRS, 256, 512), F32),
            pltpu.VMEM((PAIRS, 256, 128), F32),
            pltpu.VMEM((SLOTS, 128), F32),
            pltpu.VMEM((256, 256), BF16),
            pltpu.VMEM((256, 256), BF16),
            pltpu.VMEM((256, 256), BF16),
            pltpu.VMEM((256, 256), BF16),
            pltpu.VMEM((4, 256, 512), BF16),
            pltpu.VMEM((512, 1024), BF16),
            pltpu.VMEM((1024, FULL), BF16),
            pltpu.VMEM((SLOTS, FULL), F32),
            pltpu.VMEM((SLOTS, FULL), BF16),
            pltpu.VMEM((PAIRS, 256, CS), BF16),
            pltpu.VMEM((PAIRS, 256, 512), F32),
            pltpu.VMEM((2,) + band, BF16),
            pltpu.VMEM((512, ROWS * LONG), BF16),
            pltpu.VMEM((PIECES * EARLY, 128), BF16),
            pltpu.VMEM((PIECES * LATE, 128), BF16),
            pltpu.VMEM((PIECES * EARLY, 128), BF16),
            pltpu.VMEM((PIECES * LATE, 128), BF16),
            pltpu.VMEM((EARLY, 128), BF16),
            pltpu.VMEM((LATE, 128), BF16),
            pltpu.VMEM((4, 8, 128), F32),
            pltpu.VMEM((4, MEMBERS, 8, 128), F32),
            pltpu.VMEM((2, MEMBERS, 32, FULL), BF16),
            pltpu.VMEM((2, MEMBERS, 32, FULL), BF16),
            pltpu.VMEM((LAYERS, 16, 512), F32),
            pltpu.VMEM((LAYERS, 16, 512), F32),
            dma((3, 8)),
            dma((2,)),
            dma((ROWS, 2)),
            dma((2,)),
            dma((2,)),
            dma((4, MEMBERS)),
            dma((4, MEMBERS)),
            dma((2, MEMBERS)),
            dma((2, MEMBERS)),
            dma((2, ROWS)),
            dma((2, ROWS)),
            dma((2, ROWS)),
            dma((2, ROWS)),
            dma((2, 2, 8, 4)),
            dma((2, 2, 8, 4)),
            dma((2,)),
        ],
        compiler_params=pltpu.CompilerParams(
            collective_id=0, has_side_effects=True, vmem_limit_bytes=63 << 20
        ),
        name="network",
    )(
        inputs[:, 0],
        cotangent[:, 0],
        shapes,
        local_to_local[0],
        global_to_local[0],
        local_to_global[0],
        jnp.swapaxes(spec_reduce[0], 1, 2),
        spec_mix[0],
        spec_expand[0],
        norm_gains[0],
        norm_biases[0],
        run_means[0],
        run_vars[0],
    )
    grad_local = out_we[2:, AT_KL:AT_KG].reshape(2, 9, 512, 128)
    grad_lift = out_we[2:, AT_KG:AT_E].reshape(2, 9, 3, 128, 128)
    grad_lift = jnp.concatenate([grad_lift[:, :, n].astype(F32) for n in range(3)], axis=-1)
    grad_expand = tiles_of(CS, out_we[2:, AT_E:])
    grad_mix = tiles_of(FULL, out_wl[2:, AT_M:])
    grad_reduce = jnp.swapaxes(tiles_of(CS, out_wl[2:, AT_R:]), 1, 2)
    out_gains, out_biases, out_means, out_vars = out_norms
    return (
        out_y[None, :, None],
        out_g.astype(F32)[None, :, None],
        grad_local[:, :, :CL].astype(F32)[None],
        grad_local[:, :, CL:].astype(F32)[None],
        grad_lift[None],
        grad_reduce[None],
        grad_mix[None],
        grad_expand[None],
        out_gains[None],
        out_biases[None],
        out_means[None],
        out_vars[None],
    )


def solution(mesh):
    in_specs = (
        P(None, None, "dp", None, None),
        P(None, None, "dp", None, None),
        P(),
        P("section", None, None, None, None),
        P("section", None, None, None, None),
        P("section", None, None, None, None),
        P("section", None, None, None),
        P("section", None, None, None),
        P("section", None, None, None),
        P("section", None, None),
        P("section", None, None),
        P("section", None, None),
        P("section", None, None),
    )
    out_specs = (
        P("section", None, None, "dp", None, None),
        P("section", None, None, "dp", None, None),
        P("section", None, None, None, None),
        P("section", None, None, None, None),
        P("section", None, None, None, None),
        P("section", None, None, None),
        P("section", None, None, None),
        P("section", None, None, None),
        P("section", None, None),
        P("section", None, None),
        P("section", None, None),
        P("section", None, None),
    )
    dp_size = mesh.shape["dp"]
    banded = dp_size == MEMBERS and LONG == dp_size * ROWS
    return jax.shard_map(
        on_band if banded else on_device, mesh=mesh, in_specs=in_specs, out_specs=out_specs, check_vma=False
    )
```

```python
import jax
import jax.numpy as jnp
from jax import lax
from jax.experimental import pallas as pl
from jax.experimental.pallas import tpu as pltpu
from jax.sharding import PartitionSpec as P

CL = 128
CG = 384
CS = 192
LONG = 128


EPSILON = 1e-05
MOMENTUM = 0.1
PRECISE = lax.Precision.HIGHEST


def with_halo(block, sides, width):
    for axis, dim in sides:
        count = lax.axis_size(axis)
        forward = [(i, i + 1) for i in range(count - 1)]
        backward = [(target, source) for source, target in forward]
        low = lax.ppermute(
            lax.slice_in_dim(block, block.shape[dim] - width, None, axis=dim), axis, forward
        )
        high = lax.ppermute(lax.slice_in_dim(block, 0, width, axis=dim), axis, backward)
        block = jnp.concatenate([low, block, high], axis=dim)
    return block


def from_behind(value, axis, steps):
    count = lax.axis_size(axis)
    first, last = (max(0, -steps), min(count, count - steps))
    return lax.ppermute(value, axis, [(source, source + steps) for source in range(first, last)])


def dft_tables(height, width, long_side, freq_total):
    position = jnp.arange(long_side, dtype=jnp.int32)
    frequency = jnp.arange(freq_total, dtype=jnp.int32)
    half_width = width // 2
    width_real = width.astype(jnp.float32)
    height_real = height.astype(jnp.float32)
    width_phase = position[:, None] * frequency[None, :] % width
    width_angle = 2.0 * jnp.pi / width_real * width_phase.astype(jnp.float32)
    width_valid = ((position[:, None] < width) & (frequency[None, :] <= half_width)).astype(
        jnp.float32
    )
    width_scale = lax.rsqrt(width_real)
    fwd_cos = jnp.cos(width_angle) * width_scale * width_valid
    fwd_sin = -jnp.sin(width_angle) * width_scale * width_valid
    edge_freq = (frequency == 0) | (frequency == half_width)
    freq_weight = jnp.where(edge_freq, 1.0, 2.0).astype(jnp.float32)
    inv_cos = freq_weight[:, None] * fwd_cos.T
    inv_sin = freq_weight[:, None] * fwd_sin.T
    height_phase = position[:, None] * position[None, :] % height
    height_angle = 2.0 * jnp.pi / height_real * height_phase.astype(jnp.float32)
    height_valid = ((position[:, None] < height) & (position[None, :] < height)).astype(jnp.float32)
    height_scale = lax.rsqrt(height_real)
    row_cos = jnp.cos(height_angle) * height_scale * height_valid
    row_sin = jnp.sin(height_angle) * height_scale * height_valid
    return (fwd_cos, fwd_sin, inv_cos, inv_sin, row_cos, row_sin)


def geometry(shape_row, band_index, band_size, freq_total, freq_local, map_count):
    height = shape_row[0]
    width = shape_row[1]
    position = jnp.arange(LONG, dtype=jnp.int32)
    band_rows = band_index * band_size + jnp.arange(band_size, dtype=jnp.int32)
    pix_mask = ((band_rows[:, None] < height) & (position[None, :] < width)).astype(jnp.float32)[
        None, :, :, None
    ]
    local_freq = band_index * freq_local + jnp.arange(freq_local, dtype=jnp.int32)
    freq_mask = ((position[:, None] < height) & (local_freq[None, :] <= width // 2)).astype(
        jnp.float32
    )[None, :, :, None]
    pix_count = (map_count * height * width).astype(jnp.float32)
    spec_count = (map_count * height * (width // 2 + 1)).astype(jnp.float32)
    return (pix_mask, freq_mask, pix_count, spec_count, dft_tables(height, width, LONG, freq_total))


def conv_rows(padded, kernel):
    shaped = kernel.reshape(3, 3, kernel.shape[1], kernel.shape[2])
    return lax.conv_general_dilated(
        padded,
        shaped,
        (1, 1),
        "VALID",
        dimension_numbers=("NHWC", "HWIO", "NHWC"),
        preferred_element_type=jnp.float32,
    )


def flipped(kernel):
    shaped = kernel.reshape(3, 3, kernel.shape[1], kernel.shape[2])[::-1, ::-1]
    return jnp.swapaxes(shaped, 2, 3).reshape(9, kernel.shape[2], kernel.shape[1])


def kernel_grad(padded, grad_out, band_size, width):
    tap_grads = []
    for row_tap in range(3):
        for col_tap in range(3):
            window = padded[:, row_tap : row_tap + band_size, col_tap : col_tap + width, :]
            tap_grads.append(
                jnp.einsum("mrwi,mrwo->io", window, grad_out, preferred_element_type=jnp.float32)
            )
    return jnp.stack(tap_grads)


def width_forward(entry, table):
    return jnp.einsum("mrwc,wf->mrfc", entry, table, precision=PRECISE)


def width_forward_adj(entry, table):
    return jnp.einsum("mrfc,wf->mrwc", entry, table, precision=PRECISE)


def width_inverse(entry, table):
    return jnp.einsum("mrfc,fw->mrwc", entry, table, precision=PRECISE)


def width_inverse_adj(entry, table):
    return jnp.einsum("mrwc,fw->mrfc", entry, table, precision=PRECISE)


def height_apply(table, entry):
    return jnp.einsum("kn,mnfc->mkfc", table, entry, precision=PRECISE)


def height_adjoint(table, entry):
    return jnp.einsum("kn,mkfc->mnfc", table, entry, precision=PRECISE)


def rows_forward(row_cos, row_sin, entry):
    half_ch = entry.shape[-1] // 2
    real_in = entry[..., :half_ch]
    imag_in = entry[..., half_ch:]
    real_out = height_apply(row_cos, real_in) + height_apply(row_sin, imag_in)
    imag_out = height_apply(row_cos, imag_in) - height_apply(row_sin, real_in)
    return jnp.concatenate([real_out, imag_out], axis=-1)


def rows_inverse(row_cos, row_sin, entry):
    half_ch = entry.shape[-1] // 2
    real_in = entry[..., :half_ch]
    imag_in = entry[..., half_ch:]
    real_out = height_adjoint(row_cos, real_in) - height_adjoint(row_sin, imag_in)
    imag_out = height_adjoint(row_cos, imag_in) + height_adjoint(row_sin, real_in)
    return jnp.concatenate([real_out, imag_out], axis=-1)


def split_pairs(totals, widths):
    pairs = []
    offset = 0
    for lead_width, tail_width in zip(widths[0::2], widths[1::2]):
        lead_part = totals[offset : offset + lead_width]
        tail_part = totals[offset + lead_width : offset + lead_width + tail_width]
        pairs.append((lead_part, tail_part))
        offset = offset + lead_width + tail_width
    return pairs


def moments(entries, weights):
    pieces = []
    for entry, weight in zip(entries, weights):
        masked = entry * weight
        pieces.append(jnp.sum(masked, axis=(0, 1, 2)))
        pieces.append(jnp.sum(masked * entry, axis=(0, 1, 2)))
    totals = lax.psum(jnp.concatenate(pieces), "dp")
    return split_pairs(totals, [piece.shape[0] for piece in pieces])


def grad_moments(grads_in, normed_in):
    pieces = []
    for grad_pre, normed in zip(grads_in, normed_in):
        pieces.append(jnp.sum(grad_pre, axis=(0, 1, 2)))
        pieces.append(jnp.sum(grad_pre * normed, axis=(0, 1, 2)))
    totals = lax.psum(jnp.concatenate(pieces), "dp")
    return split_pairs(totals, [piece.shape[0] for piece in pieces])


def normalize(entry, sum_pair, count_now):
    mean_val = sum_pair[0] / count_now
    var_val = sum_pair[1] / count_now - mean_val * mean_val
    inv_std = lax.rsqrt(var_val + EPSILON)
    return ((entry - mean_val) * inv_std, inv_std, mean_val, var_val)


def silu_slope(pre_act):
    sigmoid_val = jax.nn.sigmoid(pre_act)
    return sigmoid_val * (1.0 + pre_act * (1.0 - sigmoid_val))


def norm_backward(grad_pre, normed, inv_std, gain_part, sum_pair, count_now, weight):
    return (
        weight
        * inv_std
        * gain_part
        * (grad_pre - sum_pair[0] / count_now - normed * sum_pair[1] / count_now)
    )


def layer_forward(layer_in, geometry_now, kernels, gain_vec, bias_vec):
    pix_mask, freq_mask, pix_count, spec_count, tables = geometry_now
    fwd_cos, fwd_sin, inv_cos, inv_sin, row_cos, row_sin = tables
    local_kernel, lift_kernel, reduce_kernel, mix_kernel, expand_kernel = kernels
    acts_low = layer_in.astype(jnp.bfloat16)
    padded = with_halo(acts_low, (("dp", 1),), 1)
    padded = jnp.pad(padded, ((0, 0), (0, 0), (1, 1), (0, 0)))
    local_out = conv_rows(padded, local_kernel)
    global_conv = conv_rows(padded[..., :CL], lift_kernel)
    reduced = jnp.einsum(
        "mrwc,cd->mrwd", acts_low[..., CL:], reduce_kernel, preferred_element_type=jnp.float32
    )
    one_stats = moments([reduced], [pix_mask])[0]
    normed_one, inv_one, mean_one, var_one = normalize(reduced, one_stats, pix_count)
    pre_one = normed_one * gain_vec[:CS] + bias_vec[:CS]
    upper_spec = jax.nn.silu(pre_one) * pix_mask
    spectrum = jnp.concatenate(
        [width_forward(upper_spec, fwd_cos), width_forward(upper_spec, fwd_sin)], axis=-1
    ).astype(jnp.bfloat16)
    columns = lax.all_to_all(spectrum, "dp", split_axis=2, concat_axis=1, tiled=True).astype(
        jnp.float32
    )
    spectra = rows_forward(row_cos, row_sin, columns).astype(jnp.bfloat16)
    mixed = jnp.einsum("mkfc,cd->mkfd", spectra, mix_kernel, preferred_element_type=jnp.float32)
    two_stats = moments([mixed], [freq_mask])[0]
    normed_two, inv_two, mean_two, var_two = normalize(mixed, two_stats, spec_count)
    pre_two = normed_two * gain_vec[CS : 3 * CS] + bias_vec[CS : 3 * CS]
    activated = jax.nn.silu(pre_two) * freq_mask
    inverse = rows_inverse(row_cos, row_sin, activated).astype(jnp.bfloat16)
    returned = lax.all_to_all(inverse, "dp", split_axis=1, concat_axis=2, tiled=True).astype(
        jnp.float32
    )
    half_ch = returned.shape[-1] // 2
    restored = width_inverse(returned[..., :half_ch], inv_cos) + width_inverse(
        returned[..., half_ch:], inv_sin
    )
    summed = (upper_spec + restored).astype(jnp.bfloat16)
    spec_out = jnp.einsum(
        "mrwc,cd->mrwd", summed, expand_kernel, preferred_element_type=jnp.float32
    )
    global_out = global_conv + spec_out
    loc_stats, glo_stats = moments([local_out, global_out], [pix_mask, pix_mask])
    normed_loc, inv_loc, mean_loc, var_loc = normalize(local_out, loc_stats, pix_count)
    normed_glo, inv_glo, mean_glo, var_glo = normalize(global_out, glo_stats, pix_count)
    pre_loc = normed_loc * gain_vec[3 * CS : 3 * CS + CL] + bias_vec[3 * CS : 3 * CS + CL]
    pre_glo = normed_glo * gain_vec[3 * CS + CL :] + bias_vec[3 * CS + CL :]
    result = jnp.concatenate([jax.nn.silu(pre_loc), jax.nn.silu(pre_glo)], axis=-1) * pix_mask
    stored = (
        padded,
        pre_one,
        normed_one,
        inv_one,
        spectra,
        pre_two,
        normed_two,
        inv_two,
        summed,
        pre_loc,
        normed_loc,
        inv_loc,
        pre_glo,
        normed_glo,
        inv_glo,
    )
    means_layer = jnp.concatenate([mean_one, mean_two, mean_loc, mean_glo])
    vars_layer = jnp.concatenate([var_one, var_two, var_loc, var_glo])
    return (result, stored, (means_layer, vars_layer))


def layer_backward(grad_result, stored, geometry_now, kernels, gain_vec):
    (
        padded,
        pre_one,
        normed_one,
        inv_one,
        spectra,
        pre_two,
        normed_two,
        inv_two,
        summed,
        pre_loc,
        normed_loc,
        inv_loc,
        pre_glo,
        normed_glo,
        inv_glo,
    ) = stored
    pix_mask, freq_mask, pix_count, spec_count, tables = geometry_now
    fwd_cos, fwd_sin, inv_cos, inv_sin, row_cos, row_sin = tables
    local_kernel, lift_kernel, reduce_kernel, mix_kernel, expand_kernel = kernels
    band_size = pre_one.shape[1]
    width = pre_one.shape[2]
    grad_loc = grad_result[..., :CL] * pix_mask * silu_slope(pre_loc)
    grad_glo = grad_result[..., CL:] * pix_mask * silu_slope(pre_glo)
    loc_pair, glo_pair = grad_moments([grad_loc, grad_glo], [normed_loc, normed_glo])
    d_local = norm_backward(
        grad_loc, normed_loc, inv_loc, gain_vec[3 * CS : 3 * CS + CL], loc_pair, pix_count, pix_mask
    ).astype(jnp.bfloat16)
    d_global = norm_backward(
        grad_glo, normed_glo, inv_glo, gain_vec[3 * CS + CL :], glo_pair, pix_count, pix_mask
    ).astype(jnp.bfloat16)
    grad_expand = jnp.einsum("mrwc,mrwd->cd", summed, d_global, preferred_element_type=jnp.float32)
    d_summed = jnp.einsum(
        "mrwd,cd->mrwc", d_global, expand_kernel, preferred_element_type=jnp.float32
    )
    d_returned = jnp.concatenate(
        [width_inverse_adj(d_summed, inv_cos), width_inverse_adj(d_summed, inv_sin)], axis=-1
    ).astype(jnp.bfloat16)
    d_inverse = lax.all_to_all(d_returned, "dp", split_axis=2, concat_axis=1, tiled=True).astype(
        jnp.float32
    )
    d_activated = rows_forward(row_cos, row_sin, d_inverse)
    grad_two = d_activated * freq_mask * silu_slope(pre_two)
    two_pair = grad_moments([grad_two], [normed_two])[0]
    d_mixed = norm_backward(
        grad_two, normed_two, inv_two, gain_vec[CS : 3 * CS], two_pair, spec_count, freq_mask
    ).astype(jnp.bfloat16)
    grad_mix = jnp.einsum("mkfc,mkfd->cd", spectra, d_mixed, preferred_element_type=jnp.float32)
    d_spectra = jnp.einsum("mkfd,cd->mkfc", d_mixed, mix_kernel, preferred_element_type=jnp.float32)
    d_columns = rows_inverse(row_cos, row_sin, d_spectra).astype(jnp.bfloat16)
    d_spectrum = lax.all_to_all(d_columns, "dp", split_axis=1, concat_axis=2, tiled=True).astype(
        jnp.float32
    )
    half_ch = d_spectrum.shape[-1] // 2
    d_upper = (
        d_summed
        + width_forward_adj(d_spectrum[..., :half_ch], fwd_cos)
        + width_forward_adj(d_spectrum[..., half_ch:], fwd_sin)
    )
    grad_one = d_upper * pix_mask * silu_slope(pre_one)
    one_pair = grad_moments([grad_one], [normed_one])[0]
    d_reduced = norm_backward(
        grad_one, normed_one, inv_one, gain_vec[:CS], one_pair, pix_count, pix_mask
    ).astype(jnp.bfloat16)
    acts_low = padded[:, 1:-1, 1:-1, :]
    grad_reduce = jnp.einsum(
        "mrwc,mrwd->cd", acts_low[..., CL:], d_reduced, preferred_element_type=jnp.float32
    )
    d_global_in = jnp.einsum(
        "mrwd,cd->mrwc", d_reduced, reduce_kernel, preferred_element_type=jnp.float32
    )
    grad_outs = jnp.concatenate([d_local, d_global], axis=-1)
    grad_pad = with_halo(grad_outs, (("dp", 1),), 1)
    grad_pad = jnp.pad(grad_pad, ((0, 0), (0, 0), (1, 1), (0, 0)))
    d_acts = conv_rows(grad_pad[..., :CL], flipped(local_kernel))
    d_lift = conv_rows(grad_pad[..., CL:], flipped(lift_kernel))
    d_input = d_acts + jnp.concatenate([d_lift, d_global_in], axis=-1)
    grad_local_kernel = kernel_grad(padded, d_local, band_size, width)
    grad_lift = kernel_grad(padded[..., :CL], d_global, band_size, width)
    gains_grad = jnp.concatenate([one_pair[1], two_pair[1], loc_pair[1], glo_pair[1]])
    biases_grad = jnp.concatenate([one_pair[0], two_pair[0], loc_pair[0], glo_pair[0]])
    return (
        d_input,
        (grad_local_kernel, grad_lift, grad_reduce, grad_mix, grad_expand),
        (gains_grad, biases_grad),
    )


def block_forward(block_in, geometry_now, kernels, gain_all, bias_all):
    base = block_in.astype(jnp.float32) * geometry_now[0]
    first_out, first_stored, first_stats = layer_forward(
        base, geometry_now, kernels[0], gain_all[0], bias_all[0]
    )
    second_out, second_stored, second_stats = layer_forward(
        first_out, geometry_now, kernels[1], gain_all[1], bias_all[1]
    )
    return (
        (second_out + base).astype(jnp.bfloat16),
        (first_stored, second_stored),
        (first_stats, second_stats),
    )


def block_backward(grad_in, stored, geometry_now, kernels, gain_all):
    pix_mask = geometry_now[0]
    grad_masked = grad_in * pix_mask
    d_first, second_kernels, second_norms = layer_backward(
        grad_masked, stored[1], geometry_now, kernels[1], gain_all[1]
    )
    d_base, first_kernels, first_norms = layer_backward(
        d_first, stored[0], geometry_now, kernels[0], gain_all[0]
    )
    return (
        (grad_masked + d_base) * pix_mask,
        (first_kernels, second_kernels),
        (first_norms, second_norms),
    )


def running_update(mean_now, var_now, layer_stats, geometry_now):
    pix_count = geometry_now[2]
    spec_count = geometry_now[3]
    counts = jnp.concatenate(
        [
            jnp.full((CS,), pix_count, jnp.float32),
            jnp.full((2 * CS,), spec_count, jnp.float32),
            jnp.full((CL + CG,), pix_count, jnp.float32),
        ]
    )
    batch_means = jnp.stack([layer_stats[0][0], layer_stats[1][0]])
    batch_vars = jnp.stack([layer_stats[0][1], layer_stats[1][1]])
    new_mean = (1.0 - MOMENTUM) * mean_now + MOMENTUM * batch_means
    new_var = (1.0 - MOMENTUM) * var_now + MOMENTUM * batch_vars * counts / (counts - 1.0)
    return (new_mean, new_var)


def on_device(
    inputs,
    cotangent,
    shapes,
    local_to_local,
    global_to_local,
    local_to_global,
    spec_reduce,
    spec_mix,
    spec_expand,
    norm_gains,
    norm_biases,
    run_means,
    run_vars,
):
    section_id = lax.axis_index("section")
    band_index = lax.axis_index("dp")
    n_dp = lax.axis_size("dp")
    micro_count = inputs.shape[0]
    map_count = inputs.shape[1]
    band_size = inputs.shape[2]
    freq_total = (LONG // 2 + n_dp) // n_dp * n_dp
    freq_local = freq_total // n_dp
    kernels = []
    for layer_pos in range(2):
        local_kernel = jnp.concatenate(
            [local_to_local[0, layer_pos], global_to_local[0, layer_pos]], axis=1
        )
        kernels.append(
            (
                local_kernel,
                local_to_global[0, layer_pos],
                spec_reduce[0, layer_pos],
                spec_mix[0, layer_pos],
                spec_expand[0, layer_pos],
            )
        )
    gain_all = norm_gains[0]
    bias_all = norm_biases[0]
    received = jnp.zeros(inputs.shape[1:], jnp.bfloat16)
    run_mean = run_means[0]
    run_var = run_vars[0]
    outputs = jnp.zeros(inputs.shape, jnp.bfloat16)
    saved_inputs = []
    saved_geometry = []
    for tick_pos in range(micro_count + 1):
        micro_index = tick_pos - section_id
        is_valid = (micro_index >= 0) & (micro_index < micro_count)
        micro_slot = jnp.clip(micro_index, 0, micro_count - 1)
        own_input = lax.dynamic_index_in_dim(inputs, micro_slot, 0, keepdims=False)
        block_in = jnp.where(section_id == 0, own_input, received)
        shape_row = lax.dynamic_index_in_dim(shapes, micro_slot, 0, keepdims=False)
        geometry_now = geometry(shape_row, band_index, band_size, freq_total, freq_local, map_count)
        block_out, stored, layer_stats = block_forward(
            block_in, geometry_now, kernels, gain_all, bias_all
        )
        new_mean, new_var = running_update(run_mean, run_var, layer_stats, geometry_now)
        run_mean = jnp.where(is_valid, new_mean, run_mean)
        run_var = jnp.where(is_valid, new_var, run_var)
        updated = lax.dynamic_update_index_in_dim(outputs, block_out, micro_slot, 0)
        outputs = jnp.where(is_valid, updated, outputs)
        saved_inputs.append(block_in)
        saved_geometry.append(geometry_now)
        if tick_pos < micro_count:
            received = from_behind(block_out, "section", 1)
    kernel_acc = [jnp.zeros((2,) + part_now.shape, jnp.float32) for part_now in kernels[0]]
    gain_acc = jnp.zeros(gain_all.shape, jnp.float32)
    bias_acc = jnp.zeros(bias_all.shape, jnp.float32)
    received_grad = jnp.zeros(inputs.shape[1:], jnp.bfloat16)
    grads_out = jnp.zeros(inputs.shape, jnp.float32)
    for tick_pos in range(micro_count + 1):
        micro_index = micro_count - tick_pos - section_id
        is_valid = (micro_index >= 0) & (micro_index < micro_count)
        micro_slot = jnp.clip(micro_index, 0, micro_count - 1)
        scale_valid = is_valid.astype(jnp.float32)
        forward_tick = micro_count - tick_pos
        geometry_now = saved_geometry[forward_tick]
        recomputed = block_forward(
            saved_inputs[forward_tick], geometry_now, kernels, gain_all, bias_all
        )
        stored = recomputed[1]
        own_grad = lax.dynamic_index_in_dim(cotangent, micro_slot, 0, keepdims=False)
        grad_in = jnp.where(section_id == 1, own_grad, received_grad).astype(jnp.float32)
        grad_input, kernel_grads, norm_grads = block_backward(
            grad_in, stored, geometry_now, kernels, gain_all
        )
        sent_grad = grad_input.astype(jnp.bfloat16)
        kept_grad = jnp.where(section_id == 1, sent_grad.astype(jnp.float32), grad_input)
        updated = lax.dynamic_update_index_in_dim(grads_out, kept_grad, micro_slot, 0)
        grads_out = jnp.where(is_valid, updated, grads_out)
        stacked = [
            jnp.stack([kernel_grads[0][part_pos], kernel_grads[1][part_pos]]) * scale_valid
            for part_pos in range(5)
        ]
        gain_acc = gain_acc + jnp.stack([norm_grads[0][0], norm_grads[1][0]]) * scale_valid
        bias_acc = bias_acc + jnp.stack([norm_grads[0][1], norm_grads[1][1]]) * scale_valid
        kernel_acc = [acc_part + new_part for acc_part, new_part in zip(kernel_acc, stacked)]
        if tick_pos < micro_count:
            received_grad = from_behind(sent_grad, "section", -1)
    totals = lax.psum(
        (kernel_acc[0], kernel_acc[1], kernel_acc[2], kernel_acc[3], kernel_acc[4]), "dp"
    )
    grad_ll = totals[0][:, :, :CL, :]
    grad_gl = totals[0][:, :, CL:, :]
    return (
        outputs[None],
        grads_out[None],
        grad_ll[None],
        grad_gl[None],
        totals[1][None],
        totals[2][None],
        totals[3][None],
        totals[4][None],
        gain_acc[None],
        bias_acc[None],
        run_mean[None],
        run_var[None],
    )


F32 = jnp.float32
BF16 = jnp.bfloat16
MESH = pl.DeviceIdType.MESH
MEMBERS = 16
ROWS = 8
LAYERS = 4
PAIRS = 4
HALF = 192
FULL = 384
SLOTS = 640
PIECES = 32
EARLY = 272
LATE = 64
AT_LL = 0
AT_GL = 1152
AT_KG = 4608
AT_E = 8064
AT_M = 0
AT_R = 1152
SECTION_NAMES = ("one", "two", "out")


def dot(a, b):
    return lax.dot_general(a, b, (((1,), (0,)), ((), ())), preferred_element_type=F32)


def dot_nt(a, b):
    return lax.dot_general(a, b, (((1,), (1,)), ((), ())), preferred_element_type=F32)


def dot_tn(a, b):
    return lax.dot_general(a, b, (((0,), (0,)), ((), ())), preferred_element_type=F32)


def sigmoid(v):
    return 0.5 * jnp.tanh(0.5 * v) + 0.5


def fold(v):
    return jnp.sum(v.reshape(v.shape[0] // 8, 8, v.shape[1]), axis=0)


def wide(row, lanes):
    whole, rest = divmod(lanes, 128)
    parts = [row] * whole + ([row[:, :rest]] if rest else [])
    return jnp.concatenate(parts, axis=1)


def network_kernel(
    inputs, cot, shapes, ll, gl, lg, red, mix, exp, gains, biases, run_m, run_v,
    out_y, out_g, out_we, out_wl, out_gains, out_biases, out_m, out_v,
    w_c, w_gl, w_r, w_m, w_e, raw_g, raw_b, pars, acts, shifted, halo, v1, u, spec, mixed, tsum, v34,
    pmask, qmask, tf, tft, tg, tgt, hf, hi, vab, e2, dq, ds, g, gblk, at,
    gwe, gwl, rbe, rbl, fine, finl,
    ssum, rsum, send, recv, stats, stats_far,
    sem_w, sem_in, sem_cot, sem_halo_s, sem_halo_r, sem_ar_s, sem_ar_r, sem_aa_s, sem_aa_r,
    sem_y_s, sem_y_r, sem_g_s, sem_g_r, sem_rs, sem_rr, sem_st,
):
    s = lax.axis_index("section")
    d = lax.axis_index("dp")
    n_dp = lax.axis_size("dp")
    per = n_dp // 2
    grp = lax.div(d, per)

    def differ(a, b):
        return a + b - 2 * a * b

    def mirrored(chip):
        return (3 - lax.div(chip, 4)) * 4 + lax.rem(chip, 4)

    half = differ(s, grp)
    me = jnp.where(s == 0, d, mirrored(d))
    first = (me == 0).astype(F32)
    at_z = lax.div(d, 4)
    outer = (at_z == 0) | (at_z == 3)

    def member(group, k):
        core = differ(lax.div(k, per), group)
        return (core, jnp.where(core == 0, k, mirrored(k)))

    def peer(i):
        flips = MEMBERS - 1 - i
        chip = lax.rem(d, per)
        other = grp * per
        for bit in (1, 2, 4):
            other = other + bit * differ(lax.rem(lax.div(chip, bit), 2), lax.rem(lax.div(flips, 2 * bit), 2))
        core = differ(s, lax.rem(flips, 2))
        return jnp.where(core == 0, other, mirrored(other)), (core, other)

    barrier = pltpu.get_barrier_semaphore()
    total = 2 * n_dp
    flat = s * n_dp + d

    def greet(i, c):
        other = lax.rem(flat + 1 + i, total)
        pl.semaphore_signal(
            barrier, inc=1, device_id=(lax.div(other, n_dp), lax.rem(other, n_dp)), device_id_type=MESH
        )
        return c

    lax.fori_loop(0, total - 1, greet, 0)

    own = pl.ds(2 * s, 2)
    places = [
        (red, w_r.at[own]),
        (gains, raw_g.at[s]),
        (biases, raw_b.at[s]),
        (ll, w_c.at[own, :, :, 0:CL]),
        (lg, w_c.at[own, :, :, CL:]),
        (gl, w_gl.at[own]),
        (mix, w_m.at[own]),
        (exp, w_e.at[own]),
    ]
    local_w = [pltpu.make_async_copy(a, b, sem_w.at[0, i]) for i, (a, b) in enumerate(places)]
    for c in local_w:
        c.start()

    pl.semaphore_wait(barrier, total - 1)

    across = (s, mirrored(d))
    stays = s == 0

    def across_copy(source, target, sems):
        return pltpu.make_async_remote_copy(
            source, target, sems.at[0], sems.at[1], device_id=across, device_id_type=MESH
        )

    def when_far(do):
        pl.when(jnp.logical_not(stays))(do)

    input_near = lambda: pltpu.make_async_copy(inputs.at[half], acts.at[0], sem_in.at[0, 0])

    def input_far(part):
        lanes = pl.ds(CL, CG) if part == 0 else pl.ds(0, CL)
        return across_copy(inputs.at[half, :, :, lanes], acts.at[0, :, :, lanes], sem_in.at[part])

    cot_near = lambda: pltpu.make_async_copy(cot.at[half], gblk.at[1], sem_cot.at[0, 0])

    def cot_far(row):
        return across_copy(cot.at[half, row], gblk.at[1, row], sem_cot.at[row])

    def push_rows(parity, window, do):
        if window % 2:
            row = 4 * parity + window - 1

            @pl.when(jnp.logical_not(outer))
            def _():
                do(row)
                do(row + 1)
        else:
            index = 3 * parity + window // 2
            row = jnp.where(index < 4, index, 2 * index - 4)

            @pl.when(outer)
            def _():
                do(row)
                pl.when(index >= 4)(lambda: do(row + 1))

    pl.when(stays)(lambda: input_near().start())
    when_far(lambda: input_far(0).start())
    when_far(lambda: input_far(1).start())
    partner = (1 - s, d)
    remote_w = [
        pltpu.make_async_remote_copy(
            a, b, sem_w.at[1, i], sem_w.at[2, i], device_id=partner, device_id_type=MESH
        )
        for i, (a, b) in enumerate(places)
    ]
    for c in remote_w:
        c.start()

    height = shapes[grp, 0]
    width = shapes[grp, 1]
    col = lax.broadcasted_iota(jnp.int32, (128, 128), 0)
    for q in range(PAIRS):
        for h in range(2):
            row_ok = (ROWS * me + 2 * q + h < height).astype(F32)
            pmask[q, h * 128 : (h + 1) * 128, :] = (col < width).astype(F32) * row_ok
    for f in range(4):
        f_ok = (4 * me + f <= lax.div(width, 2)).astype(F32)
        qmask[f * 128 : (f + 1) * 128, :] = (col < height).astype(F32) * f_ok
    qmask[512:640, :] = (col < height).astype(F32) * (64 <= lax.div(width, 2)).astype(F32) * first

    def inverse(count, less=0):
        return 1.0 / jnp.full((1, 128), (count - less).astype(F32))

    inv_n = inverse(height * width)
    inv_ns = inverse(height * (lax.div(width, 2) + 1))

    row_a = lax.broadcasted_iota(jnp.int32, (128, 512), 0)
    col_a = lax.broadcasted_iota(jnp.int32, (128, 512), 1)
    r_of = (col_a >> 5) * 8 + ((col_a & 31) >> 3) * 2 + (col_a & 1)
    sel_r = (row_a == r_of).astype(F32).astype(BF16)
    f_of = (col_a >> 1) & 3
    row_b = lax.broadcasted_iota(jnp.int32, (512, 128), 0)
    col_b = lax.broadcasted_iota(jnp.int32, (512, 128), 1)
    r_ob = (row_b >> 5) * 8 + ((row_b & 31) >> 3) * 2 + (row_b & 1)
    sel_rt = (col_b == r_ob).astype(F32).astype(BF16)
    f_ob = (row_b >> 1) & 3
    position = lax.broadcasted_iota(jnp.int32, (128, 128), 0)
    other_axis = lax.broadcasted_iota(jnp.int32, (128, 128), 1)

    def wave(index, side, limit, turn):
        side_real = jnp.full((128, 128), side.astype(F32))
        product = (index * other_axis).astype(F32)
        phase = product - side_real * jnp.floor((product + 0.5) / side_real)
        value = jnp.cos(phase * (2.0 * jnp.pi / side_real) + turn) * lax.rsqrt(side_real)
        return jnp.where((index < limit) & (other_axis < side), value, 0.0)

    half_turn = 0.5 * jnp.pi
    for part in range(2):
        base = wave(position, height, height, -half_turn * part).astype(BF16)
        spread = dot(base, sel_r)
        spread_t = dot(sel_rt, base)
        for f in range(4):
            hf[f, part * 128 : (part + 1) * 128, :] = jnp.where(f_of == f, spread, 0.0).astype(BF16)
            at_col = part * 512 + f * 128
            hi[:, at_col : at_col + 128] = jnp.where(f_ob == f, spread_t, 0.0).astype(BF16)
    row_c = lax.broadcasted_iota(jnp.int32, (128, 128), 0)
    sel_f = ((row_c >> 1) == lax.broadcasted_iota(jnp.int32, (128, 128), 1)).astype(F32).astype(BF16)
    half_width = lax.div(width, 2)
    lifted = jnp.where(position == 0, 64, position)
    waves = (
        wave(position, width, half_width + 1, 0.0),
        wave(lifted, width, half_width + 1, jnp.where(position == 0, 0.0, half_turn)),
    )
    weight = jnp.where((position == 0) | (position == half_width), 1.0, 2.0)
    for which, (plain, flipped_table) in enumerate(((tf, tft), (tg, tgt))):
        for part in range(2):
            spread = dot(sel_f, (waves[part] * weight if which else waves[part]).astype(BF16))
            spread_t = jnp.transpose(spread)
            for h in range(2):
                rows = slice(part * 128, (part + 1) * 128)
                cols = slice(h * 128, (h + 1) * 128)
                plain[rows, cols] = jnp.where((row_c & 1) == h, spread, 0.0).astype(BF16)
                flipped_table[cols, rows] = jnp.where(
                    (lax.broadcasted_iota(jnp.int32, (128, 128), 1) & 1) == h, spread_t, 0.0
                ).astype(BF16)
    stats[...] = jnp.zeros_like(stats)
    ssum[...] = jnp.zeros_like(ssum)
    shifted[0] = jnp.zeros((128, 1536), BF16)
    shifted[9] = jnp.zeros((128, 1536), BF16)
    gwe[...] = jnp.zeros_like(gwe)
    gwl[...] = jnp.zeros_like(gwl)

    def sums_start(slot):
        rsum[slot, me] = ssum[slot]

        def go(i, c):
            k, device = peer(i)
            pltpu.make_async_remote_copy(
                ssum.at[slot], rsum.at[slot, me], sem_ar_s.at[slot, k], sem_ar_r.at[slot, me],
                device_id=device, device_id_type=MESH,
            ).start()
            return c

        lax.fori_loop(0, MEMBERS - 1, go, 0)

    def sums_wait(slot, lanes):
        def go(i, c):
            k, device = peer(i)
            pltpu.make_async_remote_copy(
                ssum.at[slot], rsum.at[slot, k], sem_ar_s.at[slot, k], sem_ar_r.at[slot, k],
                device_id=device, device_id_type=MESH,
            ).wait()
            return c

        lax.fori_loop(0, MEMBERS - 1, go, 0)
        tot = jnp.sum(rsum[slot], axis=0)
        tiles = (lanes + 127) // 128
        one = jnp.concatenate([tot[i : i + 1] for i in range(tiles)], axis=1)[:, :lanes]
        two = jnp.concatenate([tot[4 + i : 5 + i] for i in range(tiles)], axis=1)[:, :lanes]
        return one, two

    def put_sums(slot, one, two):
        lanes = one.shape[1]
        for base_row, part in ((0, one), (4, two)):
            flat_part = jnp.sum(part, axis=0, keepdims=True)
            for i in range((lanes + 127) // 128):
                w = min(128, lanes - i * 128)
                ssum[slot, base_row + i : base_row + i + 1, 0:w] = flat_part[:, i * 128 : i * 128 + w]

    def swap_start(slot):
        recv[slot, me] = send[slot, me]

        def go(i, c):
            k, device = peer(i)
            pltpu.make_async_remote_copy(
                send.at[slot, k], recv.at[slot, me], sem_aa_s.at[slot, k], sem_aa_r.at[slot, me],
                device_id=device, device_id_type=MESH,
            ).start()
            return c

        lax.fori_loop(0, MEMBERS - 1, go, 0)

    def swap_wait(slot):
        def go(i, c):
            k, device = peer(i)
            pltpu.make_async_remote_copy(
                send.at[slot, k], recv.at[slot, k], sem_aa_s.at[slot, k], sem_aa_r.at[slot, k],
                device_id=device, device_id_type=MESH,
            ).wait()
            return c

        lax.fori_loop(0, MEMBERS - 1, go, 0)

    def halo_copies():
        up = lambda: pltpu.make_async_remote_copy(
            shifted.at[1, :, 512:1024], halo.at[1], sem_halo_s.at[0], sem_halo_r.at[1],
            device_id=member(grp, lax.rem(me + MEMBERS - 1, MEMBERS)), device_id_type=MESH,
        )
        down = lambda: pltpu.make_async_remote_copy(
            shifted.at[8, :, 512:1024], halo.at[0], sem_halo_s.at[1], sem_halo_r.at[0],
            device_id=member(grp, lax.rem(me + 1, MEMBERS)), device_id_type=MESH,
        )
        return up, down

    has_up = me > 0
    has_down = me < MEMBERS - 1

    def halo_start():
        up, down = halo_copies()

        @pl.when(has_up)
        def _():
            up().start()

        @pl.when(has_down)
        def _():
            down().start()

    def put_sides(index, x, flip):
        at_col = lax.broadcasted_iota(jnp.int32, (128, 512), 0)
        before = jnp.where(at_col == 0, 0.0, pltpu.roll(x, 1, 0)).astype(BF16)
        after = jnp.where(at_col == 127, 0.0, pltpu.roll(x, 127, 0)).astype(BF16)
        shifted[index, :, 0:512] = after if flip else before
        shifted[index, :, 1024:1536] = before if flip else after

    def put_shifted(index, row, flip):
        shifted[index, :, 512:1024] = row
        put_sides(index, row.astype(F32), flip)

    def halo_wait(flip):
        up, down = halo_copies()

        @pl.when(has_up)
        def _():
            up().wait_send()
            down().wait_recv()
            put_shifted(0, halo[0], flip)

        @pl.when(has_down)
        def _():
            down().wait_send()
            up().wait_recv()
            put_shifted(9, halo[1], flip)

    lane = lax.broadcasted_iota(jnp.int32, (128, FULL), 1)
    low = lane < HALF

    def width_out(slot, h, table, get):
        parts = []
        for q in (2 * h, 2 * h + 1):
            x = dot(table[...], get(q))
            both = jnp.concatenate([x[:128], x[128:]], axis=1)
            parts.append(both.reshape(MEMBERS, 8, FULL))
        send[slot, :, pl.ds(pl.multiple_of(16 * h, 16), 16), :] = jnp.concatenate(parts, axis=1).astype(BF16)

    def width_back(slot, h, table):
        block = recv[slot, :, pl.ds(pl.multiple_of(16 * h, 16), 16), :].astype(F32)
        results = []
        for o in range(2):
            z = block[:, 8 * o : 8 * o + 8, :].reshape(128, FULL)
            zi = pltpu.roll(z, HALF, 1)
            stacked = jnp.concatenate([z[:, :HALF], zi[:, :HALF]], axis=0).astype(BF16)
            results.append(dot(table[...], stacked))
        return results

    def rows_forward_into(slot, put):
        x = recv[slot].reshape(512, FULL)
        for f in range(4):
            both = dot(hf[f], x)
            a, b = both[:128], both[128:]
            turned = pltpu.roll(b, HALF, 1)
            if f == 0:
                rest = 1.0 - first
                put(0, jnp.where(low, a + rest * turned, rest * a - turned))
                put(4, jnp.where(low, pltpu.roll(a, HALF, 1), -b) * first)
            else:
                put(f, jnp.where(low, a + turned, a - turned))

    def rows_inverse_from(slot, get):
        last = get(4)
        for f in range(4):
            v = get(f)
            turned = pltpu.roll(v, HALF, 1)
            if f == 0:
                rest = 1.0 - first
                a = jnp.where(low, v, rest * v + first * pltpu.roll(last, HALF, 1))
                b = jnp.where(low, -turned, rest * turned - first * last)
            else:
                a = v
                b = jnp.where(low, -turned, turned)
            vab[f * 128 : (f + 1) * 128, :] = a.astype(BF16)
            vab[512 + f * 128 : 640 + f * 128, :] = b.astype(BF16)

        def go(c, carry):
            z = dot(hi[pl.ds(pl.multiple_of(c * 256, 256), 256), :], vab[...])
            send[slot, pl.ds(c * 8, 8)] = z.astype(BF16).reshape(8, 32, FULL)
            return carry

        lax.fori_loop(0, 2, go, 0)

    def moments(layer, which, lanes, one, two, inv_count):
        count = wide(inv_count, lanes)
        mean = one * count
        var = two * count - mean * mean
        inv = lax.rsqrt(var + EPSILON)
        stats[layer, which : which + 1, 0:lanes] = mean
        stats[layer, 3 + which : 4 + which, 0:lanes] = inv
        stats[layer, 6 + which : 7 + which, 0:lanes] = var
        scale = pars[layer, which : which + 1, 0:lanes] * inv
        shift = pars[layer, 3 + which : 4 + which, 0:lanes] - mean * scale
        return scale, shift

    def affine(layer, which, lanes):
        mean = stats[layer, which : which + 1, 0:lanes]
        inv = stats[layer, 3 + which : 4 + which, 0:lanes]
        gain = pars[layer, which : which + 1, 0:lanes]
        return mean, inv, gain, pars[layer, 3 + which : 4 + which, 0:lanes]

    def keep_grad_sums(layer, which, lanes, one, two):
        stats[layer, 9 + which : 10 + which, 0:lanes] = one
        stats[layer, 12 + which : 13 + which, 0:lanes] = two

    zero_of = lambda lanes: jnp.zeros((8, lanes), F32)

    def conv_pair(layer, c):
        loc = jnp.zeros((256, 512), F32)
        glo = jnp.zeros((256, 128), F32)
        for i in range(3):
            a_loc = jnp.concatenate(
                [shifted[pl.ds(2 * c + i, 2), :, j * 512 : j * 512 + 128].reshape(256, 128) for j in range(3)], axis=1
            )
            a_glo = jnp.concatenate(
                [shifted[pl.ds(2 * c + i, 2), :, j * 512 + 128 : (j + 1) * 512].reshape(256, 384) for j in range(3)],
                axis=1,
            )
            loc = loc + dot(a_loc, w_c[layer, 3 * i : 3 * i + 3].reshape(384, 512))
            glo = glo + dot(a_glo, w_gl[layer, 3 * i : 3 * i + 3].reshape(1152, 128))
        v34[layer, c, :, 0:CL] = loc[:, :CL] + glo
        v34[layer, c, :, CL:] = loc[:, CL:]

    pl.when(stays)(lambda: input_near().wait())
    when_far(lambda: input_far(0).wait())
    pl.when(stays)(lambda: cot_near().start())

    def pixel_rows(r):
        return lax.div(r, 2), pl.ds(pl.multiple_of(lax.rem(r, 2) * 128, 128), 128)

    def mask_global(r, c):
        q, here = pixel_rows(r)
        x = acts[0, r, :, CL:].astype(F32) * wide(pmask[q, here, :], CG)
        acts[0, r, :, CL:] = x.astype(BF16)
        return c

    lax.fori_loop(0, ROWS, mask_global, 0)
    for c in local_w[:3] + remote_w[:3]:
        c.wait()
    for lay in range(LAYERS):
        for base_row, raw in ((0, raw_g), (3, raw_b)):
            row = raw[lay // 2, lay % 2 : lay % 2 + 1, :]
            pars[lay, base_row : base_row + 1, 0:CS] = row[:, :CS]
            pars[lay, base_row + 1 : base_row + 2, 0:FULL] = row[:, CS : 3 * CS]
            pars[lay, base_row + 2 : base_row + 3, :] = row[:, 3 * CS :]

    def start_row(r, c):
        q, here = pixel_rows(r)
        acts[0, r, :, 0:CL] = (acts[0, r, :, 0:CL].astype(F32) * pmask[q, here, :]).astype(BF16)
        return c

    def finish_start():
        when_far(lambda: input_far(1).wait())
        lax.fori_loop(0, ROWS, start_row, 0)
        for c in local_w[3:] + remote_w[3:]:
            c.wait()

    def out_copies(source, target, sems, block, row):
        send_sem, arrive_sem = sems
        far = lambda: pltpu.make_async_remote_copy(
            source.at[row], target.at[grp, row], send_sem.at[block, row], arrive_sem.at[grp, row],
            device_id=(block, me), device_id_type=MESH,
        )
        near = lambda: pltpu.make_async_copy(source.at[row], target.at[grp, row], send_sem.at[block, row])
        return (block == s) & (me == d), far, near

    def y_copies(block, row):
        return out_copies(acts.at[2 * block + 2], out_y, (sem_y_s, sem_y_r), block, row)

    def g_copies(block, row):
        return out_copies(gblk.at[1 - block], out_g, (sem_g_s, sem_g_r), block, row)

    def start_out(made):
        here, far, near = made
        pl.when(here)(lambda: near().start())
        pl.when(jnp.logical_not(here))(lambda: far().start())

    def wait_out(made):
        here, far, near = made
        pl.when(here)(lambda: near().wait())
        pl.when(jnp.logical_not(here))(lambda: far().wait_send())

    def forward_window(layer, window):
        parity = lax.rem(layer, 2)

        @pl.when(layer < 2)
        def _():
            push_rows(parity, window, lambda row: when_far(lambda: cot_far(row).start()))

        @pl.when(layer >= 2)
        def _():
            push_rows(parity, window, lambda row: start_out(y_copies(0, row)))

    def backward_window(step, window):
        parity = lax.rem(step, 2)

        @pl.when(step < 2)
        def _():
            push_rows(parity, window, lambda row: start_out(y_copies(1, row)))

        @pl.when(step >= 2)
        def _():
            push_rows(parity, window, lambda row: start_out(g_copies(1, row)))

    def forward(layer, carry):
        def reduce_pair(q, sums):
            a = acts[layer, pl.ds(2 * q, 2), :, CL:].reshape(256, CG)
            v = dot_nt(a, w_r[layer])
            v1[layer, q] = v
            return sums[0] + fold(v), sums[1] + fold(v * v)

        put_sums(0, *lax.fori_loop(0, PAIRS, reduce_pair, (zero_of(HALF), zero_of(HALF))))
        sums_start(0)
        pl.when(layer == 0)(finish_start)

        def lay_out(r, carry):
            put_shifted(1 + r, acts[layer, r], False)
            return carry

        lax.fori_loop(0, ROWS, lay_out, 0)
        halo_start()
        forward_window(layer, 0)

        def conv_go(c, carry):
            conv_pair(layer, c)
            return carry

        lax.fori_loop(1, 3, conv_go, 0)
        scale, shift = moments(layer, 0, HALF, *sums_wait(0, HALF), inv_n)

        def spectral_in(h, carry):
            def get(q):
                pre = v1[layer, q] * scale + shift
                x = pre * sigmoid(pre) * wide(pmask[q], HALF)
                u[q] = x
                return x.astype(BF16)

            width_out(0, h, tf, get)
            return carry

        lax.fori_loop(0, 2, spectral_in, 0)
        swap_start(0)
        halo_wait(False)
        conv_pair(layer, 0)
        forward_window(layer, 1)
        swap_wait(0)

        def put(f, y):
            spec[layer, f * 128 : (f + 1) * 128, :] = y.astype(BF16)

        rows_forward_into(0, put)

        def mix_block(f, sums):
            at_row = pl.ds(pl.multiple_of(f * 128, 128), 128)
            v = dot(spec[layer, at_row, :], w_m[layer])
            mixed[layer, at_row, :] = v
            return sums[0] + fold(v), sums[1] + fold(v * v)

        put_sums(1, *lax.fori_loop(0, 5, mix_block, (zero_of(FULL), zero_of(FULL))))
        sums_start(1)
        forward_window(layer, 2)
        scale2, shift2 = moments(layer, 1, FULL, *sums_wait(1, FULL), inv_ns)

        def get_v(f):
            rows = slice(f * 128, (f + 1) * 128)
            pre = mixed[layer, rows, :] * scale2 + shift2
            return pre * sigmoid(pre) * wide(qmask[rows, :], FULL)

        rows_inverse_from(1, get_v)
        swap_start(1)
        conv_pair(layer, 3)
        forward_window(layer, 3)
        swap_wait(1)

        def spectral_out(h, sums):
            backs = width_back(1, h, tgt)
            one, two = sums
            for o in range(2):
                q = 2 * h + o
                t = (u[q] + backs[o]).astype(BF16)
                tsum[layer, q] = t
                pm = pmask[q]
                v_loc = v34[layer, q, :, 0:CL] * pm
                v_glo = (v34[layer, q, :, CL:] + dot(t, w_e[layer])) * wide(pm, CG)
                v34[layer, q, :, 0:CL] = v_loc
                v34[layer, q, :, CL:] = v_glo
                v = jnp.concatenate([v_loc, v_glo], axis=1)
                one = one + fold(v)
                two = two + fold(v * v)
            return one, two

        put_sums(2, *lax.fori_loop(0, 2, spectral_out, (zero_of(512), zero_of(512))))
        sums_start(2)
        forward_window(layer, 4)
        scale3, shift3 = moments(layer, 2, 512, *sums_wait(2, 512), inv_n)
        odd = lax.rem(layer, 2)
        oddf = odd.astype(F32)

        def next_row(r, carry):
            q = lax.div(r, 2)
            here = pl.ds(pl.multiple_of(lax.rem(r, 2) * 128, 128), 128)
            pre = v34[layer, q, here, :] * scale3 + shift3
            x = pre * sigmoid(pre) * wide(pmask[q, here, :], 512)
            x = x + oddf * acts[layer - odd, r].astype(F32)
            acts[layer + 1, r] = x.astype(BF16)
            return carry

        lax.fori_loop(0, ROWS, next_row, 0)

        return carry

    lax.fori_loop(0, LAYERS, forward, 0)

    pl.when(stays)(lambda: cot_near().wait())

    def cot_wait(row, c):
        when_far(lambda: cot_far(row).wait())
        return c

    lax.fori_loop(0, ROWS, cot_wait, 0)

    def cot_row(r, c):
        q = lax.div(r, 2)
        here = pl.ds(pl.multiple_of(lax.rem(r, 2) * 128, 128), 128)
        x = gblk[1, r].astype(F32) * wide(pmask[q, here, :], 512)
        gblk[1, r] = x.astype(BF16)
        g[q, here, :] = x
        return c

    lax.fori_loop(0, ROWS, cot_row, 0)

    x_bit = lax.rem(d, 2)
    y_bit = lax.rem(lax.div(d, 2), 2)
    at_x = jnp.where(s == 0, x_bit, y_bit)
    at_y = jnp.where(s == 0, y_bit, x_bit)
    step_x = jnp.where(s == 0, 1, 2)
    step_y = 3 - step_x
    in_core = s * 16
    in_x = in_core + at_x * 8
    in_y = in_x + at_y * 4
    near_x = (s, d + step_x * (1 - 2 * at_x))
    near_y = (s, d + step_y * (1 - 2 * at_y))

    def sum_part(p, layer):
        gw, rb, fin, out, rows = ((gwe, rbe, fine, out_we, EARLY), (gwl, rbl, finl, out_wl, LATE))[p]
        block = lax.div(layer, 2)
        odd = lax.rem(layer, 2)
        slot = jnp.where(block == s, 2, 0) + odd

        def remote(stage, source, target, other, n=0):
            return pltpu.make_async_remote_copy(
                source, target, sem_rs.at[p, odd, stage, n], sem_rr.at[p, odd, stage, n], device_id=other, device_id_type=MESH
            )

        def rows_of(first_piece, pieces):
            return pl.ds(pl.multiple_of(first_piece * rows, rows), pieces * rows)

        one = lambda: remote(0, gw.at[rows_of((1 - s) * 16, 16)], rb.at[rows_of(0, 16)], partner)
        far_x = in_core + (1 - at_x) * 8

        def two(n):
            first_four = (1 - at_y) * 4 if n == 0 else at_y * 4
            return remote(1, gw.at[rows_of(far_x + first_four, 4)], rb.at[rows_of(16 + first_four, 4)], near_x, n)

        three = lambda: remote(2, gw.at[rows_of(in_x + (1 - at_y) * 4, 4)], rb.at[rows_of(24, 4)], near_y)

        def add(first_piece, from_piece, pieces):
            def go(i, carry):
                here = rows_of(first_piece + i, 1)
                there = rows_of(from_piece + i, 1)
                gw[here, :] = (gw[here, :].astype(F32) + rb[there, :].astype(F32)).astype(BF16)
                return carry

            lax.fori_loop(0, pieces, go, 0)

        def along_z(i):
            other = lax.rem(at_z + 1 + i, 4)
            return other, (s, d + 4 * (other - at_z))

        def four(i, arriving):
            other, device = along_z(i)
            return pltpu.make_async_remote_copy(
                gw.at[rows_of(in_y + other, 1)],
                rb.at[rows_of(28 + (other if arriving else at_z), 1)],
                sem_rs.at[p, odd, 3, i], sem_rr.at[p, odd, 3, other if arriving else at_z],
                device_id=device, device_id_type=MESH,
            )

        def five(i, arriving):
            other, device = along_z(i)
            return pltpu.make_async_remote_copy(
                fin, out.at[slot, rows_of(in_y + (other if arriving else at_z), 1)],
                sem_rs.at[p, odd, 4, i], sem_rr.at[p, odd, 4, other if arriving else at_z],
                device_id=device, device_id_type=MESH,
            )

        five_own = lambda: pltpu.make_async_copy(fin, out.at[slot, rows_of(in_y + at_z, 1)], sem_rs.at[p, odd, 4, 3])

        def spread_copy(stage, first_piece, other, n=0):
            here = out.at[slot, rows_of(first_piece, 4)]
            return remote(stage, here, here, other, n)

        six = lambda: spread_copy(5, in_y, near_y)
        seven = lambda n: spread_copy(6, in_y if n == 0 else in_x + (1 - at_y) * 4, near_x, n)
        eight = lambda: remote(
            7, out.at[odd, rows_of(in_core, 16)],
            out.at[2 + odd, rows_of(in_core, 16)], partner,
        )
        starts = s != block

        def begin_one():
            one().start()

        def begin_two():
            one().wait()
            add(in_core, 0, 16)
            two(0).start()

        def begin_three():
            two(0).wait()
            add(in_x + (1 - at_y) * 4, 16 + (1 - at_y) * 4, 4)
            two(1).start()
            three().start()

        def begin_four():
            two(1).wait()
            three().wait()
            add(in_y, 16 + at_y * 4, 4)
            add(in_y, 24, 4)
            for i in range(3):
                four(i, False).start()

        def begin_five():
            total_now = gw[rows_of(in_y + at_z, 1), :].astype(F32)
            for i in range(3):
                four(i, False).wait_send()
                four(i, True).wait_recv()
                total_now = total_now + rb[rows_of(28 + lax.rem(at_z + 1 + i, 4), 1), :].astype(F32)
            fin[...] = total_now.astype(BF16)
            five_own().start()
            for i in range(3):
                five(i, False).start()

        def begin_six():
            five_own().wait()
            for i in range(3):
                five(i, False).wait_send()
                five(i, True).wait_recv()
            six().start()
            seven(0).start()

        def begin_seven():
            six().wait()
            seven(0).wait()
            seven(1).start()

        def begin_eight():
            seven(1).wait()
            pl.when(starts)(lambda: eight().start())

        def end():
            pl.when(starts)(lambda: eight().wait_send())
            pl.when(jnp.logical_not(starts))(lambda: eight().wait_recv())

        return (
            begin_one, begin_two, begin_three, begin_four, begin_five,
            begin_six, begin_seven, begin_eight, end,
        )

    def stage(p, layer, which):
        pl.when(layer < LAYERS)(lambda: sum_part(p, layer)[which]())

    def backward(step, carry):
        layer = LAYERS - 1 - step
        mean3, inv3, gain3, bias3 = affine(layer, 2, 512)
        scale3 = gain3 * inv3
        shift3 = bias3 - mean3 * scale3

        def slope_row(r, sums):
            q = lax.div(r, 2)
            here = pl.ds(pl.multiple_of(lax.rem(r, 2) * 128, 128), 128)
            v = v34[layer, q, here, :]
            pre = v * scale3 + shift3
            sg = sigmoid(pre)
            e = g[q, here, :] * wide(pmask[q, here, :], 512) * (sg * (1.0 + pre * (1.0 - sg)))
            g[q, here, :] = e
            return sums[0] + fold(e), sums[1] + fold(e * ((v - mean3) * inv3))

        put_sums(3, *lax.fori_loop(0, ROWS, slope_row, (zero_of(512), zero_of(512))))
        sums_start(3)
        backward_window(step, 0)

        def turn_row(r, carry):
            at[:, pl.ds(pl.multiple_of(r * 128, 128), 128)] = jnp.transpose(acts[layer, r])
            return carry

        stage(0, layer + 1, 4)
        stage(1, layer + 1, 1)
        stage(1, layer + 2, 6)
        lax.fori_loop(0, ROWS, turn_row, 0)
        one3, two3 = sums_wait(3, 512)
        keep_grad_sums(layer, 2, 512, one3, two3)
        part_a = one3 * wide(inv_n, 512)
        part_b = two3 * wide(inv_n, 512)

        def d_row(r, carry):
            q = lax.div(r, 2)
            here = pl.ds(pl.multiple_of(lax.rem(r, 2) * 128, 128), 128)
            z = (v34[layer, q, here, :] - mean3) * inv3
            dv = wide(pmask[q, here, :], 512) * scale3 * (g[q, here, :] - part_a - z * part_b)
            shifted[1 + r, :, 512:1024] = dv.astype(BF16)
            return carry

        lax.fori_loop(0, ROWS, d_row, 0)
        halo_start()

        def grad_out(h, carry):
            def get(q):
                dg = shifted[pl.ds(1 + 2 * q, 2), :, 512 + CL : 1024].reshape(256, CG)
                dt = dot_nt(dg, w_e[layer])
                u[q] = dt
                return dt.astype(BF16)

            width_out(0, h, tg, get)
            return carry

        lax.fori_loop(0, 2, grad_out, 0)
        swap_start(0)

        def lay_sides(r, carry):
            put_sides(1 + r, shifted[1 + r, :, 512:1024].astype(F32), True)
            return carry

        lax.fori_loop(0, ROWS, lay_sides, 0)
        halo_wait(True)

        def conv_back(c, carry):
            d_loc = jnp.zeros((256, 128), F32)
            d_glo = jnp.zeros((256, 384), F32)
            for i in range(3):
                for j in range(3):
                    rows = pl.ds(2 * c + 2 - i, 2)
                    dd = shifted[rows, :, j * 512 : (j + 1) * 512].reshape(256, 512)
                    d_loc = d_loc + dot_nt(dd, w_c[layer, 3 * i + j])
                    d_glo = d_glo + dot_nt(dd[:, :CL], w_gl[layer, 3 * i + j])
            g[c, :, 0:CL] = d_loc
            g[c, :, CL:] = d_glo
            return carry

        def block_rows(i, lanes):
            return jnp.concatenate(
                [
                    shifted[2 - i : 10 - i, :, j * 512 + lanes[0] : j * 512 + lanes[1]].reshape(1024, lanes[1] - lanes[0])
                    for j in range(3)
                ],
                axis=1,
            )

        def lift_grad(i):
            acc = dot(at[0:CL, :], block_rows(i, (CL, 512)))
            for j in range(3):
                for n in range(3):
                    base = AT_KG + n * 1152 + (3 * i + j) * 128
                    gwe[base : base + 128, :] = acc[:, (3 * j + n) * 128 : (3 * j + n + 1) * 128].astype(BF16)

        def local_grad(i):
            acc = dot(at[...], block_rows(i, (0, CL)))
            for j in range(3):
                tap = 3 * i + j
                block = acc[:, j * 128 : (j + 1) * 128].astype(BF16)
                gwe[AT_LL + tap * CL : AT_LL + (tap + 1) * CL, :] = block[:CL]
                gwe[AT_GL + tap * CG : AT_GL + (tap + 1) * CG, :] = block[CL:]

        conv_back(0, 0)
        stage(0, layer + 1, 5)
        stage(1, layer + 2, 7)
        stage(1, layer + 1, 2)
        backward_window(step, 1)
        for i in range(3):
            local_grad(i)
        swap_wait(0)

        def put(f, y):
            e2[f * 128 : (f + 1) * 128, :] = y

        rows_forward_into(0, put)
        mean2, inv2, gain2, bias2 = affine(layer, 1, FULL)
        scale2 = gain2 * inv2
        shift2 = bias2 - mean2 * scale2

        def slope_block(f, sums):
            rows = pl.ds(pl.multiple_of(f * 128, 128), 128)
            v = mixed[layer, rows, :]
            pre = v * scale2 + shift2
            sg = sigmoid(pre)
            e = e2[rows, :] * wide(qmask[rows, :], FULL) * (sg * (1.0 + pre * (1.0 - sg)))
            e2[rows, :] = e
            return sums[0] + fold(e), sums[1] + fold(e * ((v - mean2) * inv2))

        put_sums(1, *lax.fori_loop(0, 5, slope_block, (zero_of(FULL), zero_of(FULL))))
        sums_start(1)
        backward_window(step, 2)
        stage(0, layer + 1, 6)
        stage(1, layer + 2, 8)
        stage(1, layer + 1, 3)
        for i in range(3):
            lift_grad(i)
        acc_e = jnp.zeros((HALF, CG), F32)
        for q in range(PAIRS):
            dg = shifted[1 + 2 * q : 3 + 2 * q, :, 512 + CL : 1024].reshape(256, CG)
            acc_e = acc_e + dot_tn(tsum[layer, q], dg)
        for n in range(3):
            gwe[AT_E + n * HALF : AT_E + (n + 1) * HALF, :] = acc_e[:, n * 128 : (n + 1) * 128].astype(BF16)
        stage(0, layer, 0)
        one2, two2 = sums_wait(1, FULL)
        stage(0, layer, 1)
        keep_grad_sums(layer, 1, FULL, one2, two2)
        part_a2 = one2 * wide(inv_ns, FULL)
        part_b2 = two2 * wide(inv_ns, FULL)

        def dq_block(f, carry):
            rows = pl.ds(pl.multiple_of(f * 128, 128), 128)
            z = (mixed[layer, rows, :] - mean2) * inv2
            dv = wide(qmask[rows, :], FULL) * scale2 * (e2[rows, :] - part_a2 - z * part_b2)
            low_dv = dv.astype(BF16)
            dq[rows, :] = low_dv
            e2[rows, :] = dot_nt(low_dv, w_m[layer])
            return carry

        lax.fori_loop(0, 5, dq_block, 0)
        rows_inverse_from(1, lambda f: e2[f * 128 : (f + 1) * 128, :])
        swap_start(1)
        conv_back(1, 0)
        stage(0, layer, 2)
        stage(0, layer + 1, 7)
        stage(1, layer + 1, 4)
        backward_window(step, 3)
        conv_back(2, 0)
        swap_wait(1)

        mean1, inv1, gain1, bias1 = affine(layer, 0, HALF)
        scale1 = gain1 * inv1
        shift1 = bias1 - mean1 * scale1

        def slope_in(h, sums):
            backs = width_back(1, h, tft)
            one, two = sums
            for o in range(2):
                q = 2 * h + o
                v = v1[layer, q]
                pre = v * scale1 + shift1
                sg = sigmoid(pre)
                e = (u[q] + backs[o]) * wide(pmask[q], HALF) * (sg * (1.0 + pre * (1.0 - sg)))
                u[q] = e
                one = one + fold(e)
                two = two + fold(e * ((v - mean1) * inv1))
            return one, two

        put_sums(0, *lax.fori_loop(0, 2, slope_in, (zero_of(HALF), zero_of(HALF))))
        sums_start(0)
        backward_window(step, 4)
        stage(0, layer, 3)
        stage(0, layer + 1, 8)
        stage(1, layer + 1, 5)
        conv_back(3, 0)
        acc_m = jnp.zeros((FULL, FULL), F32)
        for f in range(5):
            rows = slice(f * 128, (f + 1) * 128)
            acc_m = acc_m + dot_tn(spec[layer, rows, :], dq[rows, :])
        for n in range(3):
            gwl[AT_M + n * FULL : AT_M + (n + 1) * FULL, :] = acc_m[:, n * 128 : (n + 1) * 128].astype(BF16)
        one1, two1 = sums_wait(0, HALF)
        keep_grad_sums(layer, 0, HALF, one1, two1)
        part_a1 = one1 * wide(inv_n, HALF)
        part_b1 = two1 * wide(inv_n, HALF)

        def ds_pair(q, carry):
            z = (v1[layer, q] - mean1) * inv1
            dv = wide(pmask[q], HALF) * scale1 * (u[q] - part_a1 - z * part_b1)
            low_dv = dv.astype(BF16)
            ds[q] = low_dv
            g[q, :, CL:] = g[q, :, CL:] + dot(low_dv, w_r[layer])
            return carry

        lax.fori_loop(0, PAIRS, ds_pair, 0)
        acc_r = jnp.zeros((HALF, CG), F32)
        for q in range(PAIRS):
            a = acts[layer, 2 * q : 2 * q + 2, :, CL:].reshape(256, CG)
            acc_r = acc_r + dot_tn(ds[q], a)
        for n in range(3):
            gwl[AT_R + n * HALF : AT_R + (n + 1) * HALF, :] = acc_r[:, n * 128 : (n + 1) * 128].astype(BF16)

        stage(1, layer, 0)

        @pl.when(lax.rem(layer, 2) == 0)
        def _():
            block = lax.div(layer, 2)

            def close_row(r, carry):
                q = lax.div(r, 2)
                here = pl.ds(pl.multiple_of(lax.rem(r, 2) * 128, 128), 128)
                x = (gblk[block, r].astype(F32) + g[q, here, :]) * wide(pmask[q, here, :], 512)
                low_x = x.astype(BF16)
                gblk[1 - block, r] = low_x
                g[q, here, :] = low_x.astype(F32)

                return carry

            lax.fori_loop(0, ROWS, close_row, 0)

        return carry

    lax.fori_loop(0, LAYERS, backward, 0)

    far = pltpu.make_async_remote_copy(
        stats.at[own], stats_far, sem_st.at[0], sem_st.at[1],
        device_id=across, device_id_type=MESH,
    )
    far.start()

    def push_last(first_row, rows):
        for row in range(first_row, first_row + rows):
            start_out(g_copies(0, row))

    stage(0, 0, 4)
    stage(1, 1, 6)
    push_last(0, 1)
    stage(1, 0, 1)
    stage(1, 0, 2)
    stage(1, 1, 7)
    stage(1, 0, 3)
    push_last(1, 2)
    stage(0, 0, 5)
    stage(1, 0, 4)
    push_last(3, 5)
    stage(1, 1, 8)
    stage(0, 0, 6)
    stage(1, 0, 5)
    stage(0, 0, 7)
    stage(1, 0, 6)
    stage(1, 0, 7)
    stage(0, 0, 8)
    stage(1, 0, 8)
    for block in range(2):
        def sent(row, carry, block=block):
            wait_out(y_copies(block, row))
            wait_out(g_copies(block, row))
            return carry

        lax.fori_loop(0, ROWS, sent, 0)
    for m in range(2):
        sender = member(m, d)
        from_self = (sender[0] == s) & (sender[1] == d)

        def arrived(row, carry, m=m):
            for source, target, sems in ((acts, out_y, (sem_y_s, sem_y_r)), (gblk, out_g, (sem_g_s, sem_g_r))):
                pltpu.make_async_remote_copy(
                    source.at[0, row], target.at[m, row], sems[0].at[0, row], sems[1].at[m, row],
                    device_id=partner, device_id_type=MESH,
                ).wait_recv()
            return carry

        @pl.when(jnp.logical_not(from_self))
        def _(arrived=arrived):
            lax.fori_loop(0, ROWS, arrived, 0)

    far.wait()
    for lay in range(2):
        mine = stats[2 * s + lay]
        other = stats_far[lay]
        zero_first = jnp.where(grp == 0, mine, other)
        one_next = jnp.where(grp == 0, other, mine)
        row = slice(lay, lay + 1)

        def joined(st, base):
            return jnp.concatenate(
                [st[base : base + 1, :HALF], st[base + 1 : base + 2, :FULL], st[base + 2 : base + 3]], axis=1
            )

        mean = run_m[row, :]
        var = run_v[row, :]
        for m, st in enumerate((zero_first, one_next)):
            pixels = shapes[m, 0] * shapes[m, 1]
            points = shapes[m, 0] * (lax.div(shapes[m, 1], 2) + 1)
            fix = [
                wide(jnp.full((1, 128), count.astype(F32)) * inverse(count, 1), lanes)
                for count, lanes in ((pixels, HALF), (points, FULL), (pixels, 512))
            ]
            mean = (1.0 - MOMENTUM) * mean + MOMENTUM * joined(st, 0)
            var = (1.0 - MOMENTUM) * var + MOMENTUM * joined(st, 6) * jnp.concatenate(fix, axis=1)
        out_m[row, :] = mean
        out_v[row, :] = var
        out_biases[row, :] = joined(zero_first, 9) + joined(one_next, 9)
        out_gains[row, :] = joined(zero_first, 12) + joined(one_next, 12)


def tiles_of(rows, array):
    return jnp.concatenate([array[:, n * rows : (n + 1) * rows].astype(F32) for n in range(3)], axis=-1)


def on_band(
    inputs,
    cotangent,
    shapes,
    local_to_local,
    global_to_local,
    local_to_global,
    spec_reduce,
    spec_mix,
    spec_expand,
    norm_gains,
    norm_biases,
    run_means,
    run_vars,
):
    anywhere = pl.BlockSpec(memory_space=pl.ANY)
    vmem = pl.BlockSpec(memory_space=pltpu.VMEM)
    dma = pltpu.SemaphoreType.DMA
    band = (ROWS, LONG, 512)
    out_y, out_g, out_we, out_wl, *out_norms = pl.pallas_call(
        network_kernel,
        out_shape=(
            jax.ShapeDtypeStruct((2,) + band, BF16),
            jax.ShapeDtypeStruct((2,) + band, BF16),
            jax.ShapeDtypeStruct((4, PIECES * EARLY, 128), BF16),
            jax.ShapeDtypeStruct((4, PIECES * LATE, 128), BF16),
            *[jax.ShapeDtypeStruct((2, 3 * CS + 512), F32)] * 4,
        ),
        in_specs=[anywhere, anywhere, pl.BlockSpec(memory_space=pltpu.SMEM)]
        + [anywhere] * 8
        + [vmem] * 2,
        out_specs=(anywhere,) * 4 + (vmem,) * 4,
        scratch_shapes=[
            pltpu.VMEM((LAYERS, 9, CL, 512), BF16),
            pltpu.VMEM((LAYERS, 9, CG, CL), BF16),
            pltpu.VMEM((LAYERS, CS, CG), BF16),
            pltpu.VMEM((LAYERS, FULL, FULL), BF16),
            pltpu.VMEM((LAYERS, CS, CG), BF16),
            pltpu.VMEM((2, 2, 3 * CS + 512), F32),
            pltpu.VMEM((2, 2, 3 * CS + 512), F32),
            pltpu.VMEM((LAYERS, 8, 512), F32),
            pltpu.VMEM((LAYERS + 1,) + band, BF16),
            pltpu.VMEM((ROWS + 2, LONG, 1536), BF16),
            pltpu.VMEM((2, LONG, 512), BF16),
            pltpu.VMEM((LAYERS, PAIRS, 256, CS), F32),
            pltpu.VMEM((PAIRS, 256, CS), F32),
            pltpu.VMEM((LAYERS, SLOTS, FULL), BF16),
            pltpu.VMEM((LAYERS, SLOTS, FULL), F32),
            pltpu.VMEM((LAYERS, PAIRS, 256, CS), BF16),
            pltpu.VMEM((LAYERS, PAIRS, 256, 512), F32),
            pltpu.VMEM((PAIRS, 256, 128), F32),
            pltpu.VMEM((SLOTS, 128), F32),
            pltpu.VMEM((256, 256), BF16),
            pltpu.VMEM((256, 256), BF16),
            pltpu.VMEM((256, 256), BF16),
            pltpu.VMEM((256, 256), BF16),
            pltpu.VMEM((4, 256, 512), BF16),
            pltpu.VMEM((512, 1024), BF16),
            pltpu.VMEM((1024, FULL), BF16),
            pltpu.VMEM((SLOTS, FULL), F32),
            pltpu.VMEM((SLOTS, FULL), BF16),
            pltpu.VMEM((PAIRS, 256, CS), BF16),
            pltpu.VMEM((PAIRS, 256, 512), F32),
            pltpu.VMEM((2,) + band, BF16),
            pltpu.VMEM((512, ROWS * LONG), BF16),
            pltpu.VMEM((PIECES * EARLY, 128), BF16),
            pltpu.VMEM((PIECES * LATE, 128), BF16),
            pltpu.VMEM((PIECES * EARLY, 128), BF16),
            pltpu.VMEM((PIECES * LATE, 128), BF16),
            pltpu.VMEM((EARLY, 128), BF16),
            pltpu.VMEM((LATE, 128), BF16),
            pltpu.VMEM((4, 8, 128), F32),
            pltpu.VMEM((4, MEMBERS, 8, 128), F32),
            pltpu.VMEM((2, MEMBERS, 32, FULL), BF16),
            pltpu.VMEM((2, MEMBERS, 32, FULL), BF16),
            pltpu.VMEM((LAYERS, 16, 512), F32),
            pltpu.VMEM((2, 16, 512), F32),
            dma((3, 8)),
            dma((2, 2)),
            dma((ROWS, 2)),
            dma((2,)),
            dma((2,)),
            dma((4, MEMBERS)),
            dma((4, MEMBERS)),
            dma((2, MEMBERS)),
            dma((2, MEMBERS)),
            dma((2, ROWS)),
            dma((2, ROWS)),
            dma((2, ROWS)),
            dma((2, ROWS)),
            dma((2, 2, 8, 4)),
            dma((2, 2, 8, 4)),
            dma((2,)),
        ],
        compiler_params=pltpu.CompilerParams(
            collective_id=0, has_side_effects=True, vmem_limit_bytes=63 << 20
        ),
        name="network",
    )(
        inputs[:, 0],
        cotangent[:, 0],
        shapes,
        local_to_local[0],
        global_to_local[0],
        local_to_global[0],
        jnp.swapaxes(spec_reduce[0], 1, 2),
        spec_mix[0],
        spec_expand[0],
        norm_gains[0],
        norm_biases[0],
        run_means[0],
        run_vars[0],
    )
    grad_ll = out_we[2:, AT_LL:AT_GL].astype(F32).reshape(2, 9, CL, CL)
    grad_gl = out_we[2:, AT_GL:AT_KG].astype(F32).reshape(2, 9, CG, CL)
    grad_lift = tiles_of(9 * CL, out_we[2:, AT_KG:AT_E]).reshape(2, 9, CL, CG)
    grad_expand = tiles_of(CS, out_we[2:, AT_E:])
    grad_mix = tiles_of(FULL, out_wl[2:, AT_M:])
    grad_reduce = jnp.swapaxes(tiles_of(CS, out_wl[2:, AT_R:]), 1, 2)
    out_gains, out_biases, out_means, out_vars = out_norms
    return (
        out_y[None, :, None],
        out_g.astype(F32)[None, :, None],
        grad_ll[None],
        grad_gl[None],
        grad_lift[None],
        grad_reduce[None],
        grad_mix[None],
        grad_expand[None],
        out_gains[None],
        out_biases[None],
        out_means[None],
        out_vars[None],
    )


def solution(mesh):
    in_specs = (
        P(None, None, "dp", None, None),
        P(None, None, "dp", None, None),
        P(),
        P("section", None, None, None, None),
        P("section", None, None, None, None),
        P("section", None, None, None, None),
        P("section", None, None, None),
        P("section", None, None, None),
        P("section", None, None, None),
        P("section", None, None),
        P("section", None, None),
        P("section", None, None),
        P("section", None, None),
    )
    out_specs = (
        P("section", None, None, "dp", None, None),
        P("section", None, None, "dp", None, None),
        P("section", None, None, None, None),
        P("section", None, None, None, None),
        P("section", None, None, None, None),
        P("section", None, None, None),
        P("section", None, None, None),
        P("section", None, None, None),
        P("section", None, None),
        P("section", None, None),
        P("section", None, None),
        P("section", None, None),
    )
    dp_size = mesh.shape["dp"]
    banded = dp_size == MEMBERS and LONG == dp_size * ROWS
    return jax.shard_map(
        on_band if banded else on_device, mesh=mesh, in_specs=in_specs, out_specs=out_specs, check_vma=False
    )
```

```python
import jax
import jax.numpy as jnp
from jax import lax
from jax.experimental import pallas as pl
from jax.experimental.pallas import tpu as pltpu
from jax.sharding import PartitionSpec as P

CL = 128
CG = 384
CS = 192
LONG = 128


EPSILON = 1e-05
MOMENTUM = 0.1
PRECISE = lax.Precision.HIGHEST


def with_halo(block, sides, width):
    for axis, dim in sides:
        count = lax.axis_size(axis)
        forward = [(i, i + 1) for i in range(count - 1)]
        backward = [(target, source) for source, target in forward]
        low = lax.ppermute(
            lax.slice_in_dim(block, block.shape[dim] - width, None, axis=dim), axis, forward
        )
        high = lax.ppermute(lax.slice_in_dim(block, 0, width, axis=dim), axis, backward)
        block = jnp.concatenate([low, block, high], axis=dim)
    return block


def from_behind(value, axis, steps):
    count = lax.axis_size(axis)
    first, last = (max(0, -steps), min(count, count - steps))
    return lax.ppermute(value, axis, [(source, source + steps) for source in range(first, last)])


def dft_tables(height, width, long_side, freq_total):
    position = jnp.arange(long_side, dtype=jnp.int32)
    frequency = jnp.arange(freq_total, dtype=jnp.int32)
    half_width = width // 2
    width_real = width.astype(jnp.float32)
    height_real = height.astype(jnp.float32)
    width_phase = position[:, None] * frequency[None, :] % width
    width_angle = 2.0 * jnp.pi / width_real * width_phase.astype(jnp.float32)
    width_valid = ((position[:, None] < width) & (frequency[None, :] <= half_width)).astype(
        jnp.float32
    )
    width_scale = lax.rsqrt(width_real)
    fwd_cos = jnp.cos(width_angle) * width_scale * width_valid
    fwd_sin = -jnp.sin(width_angle) * width_scale * width_valid
    edge_freq = (frequency == 0) | (frequency == half_width)
    freq_weight = jnp.where(edge_freq, 1.0, 2.0).astype(jnp.float32)
    inv_cos = freq_weight[:, None] * fwd_cos.T
    inv_sin = freq_weight[:, None] * fwd_sin.T
    height_phase = position[:, None] * position[None, :] % height
    height_angle = 2.0 * jnp.pi / height_real * height_phase.astype(jnp.float32)
    height_valid = ((position[:, None] < height) & (position[None, :] < height)).astype(jnp.float32)
    height_scale = lax.rsqrt(height_real)
    row_cos = jnp.cos(height_angle) * height_scale * height_valid
    row_sin = jnp.sin(height_angle) * height_scale * height_valid
    return (fwd_cos, fwd_sin, inv_cos, inv_sin, row_cos, row_sin)


def geometry(shape_row, band_index, band_size, freq_total, freq_local, map_count):
    height = shape_row[0]
    width = shape_row[1]
    position = jnp.arange(LONG, dtype=jnp.int32)
    band_rows = band_index * band_size + jnp.arange(band_size, dtype=jnp.int32)
    pix_mask = ((band_rows[:, None] < height) & (position[None, :] < width)).astype(jnp.float32)[
        None, :, :, None
    ]
    local_freq = band_index * freq_local + jnp.arange(freq_local, dtype=jnp.int32)
    freq_mask = ((position[:, None] < height) & (local_freq[None, :] <= width // 2)).astype(
        jnp.float32
    )[None, :, :, None]
    pix_count = (map_count * height * width).astype(jnp.float32)
    spec_count = (map_count * height * (width // 2 + 1)).astype(jnp.float32)
    return (pix_mask, freq_mask, pix_count, spec_count, dft_tables(height, width, LONG, freq_total))


def conv_rows(padded, kernel):
    shaped = kernel.reshape(3, 3, kernel.shape[1], kernel.shape[2])
    return lax.conv_general_dilated(
        padded,
        shaped,
        (1, 1),
        "VALID",
        dimension_numbers=("NHWC", "HWIO", "NHWC"),
        preferred_element_type=jnp.float32,
    )


def flipped(kernel):
    shaped = kernel.reshape(3, 3, kernel.shape[1], kernel.shape[2])[::-1, ::-1]
    return jnp.swapaxes(shaped, 2, 3).reshape(9, kernel.shape[2], kernel.shape[1])


def kernel_grad(padded, grad_out, band_size, width):
    tap_grads = []
    for row_tap in range(3):
        for col_tap in range(3):
            window = padded[:, row_tap : row_tap + band_size, col_tap : col_tap + width, :]
            tap_grads.append(
                jnp.einsum("mrwi,mrwo->io", window, grad_out, preferred_element_type=jnp.float32)
            )
    return jnp.stack(tap_grads)


def width_forward(entry, table):
    return jnp.einsum("mrwc,wf->mrfc", entry, table, precision=PRECISE)


def width_forward_adj(entry, table):
    return jnp.einsum("mrfc,wf->mrwc", entry, table, precision=PRECISE)


def width_inverse(entry, table):
    return jnp.einsum("mrfc,fw->mrwc", entry, table, precision=PRECISE)


def width_inverse_adj(entry, table):
    return jnp.einsum("mrwc,fw->mrfc", entry, table, precision=PRECISE)


def height_apply(table, entry):
    return jnp.einsum("kn,mnfc->mkfc", table, entry, precision=PRECISE)


def height_adjoint(table, entry):
    return jnp.einsum("kn,mkfc->mnfc", table, entry, precision=PRECISE)


def rows_forward(row_cos, row_sin, entry):
    half_ch = entry.shape[-1] // 2
    real_in = entry[..., :half_ch]
    imag_in = entry[..., half_ch:]
    real_out = height_apply(row_cos, real_in) + height_apply(row_sin, imag_in)
    imag_out = height_apply(row_cos, imag_in) - height_apply(row_sin, real_in)
    return jnp.concatenate([real_out, imag_out], axis=-1)


def rows_inverse(row_cos, row_sin, entry):
    half_ch = entry.shape[-1] // 2
    real_in = entry[..., :half_ch]
    imag_in = entry[..., half_ch:]
    real_out = height_adjoint(row_cos, real_in) - height_adjoint(row_sin, imag_in)
    imag_out = height_adjoint(row_cos, imag_in) + height_adjoint(row_sin, real_in)
    return jnp.concatenate([real_out, imag_out], axis=-1)


def split_pairs(totals, widths):
    pairs = []
    offset = 0
    for lead_width, tail_width in zip(widths[0::2], widths[1::2]):
        lead_part = totals[offset : offset + lead_width]
        tail_part = totals[offset + lead_width : offset + lead_width + tail_width]
        pairs.append((lead_part, tail_part))
        offset = offset + lead_width + tail_width
    return pairs


def moments(entries, weights):
    pieces = []
    for entry, weight in zip(entries, weights):
        masked = entry * weight
        pieces.append(jnp.sum(masked, axis=(0, 1, 2)))
        pieces.append(jnp.sum(masked * entry, axis=(0, 1, 2)))
    totals = lax.psum(jnp.concatenate(pieces), "dp")
    return split_pairs(totals, [piece.shape[0] for piece in pieces])


def grad_moments(grads_in, normed_in):
    pieces = []
    for grad_pre, normed in zip(grads_in, normed_in):
        pieces.append(jnp.sum(grad_pre, axis=(0, 1, 2)))
        pieces.append(jnp.sum(grad_pre * normed, axis=(0, 1, 2)))
    totals = lax.psum(jnp.concatenate(pieces), "dp")
    return split_pairs(totals, [piece.shape[0] for piece in pieces])


def normalize(entry, sum_pair, count_now):
    mean_val = sum_pair[0] / count_now
    var_val = sum_pair[1] / count_now - mean_val * mean_val
    inv_std = lax.rsqrt(var_val + EPSILON)
    return ((entry - mean_val) * inv_std, inv_std, mean_val, var_val)


def silu_slope(pre_act):
    sigmoid_val = jax.nn.sigmoid(pre_act)
    return sigmoid_val * (1.0 + pre_act * (1.0 - sigmoid_val))


def norm_backward(grad_pre, normed, inv_std, gain_part, sum_pair, count_now, weight):
    return (
        weight
        * inv_std
        * gain_part
        * (grad_pre - sum_pair[0] / count_now - normed * sum_pair[1] / count_now)
    )


def layer_forward(layer_in, geometry_now, kernels, gain_vec, bias_vec):
    pix_mask, freq_mask, pix_count, spec_count, tables = geometry_now
    fwd_cos, fwd_sin, inv_cos, inv_sin, row_cos, row_sin = tables
    local_kernel, lift_kernel, reduce_kernel, mix_kernel, expand_kernel = kernels
    acts_low = layer_in.astype(jnp.bfloat16)
    padded = with_halo(acts_low, (("dp", 1),), 1)
    padded = jnp.pad(padded, ((0, 0), (0, 0), (1, 1), (0, 0)))
    local_out = conv_rows(padded, local_kernel)
    global_conv = conv_rows(padded[..., :CL], lift_kernel)
    reduced = jnp.einsum(
        "mrwc,cd->mrwd", acts_low[..., CL:], reduce_kernel, preferred_element_type=jnp.float32
    )
    one_stats = moments([reduced], [pix_mask])[0]
    normed_one, inv_one, mean_one, var_one = normalize(reduced, one_stats, pix_count)
    pre_one = normed_one * gain_vec[:CS] + bias_vec[:CS]
    upper_spec = jax.nn.silu(pre_one) * pix_mask
    spectrum = jnp.concatenate(
        [width_forward(upper_spec, fwd_cos), width_forward(upper_spec, fwd_sin)], axis=-1
    ).astype(jnp.bfloat16)
    columns = lax.all_to_all(spectrum, "dp", split_axis=2, concat_axis=1, tiled=True).astype(
        jnp.float32
    )
    spectra = rows_forward(row_cos, row_sin, columns).astype(jnp.bfloat16)
    mixed = jnp.einsum("mkfc,cd->mkfd", spectra, mix_kernel, preferred_element_type=jnp.float32)
    two_stats = moments([mixed], [freq_mask])[0]
    normed_two, inv_two, mean_two, var_two = normalize(mixed, two_stats, spec_count)
    pre_two = normed_two * gain_vec[CS : 3 * CS] + bias_vec[CS : 3 * CS]
    activated = jax.nn.silu(pre_two) * freq_mask
    inverse = rows_inverse(row_cos, row_sin, activated).astype(jnp.bfloat16)
    returned = lax.all_to_all(inverse, "dp", split_axis=1, concat_axis=2, tiled=True).astype(
        jnp.float32
    )
    half_ch = returned.shape[-1] // 2
    restored = width_inverse(returned[..., :half_ch], inv_cos) + width_inverse(
        returned[..., half_ch:], inv_sin
    )
    summed = (upper_spec + restored).astype(jnp.bfloat16)
    spec_out = jnp.einsum(
        "mrwc,cd->mrwd", summed, expand_kernel, preferred_element_type=jnp.float32
    )
    global_out = global_conv + spec_out
    loc_stats, glo_stats = moments([local_out, global_out], [pix_mask, pix_mask])
    normed_loc, inv_loc, mean_loc, var_loc = normalize(local_out, loc_stats, pix_count)
    normed_glo, inv_glo, mean_glo, var_glo = normalize(global_out, glo_stats, pix_count)
    pre_loc = normed_loc * gain_vec[3 * CS : 3 * CS + CL] + bias_vec[3 * CS : 3 * CS + CL]
    pre_glo = normed_glo * gain_vec[3 * CS + CL :] + bias_vec[3 * CS + CL :]
    result = jnp.concatenate([jax.nn.silu(pre_loc), jax.nn.silu(pre_glo)], axis=-1) * pix_mask
    stored = (
        padded,
        pre_one,
        normed_one,
        inv_one,
        spectra,
        pre_two,
        normed_two,
        inv_two,
        summed,
        pre_loc,
        normed_loc,
        inv_loc,
        pre_glo,
        normed_glo,
        inv_glo,
    )
    means_layer = jnp.concatenate([mean_one, mean_two, mean_loc, mean_glo])
    vars_layer = jnp.concatenate([var_one, var_two, var_loc, var_glo])
    return (result, stored, (means_layer, vars_layer))


def layer_backward(grad_result, stored, geometry_now, kernels, gain_vec):
    (
        padded,
        pre_one,
        normed_one,
        inv_one,
        spectra,
        pre_two,
        normed_two,
        inv_two,
        summed,
        pre_loc,
        normed_loc,
        inv_loc,
        pre_glo,
        normed_glo,
        inv_glo,
    ) = stored
    pix_mask, freq_mask, pix_count, spec_count, tables = geometry_now
    fwd_cos, fwd_sin, inv_cos, inv_sin, row_cos, row_sin = tables
    local_kernel, lift_kernel, reduce_kernel, mix_kernel, expand_kernel = kernels
    band_size = pre_one.shape[1]
    width = pre_one.shape[2]
    grad_loc = grad_result[..., :CL] * pix_mask * silu_slope(pre_loc)
    grad_glo = grad_result[..., CL:] * pix_mask * silu_slope(pre_glo)
    loc_pair, glo_pair = grad_moments([grad_loc, grad_glo], [normed_loc, normed_glo])
    d_local = norm_backward(
        grad_loc, normed_loc, inv_loc, gain_vec[3 * CS : 3 * CS + CL], loc_pair, pix_count, pix_mask
    ).astype(jnp.bfloat16)
    d_global = norm_backward(
        grad_glo, normed_glo, inv_glo, gain_vec[3 * CS + CL :], glo_pair, pix_count, pix_mask
    ).astype(jnp.bfloat16)
    grad_expand = jnp.einsum("mrwc,mrwd->cd", summed, d_global, preferred_element_type=jnp.float32)
    d_summed = jnp.einsum(
        "mrwd,cd->mrwc", d_global, expand_kernel, preferred_element_type=jnp.float32
    )
    d_returned = jnp.concatenate(
        [width_inverse_adj(d_summed, inv_cos), width_inverse_adj(d_summed, inv_sin)], axis=-1
    ).astype(jnp.bfloat16)
    d_inverse = lax.all_to_all(d_returned, "dp", split_axis=2, concat_axis=1, tiled=True).astype(
        jnp.float32
    )
    d_activated = rows_forward(row_cos, row_sin, d_inverse)
    grad_two = d_activated * freq_mask * silu_slope(pre_two)
    two_pair = grad_moments([grad_two], [normed_two])[0]
    d_mixed = norm_backward(
        grad_two, normed_two, inv_two, gain_vec[CS : 3 * CS], two_pair, spec_count, freq_mask
    ).astype(jnp.bfloat16)
    grad_mix = jnp.einsum("mkfc,mkfd->cd", spectra, d_mixed, preferred_element_type=jnp.float32)
    d_spectra = jnp.einsum("mkfd,cd->mkfc", d_mixed, mix_kernel, preferred_element_type=jnp.float32)
    d_columns = rows_inverse(row_cos, row_sin, d_spectra).astype(jnp.bfloat16)
    d_spectrum = lax.all_to_all(d_columns, "dp", split_axis=1, concat_axis=2, tiled=True).astype(
        jnp.float32
    )
    half_ch = d_spectrum.shape[-1] // 2
    d_upper = (
        d_summed
        + width_forward_adj(d_spectrum[..., :half_ch], fwd_cos)
        + width_forward_adj(d_spectrum[..., half_ch:], fwd_sin)
    )
    grad_one = d_upper * pix_mask * silu_slope(pre_one)
    one_pair = grad_moments([grad_one], [normed_one])[0]
    d_reduced = norm_backward(
        grad_one, normed_one, inv_one, gain_vec[:CS], one_pair, pix_count, pix_mask
    ).astype(jnp.bfloat16)
    acts_low = padded[:, 1:-1, 1:-1, :]
    grad_reduce = jnp.einsum(
        "mrwc,mrwd->cd", acts_low[..., CL:], d_reduced, preferred_element_type=jnp.float32
    )
    d_global_in = jnp.einsum(
        "mrwd,cd->mrwc", d_reduced, reduce_kernel, preferred_element_type=jnp.float32
    )
    grad_outs = jnp.concatenate([d_local, d_global], axis=-1)
    grad_pad = with_halo(grad_outs, (("dp", 1),), 1)
    grad_pad = jnp.pad(grad_pad, ((0, 0), (0, 0), (1, 1), (0, 0)))
    d_acts = conv_rows(grad_pad[..., :CL], flipped(local_kernel))
    d_lift = conv_rows(grad_pad[..., CL:], flipped(lift_kernel))
    d_input = d_acts + jnp.concatenate([d_lift, d_global_in], axis=-1)
    grad_local_kernel = kernel_grad(padded, d_local, band_size, width)
    grad_lift = kernel_grad(padded[..., :CL], d_global, band_size, width)
    gains_grad = jnp.concatenate([one_pair[1], two_pair[1], loc_pair[1], glo_pair[1]])
    biases_grad = jnp.concatenate([one_pair[0], two_pair[0], loc_pair[0], glo_pair[0]])
    return (
        d_input,
        (grad_local_kernel, grad_lift, grad_reduce, grad_mix, grad_expand),
        (gains_grad, biases_grad),
    )


def block_forward(block_in, geometry_now, kernels, gain_all, bias_all):
    base = block_in.astype(jnp.float32) * geometry_now[0]
    first_out, first_stored, first_stats = layer_forward(
        base, geometry_now, kernels[0], gain_all[0], bias_all[0]
    )
    second_out, second_stored, second_stats = layer_forward(
        first_out, geometry_now, kernels[1], gain_all[1], bias_all[1]
    )
    return (
        (second_out + base).astype(jnp.bfloat16),
        (first_stored, second_stored),
        (first_stats, second_stats),
    )


def block_backward(grad_in, stored, geometry_now, kernels, gain_all):
    pix_mask = geometry_now[0]
    grad_masked = grad_in * pix_mask
    d_first, second_kernels, second_norms = layer_backward(
        grad_masked, stored[1], geometry_now, kernels[1], gain_all[1]
    )
    d_base, first_kernels, first_norms = layer_backward(
        d_first, stored[0], geometry_now, kernels[0], gain_all[0]
    )
    return (
        (grad_masked + d_base) * pix_mask,
        (first_kernels, second_kernels),
        (first_norms, second_norms),
    )


def running_update(mean_now, var_now, layer_stats, geometry_now):
    pix_count = geometry_now[2]
    spec_count = geometry_now[3]
    counts = jnp.concatenate(
        [
            jnp.full((CS,), pix_count, jnp.float32),
            jnp.full((2 * CS,), spec_count, jnp.float32),
            jnp.full((CL + CG,), pix_count, jnp.float32),
        ]
    )
    batch_means = jnp.stack([layer_stats[0][0], layer_stats[1][0]])
    batch_vars = jnp.stack([layer_stats[0][1], layer_stats[1][1]])
    new_mean = (1.0 - MOMENTUM) * mean_now + MOMENTUM * batch_means
    new_var = (1.0 - MOMENTUM) * var_now + MOMENTUM * batch_vars * counts / (counts - 1.0)
    return (new_mean, new_var)


def on_device(
    inputs,
    cotangent,
    shapes,
    local_to_local,
    global_to_local,
    local_to_global,
    spec_reduce,
    spec_mix,
    spec_expand,
    norm_gains,
    norm_biases,
    run_means,
    run_vars,
):
    section_id = lax.axis_index("section")
    band_index = lax.axis_index("dp")
    n_dp = lax.axis_size("dp")
    micro_count = inputs.shape[0]
    map_count = inputs.shape[1]
    band_size = inputs.shape[2]
    freq_total = (LONG // 2 + n_dp) // n_dp * n_dp
    freq_local = freq_total // n_dp
    kernels = []
    for layer_pos in range(2):
        local_kernel = jnp.concatenate(
            [local_to_local[0, layer_pos], global_to_local[0, layer_pos]], axis=1
        )
        kernels.append(
            (
                local_kernel,
                local_to_global[0, layer_pos],
                spec_reduce[0, layer_pos],
                spec_mix[0, layer_pos],
                spec_expand[0, layer_pos],
            )
        )
    gain_all = norm_gains[0]
    bias_all = norm_biases[0]
    received = jnp.zeros(inputs.shape[1:], jnp.bfloat16)
    run_mean = run_means[0]
    run_var = run_vars[0]
    outputs = jnp.zeros(inputs.shape, jnp.bfloat16)
    saved_inputs = []
    saved_geometry = []
    for tick_pos in range(micro_count + 1):
        micro_index = tick_pos - section_id
        is_valid = (micro_index >= 0) & (micro_index < micro_count)
        micro_slot = jnp.clip(micro_index, 0, micro_count - 1)
        own_input = lax.dynamic_index_in_dim(inputs, micro_slot, 0, keepdims=False)
        block_in = jnp.where(section_id == 0, own_input, received)
        shape_row = lax.dynamic_index_in_dim(shapes, micro_slot, 0, keepdims=False)
        geometry_now = geometry(shape_row, band_index, band_size, freq_total, freq_local, map_count)
        block_out, stored, layer_stats = block_forward(
            block_in, geometry_now, kernels, gain_all, bias_all
        )
        new_mean, new_var = running_update(run_mean, run_var, layer_stats, geometry_now)
        run_mean = jnp.where(is_valid, new_mean, run_mean)
        run_var = jnp.where(is_valid, new_var, run_var)
        updated = lax.dynamic_update_index_in_dim(outputs, block_out, micro_slot, 0)
        outputs = jnp.where(is_valid, updated, outputs)
        saved_inputs.append(block_in)
        saved_geometry.append(geometry_now)
        if tick_pos < micro_count:
            received = from_behind(block_out, "section", 1)
    kernel_acc = [jnp.zeros((2,) + part_now.shape, jnp.float32) for part_now in kernels[0]]
    gain_acc = jnp.zeros(gain_all.shape, jnp.float32)
    bias_acc = jnp.zeros(bias_all.shape, jnp.float32)
    received_grad = jnp.zeros(inputs.shape[1:], jnp.bfloat16)
    grads_out = jnp.zeros(inputs.shape, jnp.float32)
    for tick_pos in range(micro_count + 1):
        micro_index = micro_count - tick_pos - section_id
        is_valid = (micro_index >= 0) & (micro_index < micro_count)
        micro_slot = jnp.clip(micro_index, 0, micro_count - 1)
        scale_valid = is_valid.astype(jnp.float32)
        forward_tick = micro_count - tick_pos
        geometry_now = saved_geometry[forward_tick]
        recomputed = block_forward(
            saved_inputs[forward_tick], geometry_now, kernels, gain_all, bias_all
        )
        stored = recomputed[1]
        own_grad = lax.dynamic_index_in_dim(cotangent, micro_slot, 0, keepdims=False)
        grad_in = jnp.where(section_id == 1, own_grad, received_grad).astype(jnp.float32)
        grad_input, kernel_grads, norm_grads = block_backward(
            grad_in, stored, geometry_now, kernels, gain_all
        )
        sent_grad = grad_input.astype(jnp.bfloat16)
        kept_grad = jnp.where(section_id == 1, sent_grad.astype(jnp.float32), grad_input)
        updated = lax.dynamic_update_index_in_dim(grads_out, kept_grad, micro_slot, 0)
        grads_out = jnp.where(is_valid, updated, grads_out)
        stacked = [
            jnp.stack([kernel_grads[0][part_pos], kernel_grads[1][part_pos]]) * scale_valid
            for part_pos in range(5)
        ]
        gain_acc = gain_acc + jnp.stack([norm_grads[0][0], norm_grads[1][0]]) * scale_valid
        bias_acc = bias_acc + jnp.stack([norm_grads[0][1], norm_grads[1][1]]) * scale_valid
        kernel_acc = [acc_part + new_part for acc_part, new_part in zip(kernel_acc, stacked)]
        if tick_pos < micro_count:
            received_grad = from_behind(sent_grad, "section", -1)
    totals = lax.psum(
        (kernel_acc[0], kernel_acc[1], kernel_acc[2], kernel_acc[3], kernel_acc[4]), "dp"
    )
    grad_ll = totals[0][:, :, :CL, :]
    grad_gl = totals[0][:, :, CL:, :]
    return (
        outputs[None],
        grads_out[None],
        grad_ll[None],
        grad_gl[None],
        totals[1][None],
        totals[2][None],
        totals[3][None],
        totals[4][None],
        gain_acc[None],
        bias_acc[None],
        run_mean[None],
        run_var[None],
    )


F32 = jnp.float32
BF16 = jnp.bfloat16
MESH = pl.DeviceIdType.MESH
MEMBERS = 16
ROWS = 8
LAYERS = 4
PAIRS = 4
HALF = 192
FULL = 384
SLOTS = 640
PIECES = 32
EARLY = 272
LATE = 64
AT_LL = 0
AT_GL = 1152
AT_KG = 4608
AT_E = 8064
AT_M = 0
AT_R = 1152
SECTION_NAMES = ("one", "two", "out")


def dot(a, b):
    return lax.dot_general(a, b, (((1,), (0,)), ((), ())), preferred_element_type=F32)


def dot_nt(a, b):
    return lax.dot_general(a, b, (((1,), (1,)), ((), ())), preferred_element_type=F32)


def dot_tn(a, b):
    return lax.dot_general(a, b, (((0,), (0,)), ((), ())), preferred_element_type=F32)


def sigmoid(v):
    return 0.5 * jnp.tanh(0.5 * v) + 0.5


def fold(v):
    return jnp.sum(v.reshape(v.shape[0] // 8, 8, v.shape[1]), axis=0)


def wide(row, lanes):
    whole, rest = divmod(lanes, 128)
    parts = [row] * whole + ([row[:, :rest]] if rest else [])
    return jnp.concatenate(parts, axis=1)


def network_kernel(
    inputs, cot, shapes, ll, gl, lg, red, mix, exp, gains, biases, run_m, run_v,
    out_y, out_g, out_we, out_wl, out_gains, out_biases, out_m, out_v,
    w_c, w_gl, w_r, w_m, w_e, raw_g, raw_b, pars, acts, shifted, halo, v1, u, spec, mixed, tsum, v34,
    pmask, qmask, tf, tft, tg, tgt, hf, hi, vab, e2, dq, ds, g, gblk, at,
    gwe, gwl, rbe, rbl, fine, finl,
    ssum, rsum, send, recv, stats, stats_far,
    sem_w, sem_in, sem_cot, sem_halo_s, sem_halo_r, sem_ar_s, sem_ar_r, sem_aa_s, sem_aa_r,
    sem_y_s, sem_y_r, sem_g_s, sem_g_r, sem_rs, sem_rr, sem_st,
):
    s = lax.axis_index("section")
    d = lax.axis_index("dp")
    n_dp = lax.axis_size("dp")
    per = n_dp // 2
    grp = lax.div(d, per)

    def differ(a, b):
        return a + b - 2 * a * b

    def mirrored(chip):
        return (3 - lax.div(chip, 4)) * 4 + lax.rem(chip, 4)

    half = differ(s, grp)
    me = jnp.where(s == 0, d, mirrored(d))
    first = (me == 0).astype(F32)
    at_z = lax.div(d, 4)
    outer = (at_z == 0) | (at_z == 3)

    def member(group, k):
        core = differ(lax.div(k, per), group)
        return (core, jnp.where(core == 0, k, mirrored(k)))

    def peer(i):
        flips = MEMBERS - 1 - i
        chip = lax.rem(d, per)
        other = grp * per
        for bit in (1, 2, 4):
            other = other + bit * differ(lax.rem(lax.div(chip, bit), 2), lax.rem(lax.div(flips, 2 * bit), 2))
        core = differ(s, lax.rem(flips, 2))
        return jnp.where(core == 0, other, mirrored(other)), (core, other)

    barrier = pltpu.get_barrier_semaphore()
    total = 2 * n_dp
    flat = s * n_dp + d

    def greet(i, c):
        other = lax.rem(flat + 1 + i, total)
        pl.semaphore_signal(
            barrier, inc=1, device_id=(lax.div(other, n_dp), lax.rem(other, n_dp)), device_id_type=MESH
        )
        return c

    lax.fori_loop(0, total - 1, greet, 0)

    own = pl.ds(2 * s, 2)
    places = [
        (red, w_r.at[own]),
        (gains, raw_g.at[s]),
        (biases, raw_b.at[s]),
        (ll, w_c.at[own, :, :, 0:CL]),
        (lg, w_c.at[own, :, :, CL:]),
        (gl, w_gl.at[own]),
        (mix, w_m.at[own]),
        (exp, w_e.at[own]),
    ]
    local_w = [pltpu.make_async_copy(a, b, sem_w.at[0, i]) for i, (a, b) in enumerate(places)]
    for c in local_w:
        c.start()

    pl.semaphore_wait(barrier, total - 1)

    across = (s, mirrored(d))
    stays = s == 0

    def across_copy(source, target, sems):
        return pltpu.make_async_remote_copy(
            source, target, sems.at[0], sems.at[1], device_id=across, device_id_type=MESH
        )

    def when_far(do):
        pl.when(jnp.logical_not(stays))(do)

    input_near = lambda: pltpu.make_async_copy(inputs.at[half], acts.at[0], sem_in.at[0, 0])

    def input_far(part):
        lanes = pl.ds(CL, CG) if part == 0 else pl.ds(0, CL)
        return across_copy(inputs.at[half, :, :, lanes], acts.at[0, :, :, lanes], sem_in.at[part])

    cot_near = lambda: pltpu.make_async_copy(cot.at[half], gblk.at[1], sem_cot.at[0, 0])

    def cot_far(row):
        return across_copy(cot.at[half, row], gblk.at[1, row], sem_cot.at[row])

    def push_rows(parity, window, do):
        if window % 2:
            row = 4 * parity + window - 1

            @pl.when(jnp.logical_not(outer))
            def _():
                do(row)
                do(row + 1)
        else:
            index = 3 * parity + window // 2
            row = jnp.where(index < 4, index, 2 * index - 4)

            @pl.when(outer)
            def _():
                do(row)
                pl.when(index >= 4)(lambda: do(row + 1))

    pl.when(stays)(lambda: input_near().start())
    when_far(lambda: input_far(0).start())
    when_far(lambda: input_far(1).start())
    partner = (1 - s, d)
    remote_w = [
        pltpu.make_async_remote_copy(
            a, b, sem_w.at[1, i], sem_w.at[2, i], device_id=partner, device_id_type=MESH
        )
        for i, (a, b) in enumerate(places)
    ]
    for c in remote_w:
        c.start()

    height = shapes[grp, 0]
    width = shapes[grp, 1]
    col = lax.broadcasted_iota(jnp.int32, (128, 128), 0)
    for q in range(PAIRS):
        for h in range(2):
            row_ok = (ROWS * me + 2 * q + h < height).astype(F32)
            pmask[q, h * 128 : (h + 1) * 128, :] = (col < width).astype(F32) * row_ok
    for f in range(4):
        f_ok = (4 * me + f <= lax.div(width, 2)).astype(F32)
        qmask[f * 128 : (f + 1) * 128, :] = (col < height).astype(F32) * f_ok
    qmask[512:640, :] = (col < height).astype(F32) * (64 <= lax.div(width, 2)).astype(F32) * first

    def inverse(count, less=0):
        return 1.0 / jnp.full((1, 128), (count - less).astype(F32))

    inv_n = inverse(height * width)
    inv_ns = inverse(height * (lax.div(width, 2) + 1))

    row_a = lax.broadcasted_iota(jnp.int32, (128, 512), 0)
    col_a = lax.broadcasted_iota(jnp.int32, (128, 512), 1)
    r_of = (col_a >> 5) * 8 + ((col_a & 31) >> 3) * 2 + (col_a & 1)
    sel_r = (row_a == r_of).astype(F32).astype(BF16)
    f_of = (col_a >> 1) & 3
    row_b = lax.broadcasted_iota(jnp.int32, (512, 128), 0)
    col_b = lax.broadcasted_iota(jnp.int32, (512, 128), 1)
    r_ob = (row_b >> 5) * 8 + ((row_b & 31) >> 3) * 2 + (row_b & 1)
    sel_rt = (col_b == r_ob).astype(F32).astype(BF16)
    f_ob = (row_b >> 1) & 3
    position = lax.broadcasted_iota(jnp.int32, (128, 128), 0)
    other_axis = lax.broadcasted_iota(jnp.int32, (128, 128), 1)

    def wave(index, side, limit, turn):
        side_real = jnp.full((128, 128), side.astype(F32))
        product = (index * other_axis).astype(F32)
        phase = product - side_real * jnp.floor((product + 0.5) / side_real)
        value = jnp.cos(phase * (2.0 * jnp.pi / side_real) + turn) * lax.rsqrt(side_real)
        return jnp.where((index < limit) & (other_axis < side), value, 0.0)

    half_turn = 0.5 * jnp.pi
    for part in range(2):
        base = wave(position, height, height, -half_turn * part).astype(BF16)
        spread = dot(base, sel_r)
        spread_t = dot(sel_rt, base)
        for f in range(4):
            hf[f, part * 128 : (part + 1) * 128, :] = jnp.where(f_of == f, spread, 0.0).astype(BF16)
            at_col = part * 512 + f * 128
            hi[:, at_col : at_col + 128] = jnp.where(f_ob == f, spread_t, 0.0).astype(BF16)
    row_c = lax.broadcasted_iota(jnp.int32, (128, 128), 0)
    sel_f = ((row_c >> 1) == lax.broadcasted_iota(jnp.int32, (128, 128), 1)).astype(F32).astype(BF16)
    half_width = lax.div(width, 2)
    lifted = jnp.where(position == 0, 64, position)
    waves = (
        wave(position, width, half_width + 1, 0.0),
        wave(lifted, width, half_width + 1, jnp.where(position == 0, 0.0, half_turn)),
    )
    weight = jnp.where((position == 0) | (position == half_width), 1.0, 2.0)
    for which, (plain, flipped_table) in enumerate(((tf, tft), (tg, tgt))):
        for part in range(2):
            spread = dot(sel_f, (waves[part] * weight if which else waves[part]).astype(BF16))
            spread_t = jnp.transpose(spread)
            for h in range(2):
                rows = slice(part * 128, (part + 1) * 128)
                cols = slice(h * 128, (h + 1) * 128)
                plain[rows, cols] = jnp.where((row_c & 1) == h, spread, 0.0).astype(BF16)
                flipped_table[cols, rows] = jnp.where(
                    (lax.broadcasted_iota(jnp.int32, (128, 128), 1) & 1) == h, spread_t, 0.0
                ).astype(BF16)
    stats[...] = jnp.zeros_like(stats)
    ssum[...] = jnp.zeros_like(ssum)
    shifted[0] = jnp.zeros((128, 1536), BF16)
    shifted[9] = jnp.zeros((128, 1536), BF16)
    gwe[...] = jnp.zeros_like(gwe)
    gwl[...] = jnp.zeros_like(gwl)

    def sums_start(slot):
        rsum[slot, me] = ssum[slot]

        def go(i, c):
            k, device = peer(i)
            pltpu.make_async_remote_copy(
                ssum.at[slot], rsum.at[slot, me], sem_ar_s.at[slot, k], sem_ar_r.at[slot, me],
                device_id=device, device_id_type=MESH,
            ).start()
            return c

        lax.fori_loop(0, MEMBERS - 1, go, 0)

    def sums_wait(slot, lanes):
        def go(i, c):
            k, device = peer(i)
            pltpu.make_async_remote_copy(
                ssum.at[slot], rsum.at[slot, k], sem_ar_s.at[slot, k], sem_ar_r.at[slot, k],
                device_id=device, device_id_type=MESH,
            ).wait()
            return c

        lax.fori_loop(0, MEMBERS - 1, go, 0)
        tot = jnp.sum(rsum[slot], axis=0)
        tiles = (lanes + 127) // 128
        one = jnp.concatenate([tot[i : i + 1] for i in range(tiles)], axis=1)[:, :lanes]
        two = jnp.concatenate([tot[4 + i : 5 + i] for i in range(tiles)], axis=1)[:, :lanes]
        return one, two

    def put_sums(slot, one, two):
        lanes = one.shape[1]
        for base_row, part in ((0, one), (4, two)):
            flat_part = jnp.sum(part, axis=0, keepdims=True)
            for i in range((lanes + 127) // 128):
                w = min(128, lanes - i * 128)
                ssum[slot, base_row + i : base_row + i + 1, 0:w] = flat_part[:, i * 128 : i * 128 + w]

    def swap_start(slot):
        recv[slot, me] = send[slot, me]

        def go(i, c):
            k, device = peer(i)
            pltpu.make_async_remote_copy(
                send.at[slot, k], recv.at[slot, me], sem_aa_s.at[slot, k], sem_aa_r.at[slot, me],
                device_id=device, device_id_type=MESH,
            ).start()
            return c

        lax.fori_loop(0, MEMBERS - 1, go, 0)

    def swap_wait(slot):
        def go(i, c):
            k, device = peer(i)
            pltpu.make_async_remote_copy(
                send.at[slot, k], recv.at[slot, k], sem_aa_s.at[slot, k], sem_aa_r.at[slot, k],
                device_id=device, device_id_type=MESH,
            ).wait()
            return c

        lax.fori_loop(0, MEMBERS - 1, go, 0)

    def halo_copies():
        up = lambda: pltpu.make_async_remote_copy(
            shifted.at[1, :, 512:1024], halo.at[1], sem_halo_s.at[0], sem_halo_r.at[1],
            device_id=member(grp, lax.rem(me + MEMBERS - 1, MEMBERS)), device_id_type=MESH,
        )
        down = lambda: pltpu.make_async_remote_copy(
            shifted.at[8, :, 512:1024], halo.at[0], sem_halo_s.at[1], sem_halo_r.at[0],
            device_id=member(grp, lax.rem(me + 1, MEMBERS)), device_id_type=MESH,
        )
        return up, down

    has_up = me > 0
    has_down = me < MEMBERS - 1

    def halo_start():
        up, down = halo_copies()

        @pl.when(has_up)
        def _():
            up().start()

        @pl.when(has_down)
        def _():
            down().start()

    def put_sides(index, x, flip):
        at_col = lax.broadcasted_iota(jnp.int32, (128, 512), 0)
        before = jnp.where(at_col == 0, 0.0, pltpu.roll(x, 1, 0)).astype(BF16)
        after = jnp.where(at_col == 127, 0.0, pltpu.roll(x, 127, 0)).astype(BF16)
        shifted[index, :, 0:512] = after if flip else before
        shifted[index, :, 1024:1536] = before if flip else after

    def put_shifted(index, row, flip):
        shifted[index, :, 512:1024] = row
        put_sides(index, row.astype(F32), flip)

    def halo_wait(flip):
        up, down = halo_copies()

        @pl.when(has_up)
        def _():
            up().wait_send()
            down().wait_recv()
            put_shifted(0, halo[0], flip)

        @pl.when(has_down)
        def _():
            down().wait_send()
            up().wait_recv()
            put_shifted(9, halo[1], flip)

    lane = lax.broadcasted_iota(jnp.int32, (128, FULL), 1)
    low = lane < HALF

    def width_out(slot, h, table, get):
        parts = []
        for q in (2 * h, 2 * h + 1):
            x = dot(table[...], get(q))
            both = jnp.concatenate([x[:128], x[128:]], axis=1)
            parts.append(both.reshape(MEMBERS, 8, FULL))
        send[slot, :, pl.ds(pl.multiple_of(16 * h, 16), 16), :] = jnp.concatenate(parts, axis=1).astype(BF16)

    def width_back(slot, h, table):
        block = recv[slot, :, pl.ds(pl.multiple_of(16 * h, 16), 16), :].astype(F32)
        results = []
        for o in range(2):
            z = block[:, 8 * o : 8 * o + 8, :].reshape(128, FULL)
            zi = pltpu.roll(z, HALF, 1)
            stacked = jnp.concatenate([z[:, :HALF], zi[:, :HALF]], axis=0).astype(BF16)
            results.append(dot(table[...], stacked))
        return results

    def rows_forward_into(slot, put):
        x = recv[slot].reshape(512, FULL)
        for f in range(4):
            both = dot(hf[f], x)
            a, b = both[:128], both[128:]
            turned = pltpu.roll(b, HALF, 1)
            if f == 0:
                rest = 1.0 - first
                put(0, jnp.where(low, a + rest * turned, rest * a - turned))
                put(4, jnp.where(low, pltpu.roll(a, HALF, 1), -b) * first)
            else:
                put(f, jnp.where(low, a + turned, a - turned))

    def rows_inverse_from(slot, get):
        last = get(4)
        for f in range(4):
            v = get(f)
            turned = pltpu.roll(v, HALF, 1)
            if f == 0:
                rest = 1.0 - first
                a = jnp.where(low, v, rest * v + first * pltpu.roll(last, HALF, 1))
                b = jnp.where(low, -turned, rest * turned - first * last)
            else:
                a = v
                b = jnp.where(low, -turned, turned)
            vab[f * 128 : (f + 1) * 128, :] = a.astype(BF16)
            vab[512 + f * 128 : 640 + f * 128, :] = b.astype(BF16)

        def go(c, carry):
            z = dot(hi[pl.ds(pl.multiple_of(c * 256, 256), 256), :], vab[...])
            send[slot, pl.ds(c * 8, 8)] = z.astype(BF16).reshape(8, 32, FULL)
            return carry

        lax.fori_loop(0, 2, go, 0)

    def moments(layer, which, lanes, one, two, inv_count):
        count = wide(inv_count, lanes)
        mean = one * count
        var = two * count - mean * mean
        inv = lax.rsqrt(var + EPSILON)
        stats[layer, which : which + 1, 0:lanes] = mean
        stats[layer, 3 + which : 4 + which, 0:lanes] = inv
        stats[layer, 6 + which : 7 + which, 0:lanes] = var
        scale = pars[layer, which : which + 1, 0:lanes] * inv
        shift = pars[layer, 3 + which : 4 + which, 0:lanes] - mean * scale
        return scale, shift

    def affine(layer, which, lanes):
        mean = stats[layer, which : which + 1, 0:lanes]
        inv = stats[layer, 3 + which : 4 + which, 0:lanes]
        gain = pars[layer, which : which + 1, 0:lanes]
        return mean, inv, gain, pars[layer, 3 + which : 4 + which, 0:lanes]

    def keep_grad_sums(layer, which, lanes, one, two):
        stats[layer, 9 + which : 10 + which, 0:lanes] = one
        stats[layer, 12 + which : 13 + which, 0:lanes] = two

    zero_of = lambda lanes: jnp.zeros((8, lanes), F32)

    def conv_pair(layer, c):
        loc = jnp.zeros((256, 512), F32)
        glo = jnp.zeros((256, 128), F32)
        for i in range(3):
            a_loc = jnp.concatenate(
                [shifted[pl.ds(2 * c + i, 2), :, j * 512 : j * 512 + 128].reshape(256, 128) for j in range(3)], axis=1
            )
            a_glo = jnp.concatenate(
                [shifted[pl.ds(2 * c + i, 2), :, j * 512 + 128 : (j + 1) * 512].reshape(256, 384) for j in range(3)],
                axis=1,
            )
            loc = loc + dot(a_loc, w_c[layer, 3 * i : 3 * i + 3].reshape(384, 512))
            glo = glo + dot(a_glo, w_gl[layer, 3 * i : 3 * i + 3].reshape(1152, 128))
        v34[layer, c, :, 0:CL] = loc[:, :CL] + glo
        v34[layer, c, :, CL:] = loc[:, CL:]

    pl.when(stays)(lambda: input_near().wait())
    when_far(lambda: input_far(0).wait())
    pl.when(stays)(lambda: cot_near().start())

    def pixel_rows(r):
        return lax.div(r, 2), pl.ds(pl.multiple_of(lax.rem(r, 2) * 128, 128), 128)

    def mask_global(r, c):
        q, here = pixel_rows(r)
        x = acts[0, r, :, CL:].astype(F32) * wide(pmask[q, here, :], CG)
        acts[0, r, :, CL:] = x.astype(BF16)
        return c

    lax.fori_loop(0, ROWS, mask_global, 0)
    for c in local_w[:3] + remote_w[:3]:
        c.wait()
    for lay in range(LAYERS):
        for base_row, raw in ((0, raw_g), (3, raw_b)):
            row = raw[lay // 2, lay % 2 : lay % 2 + 1, :]
            pars[lay, base_row : base_row + 1, 0:CS] = row[:, :CS]
            pars[lay, base_row + 1 : base_row + 2, 0:FULL] = row[:, CS : 3 * CS]
            pars[lay, base_row + 2 : base_row + 3, :] = row[:, 3 * CS :]

    def start_row(r, c):
        q, here = pixel_rows(r)
        acts[0, r, :, 0:CL] = (acts[0, r, :, 0:CL].astype(F32) * pmask[q, here, :]).astype(BF16)
        return c

    def finish_start():
        when_far(lambda: input_far(1).wait())
        lax.fori_loop(0, ROWS, start_row, 0)
        for c in local_w[3:] + remote_w[3:]:
            c.wait()

    def out_copies(source, target, sems, block, row):
        send_sem, arrive_sem = sems
        far = lambda: pltpu.make_async_remote_copy(
            source.at[row], target.at[grp, row], send_sem.at[block, row], arrive_sem.at[grp, row],
            device_id=(block, me), device_id_type=MESH,
        )
        near = lambda: pltpu.make_async_copy(source.at[row], target.at[grp, row], send_sem.at[block, row])
        return (block == s) & (me == d), far, near

    def y_copies(block, row):
        return out_copies(acts.at[2 * block + 2], out_y, (sem_y_s, sem_y_r), block, row)

    def g_copies(block, row):
        return out_copies(gblk.at[1 - block], out_g, (sem_g_s, sem_g_r), block, row)

    def start_out(made):
        here, far, near = made
        pl.when(here)(lambda: near().start())
        pl.when(jnp.logical_not(here))(lambda: far().start())

    def wait_out(made):
        here, far, near = made
        pl.when(here)(lambda: near().wait())
        pl.when(jnp.logical_not(here))(lambda: far().wait_send())

    def forward_window(layer, window):
        parity = lax.rem(layer, 2)

        @pl.when(layer < 2)
        def _():
            push_rows(parity, window, lambda row: when_far(lambda: cot_far(row).start()))

        @pl.when(layer >= 2)
        def _():
            push_rows(parity, window, lambda row: start_out(y_copies(0, row)))

    def backward_window(step, window):
        parity = lax.rem(step, 2)

        @pl.when(step < 2)
        def _():
            push_rows(parity, window, lambda row: start_out(y_copies(1, row)))

        @pl.when(step >= 2)
        def _():
            push_rows(parity, window, lambda row: start_out(g_copies(1, row)))

    def forward(layer, carry):
        def reduce_pair(q, sums):
            a = acts[layer, pl.ds(2 * q, 2), :, CL:].reshape(256, CG)
            v = dot_nt(a, w_r[layer])
            v1[layer, q] = v
            return sums[0] + fold(v), sums[1] + fold(v * v)

        put_sums(0, *lax.fori_loop(0, PAIRS, reduce_pair, (zero_of(HALF), zero_of(HALF))))
        sums_start(0)
        pl.when(layer == 0)(finish_start)

        def lay_out(r, carry):
            put_shifted(1 + r, acts[layer, r], False)
            return carry

        lax.fori_loop(0, ROWS, lay_out, 0)
        halo_start()
        forward_window(layer, 0)

        def conv_go(c, carry):
            conv_pair(layer, c)
            return carry

        lax.fori_loop(1, 3, conv_go, 0)
        scale, shift = moments(layer, 0, HALF, *sums_wait(0, HALF), inv_n)

        def spectral_in(h, carry):
            def get(q):
                pre = v1[layer, q] * scale + shift
                x = pre * sigmoid(pre) * wide(pmask[q], HALF)
                u[q] = x
                return x.astype(BF16)

            width_out(0, h, tf, get)
            return carry

        lax.fori_loop(0, 2, spectral_in, 0)
        swap_start(0)
        halo_wait(False)
        conv_pair(layer, 0)
        forward_window(layer, 1)
        swap_wait(0)

        def put(f, y):
            spec[layer, f * 128 : (f + 1) * 128, :] = y.astype(BF16)

        rows_forward_into(0, put)

        mixed[layer] = dot(spec[layer], w_m[layer])

        def mix_block(f, sums):
            v = mixed[layer, pl.ds(pl.multiple_of(f * 128, 128), 128), :]
            return sums[0] + fold(v), sums[1] + fold(v * v)

        put_sums(1, *lax.fori_loop(0, 5, mix_block, (zero_of(FULL), zero_of(FULL))))
        sums_start(1)
        forward_window(layer, 2)
        scale2, shift2 = moments(layer, 1, FULL, *sums_wait(1, FULL), inv_ns)

        def get_v(f):
            rows = slice(f * 128, (f + 1) * 128)
            pre = mixed[layer, rows, :] * scale2 + shift2
            return pre * sigmoid(pre) * wide(qmask[rows, :], FULL)

        rows_inverse_from(1, get_v)
        swap_start(1)
        conv_pair(layer, 3)
        forward_window(layer, 3)
        swap_wait(1)

        def spectral_out(h, sums):
            backs = width_back(1, h, tgt)
            one, two = sums
            for o in range(2):
                q = 2 * h + o
                t = (u[q] + backs[o]).astype(BF16)
                tsum[layer, q] = t
                pm = pmask[q]
                v_loc = v34[layer, q, :, 0:CL] * pm
                v_glo = (v34[layer, q, :, CL:] + dot(t, w_e[layer])) * wide(pm, CG)
                v34[layer, q, :, 0:CL] = v_loc
                v34[layer, q, :, CL:] = v_glo
                v = jnp.concatenate([v_loc, v_glo], axis=1)
                one = one + fold(v)
                two = two + fold(v * v)
            return one, two

        put_sums(2, *lax.fori_loop(0, 2, spectral_out, (zero_of(512), zero_of(512))))
        sums_start(2)
        forward_window(layer, 4)
        scale3, shift3 = moments(layer, 2, 512, *sums_wait(2, 512), inv_n)
        odd = lax.rem(layer, 2)
        oddf = odd.astype(F32)

        def next_row(r, carry):
            q = lax.div(r, 2)
            here = pl.ds(pl.multiple_of(lax.rem(r, 2) * 128, 128), 128)
            pre = v34[layer, q, here, :] * scale3 + shift3
            x = pre * sigmoid(pre) * wide(pmask[q, here, :], 512)
            x = x + oddf * acts[layer - odd, r].astype(F32)
            acts[layer + 1, r] = x.astype(BF16)
            return carry

        lax.fori_loop(0, ROWS, next_row, 0)

        return carry

    lax.fori_loop(0, LAYERS, forward, 0)

    pl.when(stays)(lambda: cot_near().wait())

    def cot_wait(row, c):
        when_far(lambda: cot_far(row).wait())
        return c

    lax.fori_loop(0, ROWS, cot_wait, 0)

    def cot_row(r, c):
        q = lax.div(r, 2)
        here = pl.ds(pl.multiple_of(lax.rem(r, 2) * 128, 128), 128)
        x = gblk[1, r].astype(F32) * wide(pmask[q, here, :], 512)
        gblk[1, r] = x.astype(BF16)
        g[q, here, :] = x
        return c

    lax.fori_loop(0, ROWS, cot_row, 0)

    x_bit = lax.rem(d, 2)
    y_bit = lax.rem(lax.div(d, 2), 2)
    at_x = jnp.where(s == 0, x_bit, y_bit)
    at_y = jnp.where(s == 0, y_bit, x_bit)
    step_x = jnp.where(s == 0, 1, 2)
    step_y = 3 - step_x
    in_core = s * 16
    in_x = in_core + at_x * 8
    in_y = in_x + at_y * 4
    near_x = (s, d + step_x * (1 - 2 * at_x))
    near_y = (s, d + step_y * (1 - 2 * at_y))

    def sum_part(p, layer):
        gw, rb, fin, out, rows = ((gwe, rbe, fine, out_we, EARLY), (gwl, rbl, finl, out_wl, LATE))[p]
        block = lax.div(layer, 2)
        odd = lax.rem(layer, 2)
        slot = jnp.where(block == s, 2, 0) + odd

        def remote(stage, source, target, other, n=0):
            return pltpu.make_async_remote_copy(
                source, target, sem_rs.at[p, odd, stage, n], sem_rr.at[p, odd, stage, n], device_id=other, device_id_type=MESH
            )

        def rows_of(first_piece, pieces):
            return pl.ds(pl.multiple_of(first_piece * rows, rows), pieces * rows)

        one = lambda: remote(0, gw.at[rows_of((1 - s) * 16, 16)], rb.at[rows_of(0, 16)], partner)
        far_x = in_core + (1 - at_x) * 8

        def two(n):
            first_four = (1 - at_y) * 4 if n == 0 else at_y * 4
            return remote(1, gw.at[rows_of(far_x + first_four, 4)], rb.at[rows_of(16 + first_four, 4)], near_x, n)

        three = lambda: remote(2, gw.at[rows_of(in_x + (1 - at_y) * 4, 4)], rb.at[rows_of(24, 4)], near_y)

        def add(first_piece, from_piece, pieces):
            def go(i, carry):
                here = rows_of(first_piece + i, 1)
                there = rows_of(from_piece + i, 1)
                gw[here, :] = (gw[here, :].astype(F32) + rb[there, :].astype(F32)).astype(BF16)
                return carry

            lax.fori_loop(0, pieces, go, 0)

        def along_z(i):
            other = lax.rem(at_z + 1 + i, 4)
            return other, (s, d + 4 * (other - at_z))

        def four(i, arriving):
            other, device = along_z(i)
            return pltpu.make_async_remote_copy(
                gw.at[rows_of(in_y + other, 1)],
                rb.at[rows_of(28 + (other if arriving else at_z), 1)],
                sem_rs.at[p, odd, 3, i], sem_rr.at[p, odd, 3, other if arriving else at_z],
                device_id=device, device_id_type=MESH,
            )

        def five(i, arriving):
            other, device = along_z(i)
            return pltpu.make_async_remote_copy(
                fin, out.at[slot, rows_of(in_y + (other if arriving else at_z), 1)],
                sem_rs.at[p, odd, 4, i], sem_rr.at[p, odd, 4, other if arriving else at_z],
                device_id=device, device_id_type=MESH,
            )

        five_own = lambda: pltpu.make_async_copy(fin, out.at[slot, rows_of(in_y + at_z, 1)], sem_rs.at[p, odd, 4, 3])

        def spread_copy(stage, first_piece, other, n=0):
            here = out.at[slot, rows_of(first_piece, 4)]
            return remote(stage, here, here, other, n)

        six = lambda: spread_copy(5, in_y, near_y)
        seven = lambda n: spread_copy(6, in_y if n == 0 else in_x + (1 - at_y) * 4, near_x, n)
        eight = lambda: remote(
            7, out.at[odd, rows_of(in_core, 16)],
            out.at[2 + odd, rows_of(in_core, 16)], partner,
        )
        starts = s != block

        def begin_one():
            one().start()

        def begin_two():
            one().wait()
            add(in_core, 0, 16)
            two(0).start()
            two(1).start()

        def begin_three():
            two(0).wait()
            two(1).wait()
            add(in_x, 16, 8)
            three().start()

        def begin_four():
            three().wait()
            add(in_y, 24, 4)
            for i in range(3):
                four(i, False).start()

        def begin_five():
            total_now = gw[rows_of(in_y + at_z, 1), :].astype(F32)
            for i in range(3):
                four(i, False).wait_send()
                four(i, True).wait_recv()
                total_now = total_now + rb[rows_of(28 + lax.rem(at_z + 1 + i, 4), 1), :].astype(F32)
            fin[...] = total_now.astype(BF16)
            five_own().start()
            for i in range(3):
                five(i, False).start()

        def begin_six(quick):
            five_own().wait()
            for i in range(3):
                five(i, False).wait_send()
                five(i, True).wait_recv()
            six().start()
            if quick:
                seven(0).start()

        def begin_seven(quick):
            six().wait()
            if not quick:
                seven(0).start()
            seven(1).start()

        def begin_eight():
            seven(0).wait()
            seven(1).wait()
            pl.when(starts)(lambda: eight().start())

        def end():
            pl.when(starts)(lambda: eight().wait_send())
            pl.when(jnp.logical_not(starts))(lambda: eight().wait_recv())

        return (
            begin_one, begin_two, begin_three, begin_four, begin_five,
            lambda: begin_six(False), lambda: begin_seven(False), begin_eight, end,
            lambda: begin_six(True), lambda: begin_seven(True),
        )

    QUICK_SIX, QUICK_SEVEN = 9, 10

    def stage(p, layer, which):
        pl.when(layer < LAYERS)(lambda: sum_part(p, layer)[which]())

    def backward(step, carry):
        layer = LAYERS - 1 - step
        mean3, inv3, gain3, bias3 = affine(layer, 2, 512)
        scale3 = gain3 * inv3
        shift3 = bias3 - mean3 * scale3

        def slope_row(r, sums):
            q = lax.div(r, 2)
            here = pl.ds(pl.multiple_of(lax.rem(r, 2) * 128, 128), 128)
            v = v34[layer, q, here, :]
            pre = v * scale3 + shift3
            sg = sigmoid(pre)
            e = g[q, here, :] * wide(pmask[q, here, :], 512) * (sg * (1.0 + pre * (1.0 - sg)))
            g[q, here, :] = e
            return sums[0] + fold(e), sums[1] + fold(e * ((v - mean3) * inv3))

        put_sums(3, *lax.fori_loop(0, ROWS, slope_row, (zero_of(512), zero_of(512))))
        sums_start(3)
        backward_window(step, 0)

        def turn_row(r, carry):
            at[:, pl.ds(pl.multiple_of(r * 128, 128), 128)] = jnp.transpose(acts[layer, r])
            return carry

        stage(0, layer + 1, 3)
        stage(0, layer + 2, 6)
        stage(1, layer + 1, 1)
        stage(1, layer + 2, QUICK_SEVEN)
        lax.fori_loop(0, ROWS, turn_row, 0)
        one3, two3 = sums_wait(3, 512)
        keep_grad_sums(layer, 2, 512, one3, two3)
        part_a = one3 * wide(inv_n, 512)
        part_b = two3 * wide(inv_n, 512)

        def d_row(r, carry):
            q = lax.div(r, 2)
            here = pl.ds(pl.multiple_of(lax.rem(r, 2) * 128, 128), 128)
            z = (v34[layer, q, here, :] - mean3) * inv3
            dv = wide(pmask[q, here, :], 512) * scale3 * (g[q, here, :] - part_a - z * part_b)
            shifted[1 + r, :, 512:1024] = dv.astype(BF16)
            return carry

        lax.fori_loop(0, ROWS, d_row, 0)
        halo_start()

        def grad_out(h, carry):
            def get(q):
                dg = shifted[pl.ds(1 + 2 * q, 2), :, 512 + CL : 1024].reshape(256, CG)
                dt = dot_nt(dg, w_e[layer])
                u[q] = dt
                return dt.astype(BF16)

            width_out(0, h, tg, get)
            return carry

        lax.fori_loop(0, 2, grad_out, 0)
        swap_start(0)

        def lay_sides(r, carry):
            put_sides(1 + r, shifted[1 + r, :, 512:1024].astype(F32), True)
            return carry

        lax.fori_loop(0, ROWS, lay_sides, 0)
        halo_wait(True)

        def conv_back(c, carry):
            d_loc = jnp.zeros((256, 128), F32)
            d_glo = jnp.zeros((256, 384), F32)
            for i in range(3):
                for j in range(3):
                    rows = pl.ds(2 * c + 2 - i, 2)
                    dd = shifted[rows, :, j * 512 : (j + 1) * 512].reshape(256, 512)
                    d_loc = d_loc + dot_nt(dd, w_c[layer, 3 * i + j])
                    d_glo = d_glo + dot_nt(dd[:, :CL], w_gl[layer, 3 * i + j])
            g[c, :, 0:CL] = d_loc
            g[c, :, CL:] = d_glo
            return carry

        def block_rows(i, lanes):
            return jnp.concatenate(
                [
                    shifted[2 - i : 10 - i, :, j * 512 + lanes[0] : j * 512 + lanes[1]].reshape(1024, lanes[1] - lanes[0])
                    for j in range(3)
                ],
                axis=1,
            )

        def lift_grad(i):
            acc = dot(at[0:CL, :], block_rows(i, (CL, 512)))
            for j in range(3):
                for n in range(3):
                    base = AT_KG + n * 1152 + (3 * i + j) * 128
                    gwe[base : base + 128, :] = acc[:, (3 * j + n) * 128 : (3 * j + n + 1) * 128].astype(BF16)

        def local_grad(i):
            acc = dot(at[...], block_rows(i, (0, CL)))
            for j in range(3):
                tap = 3 * i + j
                block = acc[:, j * 128 : (j + 1) * 128].astype(BF16)
                gwe[AT_LL + tap * CL : AT_LL + (tap + 1) * CL, :] = block[:CL]
                gwe[AT_GL + tap * CG : AT_GL + (tap + 1) * CG, :] = block[CL:]

        stage(1, layer + 2, 7)
        stage(1, layer + 1, 2)
        backward_window(step, 1)
        stage(0, layer + 1, 4)
        for i in range(3):
            local_grad(i)
        for i in range(3):
            lift_grad(i)
        acc_e = jnp.zeros((HALF, CG), F32)
        for q in range(PAIRS):
            dg = shifted[1 + 2 * q : 3 + 2 * q, :, 512 + CL : 1024].reshape(256, CG)
            acc_e = acc_e + dot_tn(tsum[layer, q], dg)
        for n in range(3):
            gwe[AT_E + n * HALF : AT_E + (n + 1) * HALF, :] = acc_e[:, n * 128 : (n + 1) * 128].astype(BF16)
        stage(0, layer, 0)
        swap_wait(0)

        def put(f, y):
            e2[f * 128 : (f + 1) * 128, :] = y

        rows_forward_into(0, put)
        mean2, inv2, gain2, bias2 = affine(layer, 1, FULL)
        scale2 = gain2 * inv2
        shift2 = bias2 - mean2 * scale2

        def slope_block(f, sums):
            rows = pl.ds(pl.multiple_of(f * 128, 128), 128)
            v = mixed[layer, rows, :]
            pre = v * scale2 + shift2
            sg = sigmoid(pre)
            e = e2[rows, :] * wide(qmask[rows, :], FULL) * (sg * (1.0 + pre * (1.0 - sg)))
            e2[rows, :] = e
            return sums[0] + fold(e), sums[1] + fold(e * ((v - mean2) * inv2))

        put_sums(1, *lax.fori_loop(0, 5, slope_block, (zero_of(FULL), zero_of(FULL))))
        sums_start(1)
        backward_window(step, 2)
        stage(1, layer + 2, 8)
        stage(1, layer + 1, 3)
        conv_back(0, 0)
        stage(0, layer, 1)
        stage(0, layer + 2, 7)
        conv_back(1, 0)
        one2, two2 = sums_wait(1, FULL)
        keep_grad_sums(layer, 1, FULL, one2, two2)
        part_a2 = one2 * wide(inv_ns, FULL)
        part_b2 = two2 * wide(inv_ns, FULL)

        def dq_block(f, carry):
            rows = pl.ds(pl.multiple_of(f * 128, 128), 128)
            z = (mixed[layer, rows, :] - mean2) * inv2
            dv = wide(qmask[rows, :], FULL) * scale2 * (e2[rows, :] - part_a2 - z * part_b2)
            dq[rows, :] = dv.astype(BF16)
            return carry

        lax.fori_loop(0, 5, dq_block, 0)
        e2[...] = dot_nt(dq[...], w_m[layer])
        rows_inverse_from(1, lambda f: e2[f * 128 : (f + 1) * 128, :])
        swap_start(1)
        conv_back(2, 0)
        stage(1, layer + 1, 4)
        backward_window(step, 3)
        conv_back(3, 0)
        pl.when(layer == 0)(lambda: stage(0, 0, 2))
        swap_wait(1)

        mean1, inv1, gain1, bias1 = affine(layer, 0, HALF)
        scale1 = gain1 * inv1
        shift1 = bias1 - mean1 * scale1

        def slope_in(h, sums):
            backs = width_back(1, h, tft)
            one, two = sums
            for o in range(2):
                q = 2 * h + o
                v = v1[layer, q]
                pre = v * scale1 + shift1
                sg = sigmoid(pre)
                e = (u[q] + backs[o]) * wide(pmask[q], HALF) * (sg * (1.0 + pre * (1.0 - sg)))
                u[q] = e
                one = one + fold(e)
                two = two + fold(e * ((v - mean1) * inv1))
            return one, two

        put_sums(0, *lax.fori_loop(0, 2, slope_in, (zero_of(HALF), zero_of(HALF))))
        sums_start(0)
        backward_window(step, 4)
        pl.when(layer > 0)(lambda: stage(0, layer, 2))
        pl.when(layer == 0)(lambda: stage(0, 0, 3))
        stage(0, layer + 1, 5)
        stage(0, layer + 2, 8)
        stage(1, layer + 1, QUICK_SIX)
        acc_m = jnp.zeros((FULL, FULL), F32)
        for f in range(5):
            rows = slice(f * 128, (f + 1) * 128)
            acc_m = acc_m + dot_tn(spec[layer, rows, :], dq[rows, :])
        for n in range(3):
            gwl[AT_M + n * FULL : AT_M + (n + 1) * FULL, :] = acc_m[:, n * 128 : (n + 1) * 128].astype(BF16)
        one1, two1 = sums_wait(0, HALF)
        keep_grad_sums(layer, 0, HALF, one1, two1)
        part_a1 = one1 * wide(inv_n, HALF)
        part_b1 = two1 * wide(inv_n, HALF)

        def ds_pair(q, carry):
            z = (v1[layer, q] - mean1) * inv1
            dv = wide(pmask[q], HALF) * scale1 * (u[q] - part_a1 - z * part_b1)
            low_dv = dv.astype(BF16)
            ds[q] = low_dv
            g[q, :, CL:] = g[q, :, CL:] + dot(low_dv, w_r[layer])
            return carry

        lax.fori_loop(0, PAIRS, ds_pair, 0)
        acc_r = jnp.zeros((HALF, CG), F32)
        for q in range(PAIRS):
            a = acts[layer, 2 * q : 2 * q + 2, :, CL:].reshape(256, CG)
            acc_r = acc_r + dot_tn(ds[q], a)
        for n in range(3):
            gwl[AT_R + n * HALF : AT_R + (n + 1) * HALF, :] = acc_r[:, n * 128 : (n + 1) * 128].astype(BF16)


        stage(1, layer, 0)

        @pl.when(lax.rem(layer, 2) == 0)
        def _():
            block = lax.div(layer, 2)

            def close_row(r, carry):
                q = lax.div(r, 2)
                here = pl.ds(pl.multiple_of(lax.rem(r, 2) * 128, 128), 128)
                x = (gblk[block, r].astype(F32) + g[q, here, :]) * wide(pmask[q, here, :], 512)
                low_x = x.astype(BF16)
                gblk[1 - block, r] = low_x
                g[q, here, :] = low_x.astype(F32)

                return carry

            lax.fori_loop(0, ROWS, close_row, 0)

        return carry

    lax.fori_loop(0, LAYERS, backward, 0)

    far = pltpu.make_async_remote_copy(
        stats.at[own], stats_far, sem_st.at[0], sem_st.at[1],
        device_id=across, device_id_type=MESH,
    )
    far.start()

    def push_last(first_row, rows):
        for row in range(first_row, first_row + rows):
            start_out(g_copies(0, row))

    stage(0, 0, 4)
    stage(1, 1, QUICK_SEVEN)
    push_last(0, 1)
    stage(1, 0, 1)
    stage(1, 0, 2)
    stage(1, 1, 7)
    stage(0, 1, 6)
    stage(1, 0, 3)
    push_last(1, 2)
    stage(0, 0, QUICK_SIX)
    stage(1, 0, 4)
    push_last(3, 5)
    stage(1, 1, 8)
    stage(0, 1, 7)
    stage(1, 0, QUICK_SIX)
    stage(0, 0, QUICK_SEVEN)
    stage(1, 0, QUICK_SEVEN)
    stage(0, 1, 8)
    stage(0, 0, 7)
    stage(1, 0, 7)
    stage(0, 0, 8)
    stage(1, 0, 8)
    for block in range(2):
        def sent(row, carry, block=block):
            wait_out(y_copies(block, row))
            wait_out(g_copies(block, row))
            return carry

        lax.fori_loop(0, ROWS, sent, 0)
    for m in range(2):
        sender = member(m, d)
        from_self = (sender[0] == s) & (sender[1] == d)

        def arrived(row, carry, m=m):
            for source, target, sems in ((acts, out_y, (sem_y_s, sem_y_r)), (gblk, out_g, (sem_g_s, sem_g_r))):
                pltpu.make_async_remote_copy(
                    source.at[0, row], target.at[m, row], sems[0].at[0, row], sems[1].at[m, row],
                    device_id=partner, device_id_type=MESH,
                ).wait_recv()
            return carry

        @pl.when(jnp.logical_not(from_self))
        def _(arrived=arrived):
            lax.fori_loop(0, ROWS, arrived, 0)

    far.wait()
    for lay in range(2):
        mine = stats[2 * s + lay]
        other = stats_far[lay]
        zero_first = jnp.where(grp == 0, mine, other)
        one_next = jnp.where(grp == 0, other, mine)
        row = slice(lay, lay + 1)

        def joined(st, base):
            return jnp.concatenate(
                [st[base : base + 1, :HALF], st[base + 1 : base + 2, :FULL], st[base + 2 : base + 3]], axis=1
            )

        mean = run_m[row, :]
        var = run_v[row, :]
        for m, st in enumerate((zero_first, one_next)):
            pixels = shapes[m, 0] * shapes[m, 1]
            points = shapes[m, 0] * (lax.div(shapes[m, 1], 2) + 1)
            fix = [
                wide(jnp.full((1, 128), count.astype(F32)) * inverse(count, 1), lanes)
                for count, lanes in ((pixels, HALF), (points, FULL), (pixels, 512))
            ]
            mean = (1.0 - MOMENTUM) * mean + MOMENTUM * joined(st, 0)
            var = (1.0 - MOMENTUM) * var + MOMENTUM * joined(st, 6) * jnp.concatenate(fix, axis=1)
        out_m[row, :] = mean
        out_v[row, :] = var
        out_biases[row, :] = joined(zero_first, 9) + joined(one_next, 9)
        out_gains[row, :] = joined(zero_first, 12) + joined(one_next, 12)


def tiles_of(rows, array):
    return jnp.concatenate([array[:, n * rows : (n + 1) * rows].astype(F32) for n in range(3)], axis=-1)


def on_band(
    inputs,
    cotangent,
    shapes,
    local_to_local,
    global_to_local,
    local_to_global,
    spec_reduce,
    spec_mix,
    spec_expand,
    norm_gains,
    norm_biases,
    run_means,
    run_vars,
):
    anywhere = pl.BlockSpec(memory_space=pl.ANY)
    vmem = pl.BlockSpec(memory_space=pltpu.VMEM)
    dma = pltpu.SemaphoreType.DMA
    band = (ROWS, LONG, 512)
    out_y, out_g, out_we, out_wl, *out_norms = pl.pallas_call(
        network_kernel,
        out_shape=(
            jax.ShapeDtypeStruct((2,) + band, BF16),
            jax.ShapeDtypeStruct((2,) + band, BF16),
            jax.ShapeDtypeStruct((4, PIECES * EARLY, 128), BF16),
            jax.ShapeDtypeStruct((4, PIECES * LATE, 128), BF16),
            *[jax.ShapeDtypeStruct((2, 3 * CS + 512), F32)] * 4,
        ),
        in_specs=[anywhere, anywhere, pl.BlockSpec(memory_space=pltpu.SMEM)]
        + [anywhere] * 8
        + [vmem] * 2,
        out_specs=(anywhere,) * 4 + (vmem,) * 4,
        scratch_shapes=[
            pltpu.VMEM((LAYERS, 9, CL, 512), BF16),
            pltpu.VMEM((LAYERS, 9, CG, CL), BF16),
            pltpu.VMEM((LAYERS, CS, CG), BF16),
            pltpu.VMEM((LAYERS, FULL, FULL), BF16),
            pltpu.VMEM((LAYERS, CS, CG), BF16),
            pltpu.VMEM((2, 2, 3 * CS + 512), F32),
            pltpu.VMEM((2, 2, 3 * CS + 512), F32),
            pltpu.VMEM((LAYERS, 8, 512), F32),
            pltpu.VMEM((LAYERS + 1,) + band, BF16),
            pltpu.VMEM((ROWS + 2, LONG, 1536), BF16),
            pltpu.VMEM((2, LONG, 512), BF16),
            pltpu.VMEM((LAYERS, PAIRS, 256, CS), F32),
            pltpu.VMEM((PAIRS, 256, CS), F32),
            pltpu.VMEM((LAYERS, SLOTS, FULL), BF16),
            pltpu.VMEM((LAYERS, SLOTS, FULL), F32),
            pltpu.VMEM((LAYERS, PAIRS, 256, CS), BF16),
            pltpu.VMEM((LAYERS, PAIRS, 256, 512), F32),
            pltpu.VMEM((PAIRS, 256, 128), F32),
            pltpu.VMEM((SLOTS, 128), F32),
            pltpu.VMEM((256, 256), BF16),
            pltpu.VMEM((256, 256), BF16),
            pltpu.VMEM((256, 256), BF16),
            pltpu.VMEM((256, 256), BF16),
            pltpu.VMEM((4, 256, 512), BF16),
            pltpu.VMEM((512, 1024), BF16),
            pltpu.VMEM((1024, FULL), BF16),
            pltpu.VMEM((SLOTS, FULL), F32),
            pltpu.VMEM((SLOTS, FULL), BF16),
            pltpu.VMEM((PAIRS, 256, CS), BF16),
            pltpu.VMEM((PAIRS, 256, 512), F32),
            pltpu.VMEM((2,) + band, BF16),
            pltpu.VMEM((512, ROWS * LONG), BF16),
            pltpu.VMEM((PIECES * EARLY, 128), BF16),
            pltpu.VMEM((PIECES * LATE, 128), BF16),
            pltpu.VMEM((PIECES * EARLY, 128), BF16),
            pltpu.VMEM((PIECES * LATE, 128), BF16),
            pltpu.VMEM((EARLY, 128), BF16),
            pltpu.VMEM((LATE, 128), BF16),
            pltpu.VMEM((4, 8, 128), F32),
            pltpu.VMEM((4, MEMBERS, 8, 128), F32),
            pltpu.VMEM((2, MEMBERS, 32, FULL), BF16),
            pltpu.VMEM((2, MEMBERS, 32, FULL), BF16),
            pltpu.VMEM((LAYERS, 16, 512), F32),
            pltpu.VMEM((2, 16, 512), F32),
            dma((3, 8)),
            dma((2, 2)),
            dma((ROWS, 2)),
            dma((2,)),
            dma((2,)),
            dma((4, MEMBERS)),
            dma((4, MEMBERS)),
            dma((2, MEMBERS)),
            dma((2, MEMBERS)),
            dma((2, ROWS)),
            dma((2, ROWS)),
            dma((2, ROWS)),
            dma((2, ROWS)),
            dma((2, 2, 8, 4)),
            dma((2, 2, 8, 4)),
            dma((2,)),
        ],
        compiler_params=pltpu.CompilerParams(
            collective_id=0, has_side_effects=True, vmem_limit_bytes=63 << 20
        ),
        name="network",
    )(
        inputs[:, 0],
        cotangent[:, 0],
        shapes,
        local_to_local[0],
        global_to_local[0],
        local_to_global[0],
        jnp.swapaxes(spec_reduce[0], 1, 2),
        spec_mix[0],
        spec_expand[0],
        norm_gains[0],
        norm_biases[0],
        run_means[0],
        run_vars[0],
    )
    grad_ll = out_we[2:, AT_LL:AT_GL].astype(F32).reshape(2, 9, CL, CL)
    grad_gl = out_we[2:, AT_GL:AT_KG].astype(F32).reshape(2, 9, CG, CL)
    grad_lift = tiles_of(9 * CL, out_we[2:, AT_KG:AT_E]).reshape(2, 9, CL, CG)
    grad_expand = tiles_of(CS, out_we[2:, AT_E:])
    grad_mix = tiles_of(FULL, out_wl[2:, AT_M:])
    grad_reduce = jnp.swapaxes(tiles_of(CS, out_wl[2:, AT_R:]), 1, 2)
    out_gains, out_biases, out_means, out_vars = out_norms
    return (
        out_y[None, :, None],
        out_g.astype(F32)[None, :, None],
        grad_ll[None],
        grad_gl[None],
        grad_lift[None],
        grad_reduce[None],
        grad_mix[None],
        grad_expand[None],
        out_gains[None],
        out_biases[None],
        out_means[None],
        out_vars[None],
    )


def solution(mesh):
    in_specs = (
        P(None, None, "dp", None, None),
        P(None, None, "dp", None, None),
        P(),
        P("section", None, None, None, None),
        P("section", None, None, None, None),
        P("section", None, None, None, None),
        P("section", None, None, None),
        P("section", None, None, None),
        P("section", None, None, None),
        P("section", None, None),
        P("section", None, None),
        P("section", None, None),
        P("section", None, None),
    )
    out_specs = (
        P("section", None, None, "dp", None, None),
        P("section", None, None, "dp", None, None),
        P("section", None, None, None, None),
        P("section", None, None, None, None),
        P("section", None, None, None, None),
        P("section", None, None, None),
        P("section", None, None, None),
        P("section", None, None, None),
        P("section", None, None),
        P("section", None, None),
        P("section", None, None),
        P("section", None, None),
    )
    dp_size = mesh.shape["dp"]
    banded = dp_size == MEMBERS and LONG == dp_size * ROWS
    return jax.shard_map(
        on_band if banded else on_device, mesh=mesh, in_specs=in_specs, out_specs=out_specs, check_vma=False
    )
```

```python
import jax
import jax.numpy as jnp
from jax import lax
from jax.experimental import pallas as pl
from jax.experimental.pallas import tpu as pltpu
from jax.sharding import PartitionSpec as P

CL = 128
CG = 384
CS = 192
LONG = 128


EPSILON = 1e-05
MOMENTUM = 0.1
PRECISE = lax.Precision.HIGHEST


def with_halo(block, sides, width):
    for axis, dim in sides:
        count = lax.axis_size(axis)
        forward = [(i, i + 1) for i in range(count - 1)]
        backward = [(target, source) for source, target in forward]
        low = lax.ppermute(
            lax.slice_in_dim(block, block.shape[dim] - width, None, axis=dim), axis, forward
        )
        high = lax.ppermute(lax.slice_in_dim(block, 0, width, axis=dim), axis, backward)
        block = jnp.concatenate([low, block, high], axis=dim)
    return block


def from_behind(value, axis, steps):
    count = lax.axis_size(axis)
    first, last = (max(0, -steps), min(count, count - steps))
    return lax.ppermute(value, axis, [(source, source + steps) for source in range(first, last)])


def dft_tables(height, width, long_side, freq_total):
    position = jnp.arange(long_side, dtype=jnp.int32)
    frequency = jnp.arange(freq_total, dtype=jnp.int32)
    half_width = width // 2
    width_real = width.astype(jnp.float32)
    height_real = height.astype(jnp.float32)
    width_phase = position[:, None] * frequency[None, :] % width
    width_angle = 2.0 * jnp.pi / width_real * width_phase.astype(jnp.float32)
    width_valid = ((position[:, None] < width) & (frequency[None, :] <= half_width)).astype(
        jnp.float32
    )
    width_scale = lax.rsqrt(width_real)
    fwd_cos = jnp.cos(width_angle) * width_scale * width_valid
    fwd_sin = -jnp.sin(width_angle) * width_scale * width_valid
    edge_freq = (frequency == 0) | (frequency == half_width)
    freq_weight = jnp.where(edge_freq, 1.0, 2.0).astype(jnp.float32)
    inv_cos = freq_weight[:, None] * fwd_cos.T
    inv_sin = freq_weight[:, None] * fwd_sin.T
    height_phase = position[:, None] * position[None, :] % height
    height_angle = 2.0 * jnp.pi / height_real * height_phase.astype(jnp.float32)
    height_valid = ((position[:, None] < height) & (position[None, :] < height)).astype(jnp.float32)
    height_scale = lax.rsqrt(height_real)
    row_cos = jnp.cos(height_angle) * height_scale * height_valid
    row_sin = jnp.sin(height_angle) * height_scale * height_valid
    return (fwd_cos, fwd_sin, inv_cos, inv_sin, row_cos, row_sin)


def geometry(shape_row, band_index, band_size, freq_total, freq_local, map_count):
    height = shape_row[0]
    width = shape_row[1]
    position = jnp.arange(LONG, dtype=jnp.int32)
    band_rows = band_index * band_size + jnp.arange(band_size, dtype=jnp.int32)
    pix_mask = ((band_rows[:, None] < height) & (position[None, :] < width)).astype(jnp.float32)[
        None, :, :, None
    ]
    local_freq = band_index * freq_local + jnp.arange(freq_local, dtype=jnp.int32)
    freq_mask = ((position[:, None] < height) & (local_freq[None, :] <= width // 2)).astype(
        jnp.float32
    )[None, :, :, None]
    pix_count = (map_count * height * width).astype(jnp.float32)
    spec_count = (map_count * height * (width // 2 + 1)).astype(jnp.float32)
    return (pix_mask, freq_mask, pix_count, spec_count, dft_tables(height, width, LONG, freq_total))


def conv_rows(padded, kernel):
    shaped = kernel.reshape(3, 3, kernel.shape[1], kernel.shape[2])
    return lax.conv_general_dilated(
        padded,
        shaped,
        (1, 1),
        "VALID",
        dimension_numbers=("NHWC", "HWIO", "NHWC"),
        preferred_element_type=jnp.float32,
    )


def flipped(kernel):
    shaped = kernel.reshape(3, 3, kernel.shape[1], kernel.shape[2])[::-1, ::-1]
    return jnp.swapaxes(shaped, 2, 3).reshape(9, kernel.shape[2], kernel.shape[1])


def kernel_grad(padded, grad_out, band_size, width):
    tap_grads = []
    for row_tap in range(3):
        for col_tap in range(3):
            window = padded[:, row_tap : row_tap + band_size, col_tap : col_tap + width, :]
            tap_grads.append(
                jnp.einsum("mrwi,mrwo->io", window, grad_out, preferred_element_type=jnp.float32)
            )
    return jnp.stack(tap_grads)


def width_forward(entry, table):
    return jnp.einsum("mrwc,wf->mrfc", entry, table, precision=PRECISE)


def width_forward_adj(entry, table):
    return jnp.einsum("mrfc,wf->mrwc", entry, table, precision=PRECISE)


def width_inverse(entry, table):
    return jnp.einsum("mrfc,fw->mrwc", entry, table, precision=PRECISE)


def width_inverse_adj(entry, table):
    return jnp.einsum("mrwc,fw->mrfc", entry, table, precision=PRECISE)


def height_apply(table, entry):
    return jnp.einsum("kn,mnfc->mkfc", table, entry, precision=PRECISE)


def height_adjoint(table, entry):
    return jnp.einsum("kn,mkfc->mnfc", table, entry, precision=PRECISE)


def rows_forward(row_cos, row_sin, entry):
    half_ch = entry.shape[-1] // 2
    real_in = entry[..., :half_ch]
    imag_in = entry[..., half_ch:]
    real_out = height_apply(row_cos, real_in) + height_apply(row_sin, imag_in)
    imag_out = height_apply(row_cos, imag_in) - height_apply(row_sin, real_in)
    return jnp.concatenate([real_out, imag_out], axis=-1)


def rows_inverse(row_cos, row_sin, entry):
    half_ch = entry.shape[-1] // 2
    real_in = entry[..., :half_ch]
    imag_in = entry[..., half_ch:]
    real_out = height_adjoint(row_cos, real_in) - height_adjoint(row_sin, imag_in)
    imag_out = height_adjoint(row_cos, imag_in) + height_adjoint(row_sin, real_in)
    return jnp.concatenate([real_out, imag_out], axis=-1)


def split_pairs(totals, widths):
    pairs = []
    offset = 0
    for lead_width, tail_width in zip(widths[0::2], widths[1::2]):
        lead_part = totals[offset : offset + lead_width]
        tail_part = totals[offset + lead_width : offset + lead_width + tail_width]
        pairs.append((lead_part, tail_part))
        offset = offset + lead_width + tail_width
    return pairs


def moments(entries, weights):
    pieces = []
    for entry, weight in zip(entries, weights):
        masked = entry * weight
        pieces.append(jnp.sum(masked, axis=(0, 1, 2)))
        pieces.append(jnp.sum(masked * entry, axis=(0, 1, 2)))
    totals = lax.psum(jnp.concatenate(pieces), "dp")
    return split_pairs(totals, [piece.shape[0] for piece in pieces])


def grad_moments(grads_in, normed_in):
    pieces = []
    for grad_pre, normed in zip(grads_in, normed_in):
        pieces.append(jnp.sum(grad_pre, axis=(0, 1, 2)))
        pieces.append(jnp.sum(grad_pre * normed, axis=(0, 1, 2)))
    totals = lax.psum(jnp.concatenate(pieces), "dp")
    return split_pairs(totals, [piece.shape[0] for piece in pieces])


def normalize(entry, sum_pair, count_now):
    mean_val = sum_pair[0] / count_now
    var_val = sum_pair[1] / count_now - mean_val * mean_val
    inv_std = lax.rsqrt(var_val + EPSILON)
    return ((entry - mean_val) * inv_std, inv_std, mean_val, var_val)


def silu_slope(pre_act):
    sigmoid_val = jax.nn.sigmoid(pre_act)
    return sigmoid_val * (1.0 + pre_act * (1.0 - sigmoid_val))


def norm_backward(grad_pre, normed, inv_std, gain_part, sum_pair, count_now, weight):
    return (
        weight
        * inv_std
        * gain_part
        * (grad_pre - sum_pair[0] / count_now - normed * sum_pair[1] / count_now)
    )


def layer_forward(layer_in, geometry_now, kernels, gain_vec, bias_vec):
    pix_mask, freq_mask, pix_count, spec_count, tables = geometry_now
    fwd_cos, fwd_sin, inv_cos, inv_sin, row_cos, row_sin = tables
    local_kernel, lift_kernel, reduce_kernel, mix_kernel, expand_kernel = kernels
    acts_low = layer_in.astype(jnp.bfloat16)
    padded = with_halo(acts_low, (("dp", 1),), 1)
    padded = jnp.pad(padded, ((0, 0), (0, 0), (1, 1), (0, 0)))
    local_out = conv_rows(padded, local_kernel)
    global_conv = conv_rows(padded[..., :CL], lift_kernel)
    reduced = jnp.einsum(
        "mrwc,cd->mrwd", acts_low[..., CL:], reduce_kernel, preferred_element_type=jnp.float32
    )
    one_stats = moments([reduced], [pix_mask])[0]
    normed_one, inv_one, mean_one, var_one = normalize(reduced, one_stats, pix_count)
    pre_one = normed_one * gain_vec[:CS] + bias_vec[:CS]
    upper_spec = jax.nn.silu(pre_one) * pix_mask
    spectrum = jnp.concatenate(
        [width_forward(upper_spec, fwd_cos), width_forward(upper_spec, fwd_sin)], axis=-1
    ).astype(jnp.bfloat16)
    columns = lax.all_to_all(spectrum, "dp", split_axis=2, concat_axis=1, tiled=True).astype(
        jnp.float32
    )
    spectra = rows_forward(row_cos, row_sin, columns).astype(jnp.bfloat16)
    mixed = jnp.einsum("mkfc,cd->mkfd", spectra, mix_kernel, preferred_element_type=jnp.float32)
    two_stats = moments([mixed], [freq_mask])[0]
    normed_two, inv_two, mean_two, var_two = normalize(mixed, two_stats, spec_count)
    pre_two = normed_two * gain_vec[CS : 3 * CS] + bias_vec[CS : 3 * CS]
    activated = jax.nn.silu(pre_two) * freq_mask
    inverse = rows_inverse(row_cos, row_sin, activated).astype(jnp.bfloat16)
    returned = lax.all_to_all(inverse, "dp", split_axis=1, concat_axis=2, tiled=True).astype(
        jnp.float32
    )
    half_ch = returned.shape[-1] // 2
    restored = width_inverse(returned[..., :half_ch], inv_cos) + width_inverse(
        returned[..., half_ch:], inv_sin
    )
    summed = (upper_spec + restored).astype(jnp.bfloat16)
    spec_out = jnp.einsum(
        "mrwc,cd->mrwd", summed, expand_kernel, preferred_element_type=jnp.float32
    )
    global_out = global_conv + spec_out
    loc_stats, glo_stats = moments([local_out, global_out], [pix_mask, pix_mask])
    normed_loc, inv_loc, mean_loc, var_loc = normalize(local_out, loc_stats, pix_count)
    normed_glo, inv_glo, mean_glo, var_glo = normalize(global_out, glo_stats, pix_count)
    pre_loc = normed_loc * gain_vec[3 * CS : 3 * CS + CL] + bias_vec[3 * CS : 3 * CS + CL]
    pre_glo = normed_glo * gain_vec[3 * CS + CL :] + bias_vec[3 * CS + CL :]
    result = jnp.concatenate([jax.nn.silu(pre_loc), jax.nn.silu(pre_glo)], axis=-1) * pix_mask
    stored = (
        padded,
        pre_one,
        normed_one,
        inv_one,
        spectra,
        pre_two,
        normed_two,
        inv_two,
        summed,
        pre_loc,
        normed_loc,
        inv_loc,
        pre_glo,
        normed_glo,
        inv_glo,
    )
    means_layer = jnp.concatenate([mean_one, mean_two, mean_loc, mean_glo])
    vars_layer = jnp.concatenate([var_one, var_two, var_loc, var_glo])
    return (result, stored, (means_layer, vars_layer))


def layer_backward(grad_result, stored, geometry_now, kernels, gain_vec):
    (
        padded,
        pre_one,
        normed_one,
        inv_one,
        spectra,
        pre_two,
        normed_two,
        inv_two,
        summed,
        pre_loc,
        normed_loc,
        inv_loc,
        pre_glo,
        normed_glo,
        inv_glo,
    ) = stored
    pix_mask, freq_mask, pix_count, spec_count, tables = geometry_now
    fwd_cos, fwd_sin, inv_cos, inv_sin, row_cos, row_sin = tables
    local_kernel, lift_kernel, reduce_kernel, mix_kernel, expand_kernel = kernels
    band_size = pre_one.shape[1]
    width = pre_one.shape[2]
    grad_loc = grad_result[..., :CL] * pix_mask * silu_slope(pre_loc)
    grad_glo = grad_result[..., CL:] * pix_mask * silu_slope(pre_glo)
    loc_pair, glo_pair = grad_moments([grad_loc, grad_glo], [normed_loc, normed_glo])
    d_local = norm_backward(
        grad_loc, normed_loc, inv_loc, gain_vec[3 * CS : 3 * CS + CL], loc_pair, pix_count, pix_mask
    ).astype(jnp.bfloat16)
    d_global = norm_backward(
        grad_glo, normed_glo, inv_glo, gain_vec[3 * CS + CL :], glo_pair, pix_count, pix_mask
    ).astype(jnp.bfloat16)
    grad_expand = jnp.einsum("mrwc,mrwd->cd", summed, d_global, preferred_element_type=jnp.float32)
    d_summed = jnp.einsum(
        "mrwd,cd->mrwc", d_global, expand_kernel, preferred_element_type=jnp.float32
    )
    d_returned = jnp.concatenate(
        [width_inverse_adj(d_summed, inv_cos), width_inverse_adj(d_summed, inv_sin)], axis=-1
    ).astype(jnp.bfloat16)
    d_inverse = lax.all_to_all(d_returned, "dp", split_axis=2, concat_axis=1, tiled=True).astype(
        jnp.float32
    )
    d_activated = rows_forward(row_cos, row_sin, d_inverse)
    grad_two = d_activated * freq_mask * silu_slope(pre_two)
    two_pair = grad_moments([grad_two], [normed_two])[0]
    d_mixed = norm_backward(
        grad_two, normed_two, inv_two, gain_vec[CS : 3 * CS], two_pair, spec_count, freq_mask
    ).astype(jnp.bfloat16)
    grad_mix = jnp.einsum("mkfc,mkfd->cd", spectra, d_mixed, preferred_element_type=jnp.float32)
    d_spectra = jnp.einsum("mkfd,cd->mkfc", d_mixed, mix_kernel, preferred_element_type=jnp.float32)
    d_columns = rows_inverse(row_cos, row_sin, d_spectra).astype(jnp.bfloat16)
    d_spectrum = lax.all_to_all(d_columns, "dp", split_axis=1, concat_axis=2, tiled=True).astype(
        jnp.float32
    )
    half_ch = d_spectrum.shape[-1] // 2
    d_upper = (
        d_summed
        + width_forward_adj(d_spectrum[..., :half_ch], fwd_cos)
        + width_forward_adj(d_spectrum[..., half_ch:], fwd_sin)
    )
    grad_one = d_upper * pix_mask * silu_slope(pre_one)
    one_pair = grad_moments([grad_one], [normed_one])[0]
    d_reduced = norm_backward(
        grad_one, normed_one, inv_one, gain_vec[:CS], one_pair, pix_count, pix_mask
    ).astype(jnp.bfloat16)
    acts_low = padded[:, 1:-1, 1:-1, :]
    grad_reduce = jnp.einsum(
        "mrwc,mrwd->cd", acts_low[..., CL:], d_reduced, preferred_element_type=jnp.float32
    )
    d_global_in = jnp.einsum(
        "mrwd,cd->mrwc", d_reduced, reduce_kernel, preferred_element_type=jnp.float32
    )
    grad_outs = jnp.concatenate([d_local, d_global], axis=-1)
    grad_pad = with_halo(grad_outs, (("dp", 1),), 1)
    grad_pad = jnp.pad(grad_pad, ((0, 0), (0, 0), (1, 1), (0, 0)))
    d_acts = conv_rows(grad_pad[..., :CL], flipped(local_kernel))
    d_lift = conv_rows(grad_pad[..., CL:], flipped(lift_kernel))
    d_input = d_acts + jnp.concatenate([d_lift, d_global_in], axis=-1)
    grad_local_kernel = kernel_grad(padded, d_local, band_size, width)
    grad_lift = kernel_grad(padded[..., :CL], d_global, band_size, width)
    gains_grad = jnp.concatenate([one_pair[1], two_pair[1], loc_pair[1], glo_pair[1]])
    biases_grad = jnp.concatenate([one_pair[0], two_pair[0], loc_pair[0], glo_pair[0]])
    return (
        d_input,
        (grad_local_kernel, grad_lift, grad_reduce, grad_mix, grad_expand),
        (gains_grad, biases_grad),
    )


def block_forward(block_in, geometry_now, kernels, gain_all, bias_all):
    base = block_in.astype(jnp.float32) * geometry_now[0]
    first_out, first_stored, first_stats = layer_forward(
        base, geometry_now, kernels[0], gain_all[0], bias_all[0]
    )
    second_out, second_stored, second_stats = layer_forward(
        first_out, geometry_now, kernels[1], gain_all[1], bias_all[1]
    )
    return (
        (second_out + base).astype(jnp.bfloat16),
        (first_stored, second_stored),
        (first_stats, second_stats),
    )


def block_backward(grad_in, stored, geometry_now, kernels, gain_all):
    pix_mask = geometry_now[0]
    grad_masked = grad_in * pix_mask
    d_first, second_kernels, second_norms = layer_backward(
        grad_masked, stored[1], geometry_now, kernels[1], gain_all[1]
    )
    d_base, first_kernels, first_norms = layer_backward(
        d_first, stored[0], geometry_now, kernels[0], gain_all[0]
    )
    return (
        (grad_masked + d_base) * pix_mask,
        (first_kernels, second_kernels),
        (first_norms, second_norms),
    )


def running_update(mean_now, var_now, layer_stats, geometry_now):
    pix_count = geometry_now[2]
    spec_count = geometry_now[3]
    counts = jnp.concatenate(
        [
            jnp.full((CS,), pix_count, jnp.float32),
            jnp.full((2 * CS,), spec_count, jnp.float32),
            jnp.full((CL + CG,), pix_count, jnp.float32),
        ]
    )
    batch_means = jnp.stack([layer_stats[0][0], layer_stats[1][0]])
    batch_vars = jnp.stack([layer_stats[0][1], layer_stats[1][1]])
    new_mean = (1.0 - MOMENTUM) * mean_now + MOMENTUM * batch_means
    new_var = (1.0 - MOMENTUM) * var_now + MOMENTUM * batch_vars * counts / (counts - 1.0)
    return (new_mean, new_var)


def on_device(
    inputs,
    cotangent,
    shapes,
    local_to_local,
    global_to_local,
    local_to_global,
    spec_reduce,
    spec_mix,
    spec_expand,
    norm_gains,
    norm_biases,
    run_means,
    run_vars,
):
    section_id = lax.axis_index("section")
    band_index = lax.axis_index("dp")
    n_dp = lax.axis_size("dp")
    micro_count = inputs.shape[0]
    map_count = inputs.shape[1]
    band_size = inputs.shape[2]
    freq_total = (LONG // 2 + n_dp) // n_dp * n_dp
    freq_local = freq_total // n_dp
    kernels = []
    for layer_pos in range(2):
        local_kernel = jnp.concatenate(
            [local_to_local[0, layer_pos], global_to_local[0, layer_pos]], axis=1
        )
        kernels.append(
            (
                local_kernel,
                local_to_global[0, layer_pos],
                spec_reduce[0, layer_pos],
                spec_mix[0, layer_pos],
                spec_expand[0, layer_pos],
            )
        )
    gain_all = norm_gains[0]
    bias_all = norm_biases[0]
    received = jnp.zeros(inputs.shape[1:], jnp.bfloat16)
    run_mean = run_means[0]
    run_var = run_vars[0]
    outputs = jnp.zeros(inputs.shape, jnp.bfloat16)
    saved_inputs = []
    saved_geometry = []
    for tick_pos in range(micro_count + 1):
        micro_index = tick_pos - section_id
        is_valid = (micro_index >= 0) & (micro_index < micro_count)
        micro_slot = jnp.clip(micro_index, 0, micro_count - 1)
        own_input = lax.dynamic_index_in_dim(inputs, micro_slot, 0, keepdims=False)
        block_in = jnp.where(section_id == 0, own_input, received)
        shape_row = lax.dynamic_index_in_dim(shapes, micro_slot, 0, keepdims=False)
        geometry_now = geometry(shape_row, band_index, band_size, freq_total, freq_local, map_count)
        block_out, stored, layer_stats = block_forward(
            block_in, geometry_now, kernels, gain_all, bias_all
        )
        new_mean, new_var = running_update(run_mean, run_var, layer_stats, geometry_now)
        run_mean = jnp.where(is_valid, new_mean, run_mean)
        run_var = jnp.where(is_valid, new_var, run_var)
        updated = lax.dynamic_update_index_in_dim(outputs, block_out, micro_slot, 0)
        outputs = jnp.where(is_valid, updated, outputs)
        saved_inputs.append(block_in)
        saved_geometry.append(geometry_now)
        if tick_pos < micro_count:
            received = from_behind(block_out, "section", 1)
    kernel_acc = [jnp.zeros((2,) + part_now.shape, jnp.float32) for part_now in kernels[0]]
    gain_acc = jnp.zeros(gain_all.shape, jnp.float32)
    bias_acc = jnp.zeros(bias_all.shape, jnp.float32)
    received_grad = jnp.zeros(inputs.shape[1:], jnp.bfloat16)
    grads_out = jnp.zeros(inputs.shape, jnp.float32)
    for tick_pos in range(micro_count + 1):
        micro_index = micro_count - tick_pos - section_id
        is_valid = (micro_index >= 0) & (micro_index < micro_count)
        micro_slot = jnp.clip(micro_index, 0, micro_count - 1)
        scale_valid = is_valid.astype(jnp.float32)
        forward_tick = micro_count - tick_pos
        geometry_now = saved_geometry[forward_tick]
        recomputed = block_forward(
            saved_inputs[forward_tick], geometry_now, kernels, gain_all, bias_all
        )
        stored = recomputed[1]
        own_grad = lax.dynamic_index_in_dim(cotangent, micro_slot, 0, keepdims=False)
        grad_in = jnp.where(section_id == 1, own_grad, received_grad).astype(jnp.float32)
        grad_input, kernel_grads, norm_grads = block_backward(
            grad_in, stored, geometry_now, kernels, gain_all
        )
        sent_grad = grad_input.astype(jnp.bfloat16)
        kept_grad = jnp.where(section_id == 1, sent_grad.astype(jnp.float32), grad_input)
        updated = lax.dynamic_update_index_in_dim(grads_out, kept_grad, micro_slot, 0)
        grads_out = jnp.where(is_valid, updated, grads_out)
        stacked = [
            jnp.stack([kernel_grads[0][part_pos], kernel_grads[1][part_pos]]) * scale_valid
            for part_pos in range(5)
        ]
        gain_acc = gain_acc + jnp.stack([norm_grads[0][0], norm_grads[1][0]]) * scale_valid
        bias_acc = bias_acc + jnp.stack([norm_grads[0][1], norm_grads[1][1]]) * scale_valid
        kernel_acc = [acc_part + new_part for acc_part, new_part in zip(kernel_acc, stacked)]
        if tick_pos < micro_count:
            received_grad = from_behind(sent_grad, "section", -1)
    totals = lax.psum(
        (kernel_acc[0], kernel_acc[1], kernel_acc[2], kernel_acc[3], kernel_acc[4]), "dp"
    )
    grad_ll = totals[0][:, :, :CL, :]
    grad_gl = totals[0][:, :, CL:, :]
    return (
        outputs[None],
        grads_out[None],
        grad_ll[None],
        grad_gl[None],
        totals[1][None],
        totals[2][None],
        totals[3][None],
        totals[4][None],
        gain_acc[None],
        bias_acc[None],
        run_mean[None],
        run_var[None],
    )


F32 = jnp.float32
BF16 = jnp.bfloat16
MESH = pl.DeviceIdType.MESH
MEMBERS = 16
ROWS = 8
LAYERS = 4
PAIRS = 4
HALF = 192
FULL = 384
SLOTS = 640
PIECES = 32
EARLY = 272
LATE = 64
AT_LL = 0
AT_GL = 1152
AT_KG = 4608
AT_E = 8064
AT_M = 0
AT_R = 1152
SECTION_NAMES = ("one", "two", "out")


def dot(a, b):
    return lax.dot_general(a, b, (((1,), (0,)), ((), ())), preferred_element_type=F32)


def dot_nt(a, b):
    return lax.dot_general(a, b, (((1,), (1,)), ((), ())), preferred_element_type=F32)


def dot_tn(a, b):
    return lax.dot_general(a, b, (((0,), (0,)), ((), ())), preferred_element_type=F32)


def sigmoid(v):
    return 0.5 * jnp.tanh(0.5 * v) + 0.5


def fold(v):
    return jnp.sum(v.reshape(v.shape[0] // 8, 8, v.shape[1]), axis=0)


def wide(row, lanes):
    whole, rest = divmod(lanes, 128)
    parts = [row] * whole + ([row[:, :rest]] if rest else [])
    return jnp.concatenate(parts, axis=1)


def network_kernel(
    inputs, cot, shapes, ll, gl, lg, red, mix, exp, gains, biases, run_m, run_v,
    out_y, out_g, out_we, out_wl, out_gains, out_biases, out_m, out_v,
    w_c, w_gl, w_r, w_m, w_e, raw_g, raw_b, pars, acts, shifted, halo, v1, u, spec, mixed, tsum, v34,
    pmask, qmask, tf, tft, tg, tgt, hf, hi, vab, e2, dq, ds, g, gblk, at,
    gwe, gwl, rbe, rbl, fine, finl,
    ssum, rsum, send, recv, stats, stats_far,
    sem_w, sem_in, sem_cot, sem_halo_s, sem_halo_r, sem_ar_s, sem_ar_r, sem_aa_s, sem_aa_r,
    sem_y_s, sem_y_r, sem_g_s, sem_g_r, sem_rs, sem_rr, sem_st,
):
    s = lax.axis_index("section")
    d = lax.axis_index("dp")
    n_dp = lax.axis_size("dp")
    per = n_dp // 2
    grp = lax.div(d, per)

    def differ(a, b):
        return a + b - 2 * a * b

    def mirrored(chip):
        return (3 - lax.div(chip, 4)) * 4 + lax.rem(chip, 4)

    half = differ(s, grp)
    me = jnp.where(s == 0, d, mirrored(d))
    first = (me == 0).astype(F32)
    at_z = lax.div(d, 4)

    def member(group, k):
        core = differ(lax.div(k, per), group)
        return (core, jnp.where(core == 0, k, mirrored(k)))

    def peer(i):
        flips = MEMBERS - 1 - i
        chip = lax.rem(d, per)
        other = grp * per
        for bit in (1, 2, 4):
            other = other + bit * differ(lax.rem(lax.div(chip, bit), 2), lax.rem(lax.div(flips, 2 * bit), 2))
        core = differ(s, lax.rem(flips, 2))
        return jnp.where(core == 0, other, mirrored(other)), (core, other)

    barrier = pltpu.get_barrier_semaphore()
    total = 2 * n_dp
    flat = s * n_dp + d

    def greet(i, c):
        other = lax.rem(flat + 1 + i, total)
        pl.semaphore_signal(
            barrier, inc=1, device_id=(lax.div(other, n_dp), lax.rem(other, n_dp)), device_id_type=MESH
        )
        return c

    lax.fori_loop(0, total - 1, greet, 0)

    own = pl.ds(2 * s, 2)
    places = [
        (red, w_r.at[own]),
        (gains, raw_g.at[s]),
        (biases, raw_b.at[s]),
        (ll, w_c.at[own, :, :, 0:CL]),
        (lg, w_c.at[own, :, :, CL:]),
        (gl, w_gl.at[own]),
        (mix, w_m.at[own]),
        (exp, w_e.at[own]),
    ]
    local_w = [pltpu.make_async_copy(a, b, sem_w.at[0, i]) for i, (a, b) in enumerate(places)]
    for c in local_w:
        c.start()

    pl.semaphore_wait(barrier, total - 1)

    across = (s, mirrored(d))
    stays = s == 0

    def across_copy(source, target, sems):
        return pltpu.make_async_remote_copy(
            source, target, sems.at[0], sems.at[1], device_id=across, device_id_type=MESH
        )

    def when_far(do):
        pl.when(jnp.logical_not(stays))(do)

    input_near = lambda: pltpu.make_async_copy(inputs.at[half], acts.at[0], sem_in.at[0, 0])

    def input_far(part):
        lanes = pl.ds(CL, CG) if part == 0 else pl.ds(0, CL)
        return across_copy(inputs.at[half, :, :, lanes], acts.at[0, :, :, lanes], sem_in.at[part])

    cot_near = lambda: pltpu.make_async_copy(cot.at[half], gblk.at[1], sem_cot.at[0, 0])

    def cot_far(row):
        return across_copy(cot.at[half, row], gblk.at[1, row], sem_cot.at[row])

    def push_rows(parity, window, do):
        if window % 2:
            row = 4 * parity + window - 1
            do(row)
            do(row + 1)

    pl.when(stays)(lambda: input_near().start())
    when_far(lambda: input_far(0).start())
    when_far(lambda: input_far(1).start())
    partner = (1 - s, d)
    remote_w = [
        pltpu.make_async_remote_copy(
            a, b, sem_w.at[1, i], sem_w.at[2, i], device_id=partner, device_id_type=MESH
        )
        for i, (a, b) in enumerate(places)
    ]
    for c in remote_w:
        c.start()

    height = shapes[grp, 0]
    width = shapes[grp, 1]
    col = lax.broadcasted_iota(jnp.int32, (128, 128), 0)
    for q in range(PAIRS):
        for h in range(2):
            row_ok = (ROWS * me + 2 * q + h < height).astype(F32)
            pmask[q, h * 128 : (h + 1) * 128, :] = (col < width).astype(F32) * row_ok
    for f in range(4):
        f_ok = (4 * me + f <= lax.div(width, 2)).astype(F32)
        qmask[f * 128 : (f + 1) * 128, :] = (col < height).astype(F32) * f_ok
    qmask[512:640, :] = (col < height).astype(F32) * (64 <= lax.div(width, 2)).astype(F32) * first

    def inverse(count, less=0):
        return 1.0 / jnp.full((1, 128), (count - less).astype(F32))

    inv_n = inverse(height * width)
    inv_ns = inverse(height * (lax.div(width, 2) + 1))

    row_a = lax.broadcasted_iota(jnp.int32, (128, 512), 0)
    col_a = lax.broadcasted_iota(jnp.int32, (128, 512), 1)
    r_of = (col_a >> 5) * 8 + ((col_a & 31) >> 3) * 2 + (col_a & 1)
    sel_r = (row_a == r_of).astype(F32).astype(BF16)
    f_of = (col_a >> 1) & 3
    row_b = lax.broadcasted_iota(jnp.int32, (512, 128), 0)
    col_b = lax.broadcasted_iota(jnp.int32, (512, 128), 1)
    r_ob = (row_b >> 5) * 8 + ((row_b & 31) >> 3) * 2 + (row_b & 1)
    sel_rt = (col_b == r_ob).astype(F32).astype(BF16)
    f_ob = (row_b >> 1) & 3
    position = lax.broadcasted_iota(jnp.int32, (128, 128), 0)
    other_axis = lax.broadcasted_iota(jnp.int32, (128, 128), 1)

    def wave(index, side, limit, turn):
        side_real = jnp.full((128, 128), side.astype(F32))
        product = (index * other_axis).astype(F32)
        phase = product - side_real * jnp.floor((product + 0.5) / side_real)
        value = jnp.cos(phase * (2.0 * jnp.pi / side_real) + turn) * lax.rsqrt(side_real)
        return jnp.where((index < limit) & (other_axis < side), value, 0.0)

    half_turn = 0.5 * jnp.pi
    for part in range(2):
        base = wave(position, height, height, -half_turn * part).astype(BF16)
        spread = dot(base, sel_r)
        spread_t = dot(sel_rt, base)
        for f in range(4):
            hf[f, part * 128 : (part + 1) * 128, :] = jnp.where(f_of == f, spread, 0.0).astype(BF16)
            at_col = part * 512 + f * 128
            hi[:, at_col : at_col + 128] = jnp.where(f_ob == f, spread_t, 0.0).astype(BF16)
    row_c = lax.broadcasted_iota(jnp.int32, (128, 128), 0)
    sel_f = ((row_c >> 1) == lax.broadcasted_iota(jnp.int32, (128, 128), 1)).astype(F32).astype(BF16)
    half_width = lax.div(width, 2)
    lifted = jnp.where(position == 0, 64, position)
    waves = (
        wave(position, width, half_width + 1, 0.0),
        wave(lifted, width, half_width + 1, jnp.where(position == 0, 0.0, half_turn)),
    )
    weight = jnp.where((position == 0) | (position == half_width), 1.0, 2.0)
    for which, (plain, flipped_table) in enumerate(((tf, tft), (tg, tgt))):
        for part in range(2):
            spread = dot(sel_f, (waves[part] * weight if which else waves[part]).astype(BF16))
            spread_t = jnp.transpose(spread)
            for h in range(2):
                rows = slice(part * 128, (part + 1) * 128)
                cols = slice(h * 128, (h + 1) * 128)
                plain[rows, cols] = jnp.where((row_c & 1) == h, spread, 0.0).astype(BF16)
                flipped_table[cols, rows] = jnp.where(
                    (lax.broadcasted_iota(jnp.int32, (128, 128), 1) & 1) == h, spread_t, 0.0
                ).astype(BF16)
    stats[...] = jnp.zeros_like(stats)
    ssum[...] = jnp.zeros_like(ssum)
    shifted[0] = jnp.zeros((128, 1536), BF16)
    shifted[9] = jnp.zeros((128, 1536), BF16)
    gwe[...] = jnp.zeros_like(gwe)
    gwl[...] = jnp.zeros_like(gwl)

    def sums_start(slot):
        rsum[slot, me] = ssum[slot]

        def go(i, c):
            k, device = peer(i)
            pltpu.make_async_remote_copy(
                ssum.at[slot], rsum.at[slot, me], sem_ar_s.at[slot, k], sem_ar_r.at[slot, me],
                device_id=device, device_id_type=MESH,
            ).start()
            return c

        lax.fori_loop(0, MEMBERS - 1, go, 0)

    def sums_wait(slot, lanes):
        def go(i, c):
            k, device = peer(i)
            pltpu.make_async_remote_copy(
                ssum.at[slot], rsum.at[slot, k], sem_ar_s.at[slot, k], sem_ar_r.at[slot, k],
                device_id=device, device_id_type=MESH,
            ).wait()
            return c

        lax.fori_loop(0, MEMBERS - 1, go, 0)
        tot = jnp.sum(rsum[slot], axis=0)
        tiles = (lanes + 127) // 128
        one = jnp.concatenate([tot[i : i + 1] for i in range(tiles)], axis=1)[:, :lanes]
        two = jnp.concatenate([tot[4 + i : 5 + i] for i in range(tiles)], axis=1)[:, :lanes]
        return one, two

    def put_sums(slot, one, two):
        lanes = one.shape[1]
        for base_row, part in ((0, one), (4, two)):
            flat_part = jnp.sum(part, axis=0, keepdims=True)
            for i in range((lanes + 127) // 128):
                w = min(128, lanes - i * 128)
                ssum[slot, base_row + i : base_row + i + 1, 0:w] = flat_part[:, i * 128 : i * 128 + w]

    def swap_start(slot):
        recv[slot, me] = send[slot, me]

        def go(i, c):
            k, device = peer(i)
            pltpu.make_async_remote_copy(
                send.at[slot, k], recv.at[slot, me], sem_aa_s.at[slot, k], sem_aa_r.at[slot, me],
                device_id=device, device_id_type=MESH,
            ).start()
            return c

        lax.fori_loop(0, MEMBERS - 1, go, 0)

    def swap_wait(slot):
        def go(i, c):
            k, device = peer(i)
            pltpu.make_async_remote_copy(
                send.at[slot, k], recv.at[slot, k], sem_aa_s.at[slot, k], sem_aa_r.at[slot, k],
                device_id=device, device_id_type=MESH,
            ).wait()
            return c

        lax.fori_loop(0, MEMBERS - 1, go, 0)

    def halo_copies():
        up = lambda: pltpu.make_async_remote_copy(
            shifted.at[1, :, 512:1024], halo.at[1], sem_halo_s.at[0], sem_halo_r.at[1],
            device_id=member(grp, lax.rem(me + MEMBERS - 1, MEMBERS)), device_id_type=MESH,
        )
        down = lambda: pltpu.make_async_remote_copy(
            shifted.at[8, :, 512:1024], halo.at[0], sem_halo_s.at[1], sem_halo_r.at[0],
            device_id=member(grp, lax.rem(me + 1, MEMBERS)), device_id_type=MESH,
        )
        return up, down

    has_up = me > 0
    has_down = me < MEMBERS - 1

    def halo_start():
        up, down = halo_copies()

        @pl.when(has_up)
        def _():
            up().start()

        @pl.when(has_down)
        def _():
            down().start()

    def put_sides(index, x, flip):
        at_col = lax.broadcasted_iota(jnp.int32, (128, 512), 0)
        before = jnp.where(at_col == 0, 0.0, pltpu.roll(x, 1, 0)).astype(BF16)
        after = jnp.where(at_col == 127, 0.0, pltpu.roll(x, 127, 0)).astype(BF16)
        shifted[index, :, 0:512] = after if flip else before
        shifted[index, :, 1024:1536] = before if flip else after

    def put_shifted(index, row, flip):
        shifted[index, :, 512:1024] = row
        put_sides(index, row.astype(F32), flip)

    def halo_wait(flip):
        up, down = halo_copies()

        @pl.when(has_up)
        def _():
            up().wait_send()
            down().wait_recv()
            put_shifted(0, halo[0], flip)

        @pl.when(has_down)
        def _():
            down().wait_send()
            up().wait_recv()
            put_shifted(9, halo[1], flip)

    lane = lax.broadcasted_iota(jnp.int32, (128, FULL), 1)
    low = lane < HALF

    def width_out(slot, h, table, get):
        parts = []
        for q in (2 * h, 2 * h + 1):
            x = dot(table[...], get(q))
            both = jnp.concatenate([x[:128], x[128:]], axis=1)
            parts.append(both.reshape(MEMBERS, 8, FULL))
        send[slot, :, pl.ds(pl.multiple_of(16 * h, 16), 16), :] = jnp.concatenate(parts, axis=1).astype(BF16)

    def width_back(slot, h, table):
        block = recv[slot, :, pl.ds(pl.multiple_of(16 * h, 16), 16), :].astype(F32)
        results = []
        for o in range(2):
            z = block[:, 8 * o : 8 * o + 8, :].reshape(128, FULL)
            zi = pltpu.roll(z, HALF, 1)
            stacked = jnp.concatenate([z[:, :HALF], zi[:, :HALF]], axis=0).astype(BF16)
            results.append(dot(table[...], stacked))
        return results

    def rows_forward_into(slot, put):
        x = recv[slot].reshape(512, FULL)
        for f in range(4):
            both = dot(hf[f], x)
            a, b = both[:128], both[128:]
            turned = pltpu.roll(b, HALF, 1)
            if f == 0:
                rest = 1.0 - first
                put(0, jnp.where(low, a + rest * turned, rest * a - turned))
                put(4, jnp.where(low, pltpu.roll(a, HALF, 1), -b) * first)
            else:
                put(f, jnp.where(low, a + turned, a - turned))

    def rows_inverse_from(slot, get):
        last = get(4)
        for f in range(4):
            v = get(f)
            turned = pltpu.roll(v, HALF, 1)
            if f == 0:
                rest = 1.0 - first
                a = jnp.where(low, v, rest * v + first * pltpu.roll(last, HALF, 1))
                b = jnp.where(low, -turned, rest * turned - first * last)
            else:
                a = v
                b = jnp.where(low, -turned, turned)
            vab[f * 128 : (f + 1) * 128, :] = a.astype(BF16)
            vab[512 + f * 128 : 640 + f * 128, :] = b.astype(BF16)

        def go(c, carry):
            z = dot(hi[pl.ds(pl.multiple_of(c * 256, 256), 256), :], vab[...])
            send[slot, pl.ds(c * 8, 8)] = z.astype(BF16).reshape(8, 32, FULL)
            return carry

        lax.fori_loop(0, 2, go, 0)

    def moments(layer, which, lanes, one, two, inv_count):
        count = wide(inv_count, lanes)
        mean = one * count
        var = two * count - mean * mean
        inv = lax.rsqrt(var + EPSILON)
        stats[layer, which : which + 1, 0:lanes] = mean
        stats[layer, 3 + which : 4 + which, 0:lanes] = inv
        stats[layer, 6 + which : 7 + which, 0:lanes] = var
        scale = pars[layer, which : which + 1, 0:lanes] * inv
        shift = pars[layer, 3 + which : 4 + which, 0:lanes] - mean * scale
        return scale, shift

    def affine(layer, which, lanes):
        mean = stats[layer, which : which + 1, 0:lanes]
        inv = stats[layer, 3 + which : 4 + which, 0:lanes]
        gain = pars[layer, which : which + 1, 0:lanes]
        return mean, inv, gain, pars[layer, 3 + which : 4 + which, 0:lanes]

    def keep_grad_sums(layer, which, lanes, one, two):
        stats[layer, 9 + which : 10 + which, 0:lanes] = one
        stats[layer, 12 + which : 13 + which, 0:lanes] = two

    zero_of = lambda lanes: jnp.zeros((8, lanes), F32)

    def conv_pair(layer, c):
        loc = jnp.zeros((256, 512), F32)
        glo = jnp.zeros((256, 128), F32)
        for i in range(3):
            a_loc = jnp.concatenate(
                [shifted[pl.ds(2 * c + i, 2), :, j * 512 : j * 512 + 128].reshape(256, 128) for j in range(3)], axis=1
            )
            a_glo = jnp.concatenate(
                [shifted[pl.ds(2 * c + i, 2), :, j * 512 + 128 : (j + 1) * 512].reshape(256, 384) for j in range(3)],
                axis=1,
            )
            loc = loc + dot(a_loc, w_c[layer, 3 * i : 3 * i + 3].reshape(384, 512))
            glo = glo + dot(a_glo, w_gl[layer, 3 * i : 3 * i + 3].reshape(1152, 128))
        v34[layer, c, :, 0:CL] = loc[:, :CL] + glo
        v34[layer, c, :, CL:] = loc[:, CL:]

    pl.when(stays)(lambda: input_near().wait())
    when_far(lambda: input_far(0).wait())
    pl.when(stays)(lambda: cot_near().start())

    def pixel_rows(r):
        return lax.div(r, 2), pl.ds(pl.multiple_of(lax.rem(r, 2) * 128, 128), 128)

    def mask_global(r, c):
        q, here = pixel_rows(r)
        x = acts[0, r, :, CL:].astype(F32) * wide(pmask[q, here, :], CG)
        acts[0, r, :, CL:] = x.astype(BF16)
        return c

    lax.fori_loop(0, ROWS, mask_global, 0)
    for c in local_w[:3] + remote_w[:3]:
        c.wait()
    for lay in range(LAYERS):
        for base_row, raw in ((0, raw_g), (3, raw_b)):
            row = raw[lay // 2, lay % 2 : lay % 2 + 1, :]
            pars[lay, base_row : base_row + 1, 0:CS] = row[:, :CS]
            pars[lay, base_row + 1 : base_row + 2, 0:FULL] = row[:, CS : 3 * CS]
            pars[lay, base_row + 2 : base_row + 3, :] = row[:, 3 * CS :]

    def start_row(r, c):
        q, here = pixel_rows(r)
        acts[0, r, :, 0:CL] = (acts[0, r, :, 0:CL].astype(F32) * pmask[q, here, :]).astype(BF16)
        return c

    def finish_start():
        when_far(lambda: input_far(1).wait())
        lax.fori_loop(0, ROWS, start_row, 0)
        for c in local_w[3:] + remote_w[3:]:
            c.wait()

    def out_copies(source, target, sems, block, row):
        send_sem, arrive_sem = sems
        far = lambda: pltpu.make_async_remote_copy(
            source.at[row], target.at[grp, row], send_sem.at[block, row], arrive_sem.at[grp, row],
            device_id=(block, me), device_id_type=MESH,
        )
        near = lambda: pltpu.make_async_copy(source.at[row], target.at[grp, row], send_sem.at[block, row])
        return (block == s) & (me == d), far, near

    def y_copies(block, row):
        return out_copies(acts.at[2 * block + 2], out_y, (sem_y_s, sem_y_r), block, row)

    def g_copies(block, row):
        return out_copies(gblk.at[1 - block], out_g, (sem_g_s, sem_g_r), block, row)

    def start_out(made):
        here, far, near = made
        pl.when(here)(lambda: near().start())
        pl.when(jnp.logical_not(here))(lambda: far().start())

    def wait_out(made):
        here, far, near = made
        pl.when(here)(lambda: near().wait())
        pl.when(jnp.logical_not(here))(lambda: far().wait_send())

    def forward_window(layer, window):
        parity = lax.rem(layer, 2)

        @pl.when(layer < 2)
        def _():
            push_rows(parity, window, lambda row: when_far(lambda: cot_far(row).start()))

        @pl.when(layer >= 2)
        def _():
            push_rows(parity, window, lambda row: start_out(y_copies(0, row)))

    def backward_window(step, window):
        parity = lax.rem(step, 2)

        @pl.when(step < 2)
        def _():
            push_rows(parity, window, lambda row: start_out(y_copies(1, row)))

        @pl.when(step >= 2)
        def _():
            push_rows(parity, window, lambda row: start_out(g_copies(1, row)))

    def forward(layer, carry):
        def reduce_pair(q, sums):
            a = acts[layer, pl.ds(2 * q, 2), :, CL:].reshape(256, CG)
            v = dot_nt(a, w_r[layer])
            v1[layer, q] = v
            return sums[0] + fold(v), sums[1] + fold(v * v)

        put_sums(0, *lax.fori_loop(0, PAIRS, reduce_pair, (zero_of(HALF), zero_of(HALF))))
        sums_start(0)
        pl.when(layer == 0)(finish_start)

        def lay_out(r, carry):
            put_shifted(1 + r, acts[layer, r], False)
            return carry

        lax.fori_loop(0, ROWS, lay_out, 0)
        halo_start()
        forward_window(layer, 0)

        def conv_go(c, carry):
            conv_pair(layer, c)
            return carry

        lax.fori_loop(1, 3, conv_go, 0)
        scale, shift = moments(layer, 0, HALF, *sums_wait(0, HALF), inv_n)

        def spectral_in(h, carry):
            def get(q):
                pre = v1[layer, q] * scale + shift
                x = pre * sigmoid(pre) * wide(pmask[q], HALF)
                u[q] = x
                return x.astype(BF16)

            width_out(0, h, tf, get)
            return carry

        lax.fori_loop(0, 2, spectral_in, 0)
        swap_start(0)
        halo_wait(False)
        conv_pair(layer, 0)
        forward_window(layer, 1)
        swap_wait(0)

        def put(f, y):
            spec[layer, f * 128 : (f + 1) * 128, :] = y.astype(BF16)

        rows_forward_into(0, put)

        mixed[layer] = dot(spec[layer], w_m[layer])

        def mix_block(f, sums):
            v = mixed[layer, pl.ds(pl.multiple_of(f * 128, 128), 128), :]
            return sums[0] + fold(v), sums[1] + fold(v * v)

        put_sums(1, *lax.fori_loop(0, 5, mix_block, (zero_of(FULL), zero_of(FULL))))
        sums_start(1)
        forward_window(layer, 2)
        scale2, shift2 = moments(layer, 1, FULL, *sums_wait(1, FULL), inv_ns)

        def get_v(f):
            rows = slice(f * 128, (f + 1) * 128)
            pre = mixed[layer, rows, :] * scale2 + shift2
            return pre * sigmoid(pre) * wide(qmask[rows, :], FULL)

        rows_inverse_from(1, get_v)
        swap_start(1)
        conv_pair(layer, 3)
        forward_window(layer, 3)
        swap_wait(1)

        def spectral_out(h, sums):
            backs = width_back(1, h, tgt)
            one, two = sums
            for o in range(2):
                q = 2 * h + o
                t = (u[q] + backs[o]).astype(BF16)
                tsum[layer, q] = t
                pm = pmask[q]
                v_loc = v34[layer, q, :, 0:CL] * pm
                v_glo = (v34[layer, q, :, CL:] + dot(t, w_e[layer])) * wide(pm, CG)
                v34[layer, q, :, 0:CL] = v_loc
                v34[layer, q, :, CL:] = v_glo
                v = jnp.concatenate([v_loc, v_glo], axis=1)
                one = one + fold(v)
                two = two + fold(v * v)
            return one, two

        put_sums(2, *lax.fori_loop(0, 2, spectral_out, (zero_of(512), zero_of(512))))
        sums_start(2)
        forward_window(layer, 4)
        scale3, shift3 = moments(layer, 2, 512, *sums_wait(2, 512), inv_n)
        odd = lax.rem(layer, 2)
        oddf = odd.astype(F32)

        def next_row(r, carry):
            q = lax.div(r, 2)
            here = pl.ds(pl.multiple_of(lax.rem(r, 2) * 128, 128), 128)
            pre = v34[layer, q, here, :] * scale3 + shift3
            x = pre * sigmoid(pre) * wide(pmask[q, here, :], 512)
            x = x + oddf * acts[layer - odd, r].astype(F32)
            acts[layer + 1, r] = x.astype(BF16)
            return carry

        lax.fori_loop(0, ROWS, next_row, 0)

        return carry

    lax.fori_loop(0, LAYERS, forward, 0)

    pl.when(stays)(lambda: cot_near().wait())

    def cot_wait(row, c):
        when_far(lambda: cot_far(row).wait())
        return c

    lax.fori_loop(0, ROWS, cot_wait, 0)

    def cot_row(r, c):
        q = lax.div(r, 2)
        here = pl.ds(pl.multiple_of(lax.rem(r, 2) * 128, 128), 128)
        x = gblk[1, r].astype(F32) * wide(pmask[q, here, :], 512)
        gblk[1, r] = x.astype(BF16)
        g[q, here, :] = x
        return c

    lax.fori_loop(0, ROWS, cot_row, 0)

    x_bit = lax.rem(d, 2)
    y_bit = lax.rem(lax.div(d, 2), 2)
    at_x = jnp.where(s == 0, x_bit, y_bit)
    at_y = jnp.where(s == 0, y_bit, x_bit)
    step_x = jnp.where(s == 0, 1, 2)
    step_y = 3 - step_x
    in_core = s * 16
    in_x = in_core + at_x * 8
    in_y = in_x + at_y * 4
    near_x = (s, d + step_x * (1 - 2 * at_x))
    near_y = (s, d + step_y * (1 - 2 * at_y))

    def sum_part(p, layer):
        gw, rb, fin, out, rows = ((gwe, rbe, fine, out_we, EARLY), (gwl, rbl, finl, out_wl, LATE))[p]
        block = lax.div(layer, 2)
        odd = lax.rem(layer, 2)
        slot = jnp.where(block == s, 2, 0) + odd

        def remote(stage, source, target, other, n=0):
            return pltpu.make_async_remote_copy(
                source, target, sem_rs.at[p, odd, stage, n], sem_rr.at[p, odd, stage, n], device_id=other, device_id_type=MESH
            )

        def rows_of(first_piece, pieces):
            return pl.ds(pl.multiple_of(first_piece * rows, rows), pieces * rows)

        one = lambda: remote(0, gw.at[rows_of((1 - s) * 16, 16)], rb.at[rows_of(0, 16)], partner)
        far_x = in_core + (1 - at_x) * 8

        def two(n):
            first_four = (1 - at_y) * 4 if n == 0 else at_y * 4
            return remote(1, gw.at[rows_of(far_x + first_four, 4)], rb.at[rows_of(16 + first_four, 4)], near_x, n)

        three = lambda: remote(2, gw.at[rows_of(in_x + (1 - at_y) * 4, 4)], rb.at[rows_of(24, 4)], near_y)

        def add(first_piece, from_piece, pieces):
            def go(i, carry):
                here = rows_of(first_piece + i, 1)
                there = rows_of(from_piece + i, 1)
                gw[here, :] = (gw[here, :].astype(F32) + rb[there, :].astype(F32)).astype(BF16)
                return carry

            lax.fori_loop(0, pieces, go, 0)

        def along_z(i):
            other = lax.rem(at_z + 1 + i, 4)
            return other, (s, d + 4 * (other - at_z))

        def four(i, arriving):
            other, device = along_z(i)
            return pltpu.make_async_remote_copy(
                gw.at[rows_of(in_y + other, 1)],
                rb.at[rows_of(28 + (other if arriving else at_z), 1)],
                sem_rs.at[p, odd, 3, i], sem_rr.at[p, odd, 3, other if arriving else at_z],
                device_id=device, device_id_type=MESH,
            )

        def five(i, arriving):
            other, device = along_z(i)
            return pltpu.make_async_remote_copy(
                fin, out.at[slot, rows_of(in_y + (other if arriving else at_z), 1)],
                sem_rs.at[p, odd, 4, i], sem_rr.at[p, odd, 4, other if arriving else at_z],
                device_id=device, device_id_type=MESH,
            )

        five_own = lambda: pltpu.make_async_copy(fin, out.at[slot, rows_of(in_y + at_z, 1)], sem_rs.at[p, odd, 4, 3])

        def spread_copy(stage, first_piece, other, n=0):
            here = out.at[slot, rows_of(first_piece, 4)]
            return remote(stage, here, here, other, n)

        six = lambda: spread_copy(5, in_y, near_y)
        seven = lambda n: spread_copy(6, in_y if n == 0 else in_x + (1 - at_y) * 4, near_x, n)
        eight = lambda: remote(
            7, out.at[odd, rows_of(in_core, 16)],
            out.at[2 + odd, rows_of(in_core, 16)], partner,
        )
        starts = s != block

        def begin_one():
            one().start()

        def begin_two():
            one().wait()
            add(in_core, 0, 16)
            two(0).start()
            two(1).start()

        def begin_three():
            two(0).wait()
            two(1).wait()
            add(in_x, 16, 8)
            three().start()

        def begin_four():
            three().wait()
            add(in_y, 24, 4)
            for i in range(3):
                four(i, False).start()

        def begin_five():
            total_now = gw[rows_of(in_y + at_z, 1), :].astype(F32)
            for i in range(3):
                four(i, False).wait_send()
                four(i, True).wait_recv()
                total_now = total_now + rb[rows_of(28 + lax.rem(at_z + 1 + i, 4), 1), :].astype(F32)
            fin[...] = total_now.astype(BF16)
            five_own().start()
            for i in range(3):
                five(i, False).start()

        def begin_six(quick):
            five_own().wait()
            for i in range(3):
                five(i, False).wait_send()
                five(i, True).wait_recv()
            six().start()
            if quick:
                seven(0).start()

        def begin_seven(quick):
            six().wait()
            if not quick:
                seven(0).start()
            seven(1).start()

        def begin_eight():
            seven(0).wait()
            seven(1).wait()
            pl.when(starts)(lambda: eight().start())

        def end():
            pl.when(starts)(lambda: eight().wait_send())
            pl.when(jnp.logical_not(starts))(lambda: eight().wait_recv())

        return (
            begin_one, begin_two, begin_three, begin_four, begin_five,
            lambda: begin_six(False), lambda: begin_seven(False), begin_eight, end,
            lambda: begin_six(True), lambda: begin_seven(True),
        )

    QUICK_SIX, QUICK_SEVEN = 9, 10

    def stage(p, layer, which):
        pl.when(layer < LAYERS)(lambda: sum_part(p, layer)[which]())

    def backward(step, carry):
        layer = LAYERS - 1 - step
        mean3, inv3, gain3, bias3 = affine(layer, 2, 512)
        scale3 = gain3 * inv3
        shift3 = bias3 - mean3 * scale3

        def slope_row(r, sums):
            q = lax.div(r, 2)
            here = pl.ds(pl.multiple_of(lax.rem(r, 2) * 128, 128), 128)
            v = v34[layer, q, here, :]
            pre = v * scale3 + shift3
            sg = sigmoid(pre)
            e = g[q, here, :] * wide(pmask[q, here, :], 512) * (sg * (1.0 + pre * (1.0 - sg)))
            g[q, here, :] = e
            return sums[0] + fold(e), sums[1] + fold(e * ((v - mean3) * inv3))

        put_sums(3, *lax.fori_loop(0, ROWS, slope_row, (zero_of(512), zero_of(512))))
        sums_start(3)
        backward_window(step, 0)

        def turn_row(r, carry):
            at[:, pl.ds(pl.multiple_of(r * 128, 128), 128)] = jnp.transpose(acts[layer, r])
            return carry

        stage(0, layer + 1, 3)
        stage(0, layer + 2, 6)
        stage(1, layer + 1, 1)
        stage(1, layer + 2, QUICK_SEVEN)
        lax.fori_loop(0, ROWS, turn_row, 0)
        one3, two3 = sums_wait(3, 512)
        keep_grad_sums(layer, 2, 512, one3, two3)
        part_a = one3 * wide(inv_n, 512)
        part_b = two3 * wide(inv_n, 512)

        def d_row(r, carry):
            q = lax.div(r, 2)
            here = pl.ds(pl.multiple_of(lax.rem(r, 2) * 128, 128), 128)
            z = (v34[layer, q, here, :] - mean3) * inv3
            dv = wide(pmask[q, here, :], 512) * scale3 * (g[q, here, :] - part_a - z * part_b)
            shifted[1 + r, :, 512:1024] = dv.astype(BF16)
            return carry

        lax.fori_loop(0, ROWS, d_row, 0)
        halo_start()

        def grad_out(h, carry):
            def get(q):
                dg = shifted[pl.ds(1 + 2 * q, 2), :, 512 + CL : 1024].reshape(256, CG)
                dt = dot_nt(dg, w_e[layer])
                u[q] = dt
                return dt.astype(BF16)

            width_out(0, h, tg, get)
            return carry

        lax.fori_loop(0, 2, grad_out, 0)
        swap_start(0)

        def lay_sides(r, carry):
            put_sides(1 + r, shifted[1 + r, :, 512:1024].astype(F32), True)
            return carry

        lax.fori_loop(0, ROWS, lay_sides, 0)
        halo_wait(True)

        def conv_back(c, carry):
            d_loc = jnp.zeros((256, 128), F32)
            d_glo = jnp.zeros((256, 384), F32)
            for i in range(3):
                for j in range(3):
                    rows = pl.ds(2 * c + 2 - i, 2)
                    dd = shifted[rows, :, j * 512 : (j + 1) * 512].reshape(256, 512)
                    d_loc = d_loc + dot_nt(dd, w_c[layer, 3 * i + j])
                    d_glo = d_glo + dot_nt(dd[:, :CL], w_gl[layer, 3 * i + j])
            g[c, :, 0:CL] = d_loc
            g[c, :, CL:] = d_glo
            return carry

        def block_rows(i, lanes):
            return jnp.concatenate(
                [
                    shifted[2 - i : 10 - i, :, j * 512 + lanes[0] : j * 512 + lanes[1]].reshape(1024, lanes[1] - lanes[0])
                    for j in range(3)
                ],
                axis=1,
            )

        def lift_grad(i):
            acc = dot(at[0:CL, :], block_rows(i, (CL, 512)))
            for j in range(3):
                for n in range(3):
                    base = AT_KG + n * 1152 + (3 * i + j) * 128
                    gwe[base : base + 128, :] = acc[:, (3 * j + n) * 128 : (3 * j + n + 1) * 128].astype(BF16)

        def local_grad(i):
            acc = dot(at[...], block_rows(i, (0, CL)))
            for j in range(3):
                tap = 3 * i + j
                block = acc[:, j * 128 : (j + 1) * 128].astype(BF16)
                gwe[AT_LL + tap * CL : AT_LL + (tap + 1) * CL, :] = block[:CL]
                gwe[AT_GL + tap * CG : AT_GL + (tap + 1) * CG, :] = block[CL:]

        stage(1, layer + 2, 7)
        stage(1, layer + 1, 2)
        backward_window(step, 1)
        stage(0, layer + 1, 4)
        for i in range(3):
            local_grad(i)
        for i in range(3):
            lift_grad(i)
        acc_e = jnp.zeros((HALF, CG), F32)
        for q in range(PAIRS):
            dg = shifted[1 + 2 * q : 3 + 2 * q, :, 512 + CL : 1024].reshape(256, CG)
            acc_e = acc_e + dot_tn(tsum[layer, q], dg)
        for n in range(3):
            gwe[AT_E + n * HALF : AT_E + (n + 1) * HALF, :] = acc_e[:, n * 128 : (n + 1) * 128].astype(BF16)
        stage(0, layer, 0)
        swap_wait(0)

        def put(f, y):
            e2[f * 128 : (f + 1) * 128, :] = y

        rows_forward_into(0, put)
        mean2, inv2, gain2, bias2 = affine(layer, 1, FULL)
        scale2 = gain2 * inv2
        shift2 = bias2 - mean2 * scale2

        def slope_block(f, sums):
            rows = pl.ds(pl.multiple_of(f * 128, 128), 128)
            v = mixed[layer, rows, :]
            pre = v * scale2 + shift2
            sg = sigmoid(pre)
            e = e2[rows, :] * wide(qmask[rows, :], FULL) * (sg * (1.0 + pre * (1.0 - sg)))
            e2[rows, :] = e
            return sums[0] + fold(e), sums[1] + fold(e * ((v - mean2) * inv2))

        put_sums(1, *lax.fori_loop(0, 5, slope_block, (zero_of(FULL), zero_of(FULL))))
        sums_start(1)
        backward_window(step, 2)
        stage(1, layer + 2, 8)
        stage(1, layer + 1, 3)
        conv_back(0, 0)
        stage(0, layer, 1)
        stage(0, layer + 2, 7)
        conv_back(1, 0)
        one2, two2 = sums_wait(1, FULL)
        keep_grad_sums(layer, 1, FULL, one2, two2)
        part_a2 = one2 * wide(inv_ns, FULL)
        part_b2 = two2 * wide(inv_ns, FULL)

        def dq_block(f, carry):
            rows = pl.ds(pl.multiple_of(f * 128, 128), 128)
            z = (mixed[layer, rows, :] - mean2) * inv2
            dv = wide(qmask[rows, :], FULL) * scale2 * (e2[rows, :] - part_a2 - z * part_b2)
            dq[rows, :] = dv.astype(BF16)
            return carry

        lax.fori_loop(0, 5, dq_block, 0)
        e2[...] = dot_nt(dq[...], w_m[layer])
        rows_inverse_from(1, lambda f: e2[f * 128 : (f + 1) * 128, :])
        swap_start(1)
        conv_back(2, 0)
        stage(1, layer + 1, 4)
        backward_window(step, 3)
        conv_back(3, 0)
        pl.when(layer == 0)(lambda: stage(0, 0, 2))
        swap_wait(1)

        mean1, inv1, gain1, bias1 = affine(layer, 0, HALF)
        scale1 = gain1 * inv1
        shift1 = bias1 - mean1 * scale1

        def slope_in(h, sums):
            backs = width_back(1, h, tft)
            one, two = sums
            for o in range(2):
                q = 2 * h + o
                v = v1[layer, q]
                pre = v * scale1 + shift1
                sg = sigmoid(pre)
                e = (u[q] + backs[o]) * wide(pmask[q], HALF) * (sg * (1.0 + pre * (1.0 - sg)))
                u[q] = e
                one = one + fold(e)
                two = two + fold(e * ((v - mean1) * inv1))
            return one, two

        put_sums(0, *lax.fori_loop(0, 2, slope_in, (zero_of(HALF), zero_of(HALF))))
        sums_start(0)
        backward_window(step, 4)
        pl.when(layer > 0)(lambda: stage(0, layer, 2))
        pl.when(layer == 0)(lambda: stage(0, 0, 3))
        stage(0, layer + 1, 5)
        stage(0, layer + 2, 8)
        stage(1, layer + 1, QUICK_SIX)
        acc_m = jnp.zeros((FULL, FULL), F32)
        for f in range(5):
            rows = slice(f * 128, (f + 1) * 128)
            acc_m = acc_m + dot_tn(spec[layer, rows, :], dq[rows, :])
        for n in range(3):
            gwl[AT_M + n * FULL : AT_M + (n + 1) * FULL, :] = acc_m[:, n * 128 : (n + 1) * 128].astype(BF16)
        one1, two1 = sums_wait(0, HALF)
        keep_grad_sums(layer, 0, HALF, one1, two1)
        part_a1 = one1 * wide(inv_n, HALF)
        part_b1 = two1 * wide(inv_n, HALF)

        def ds_pair(q, carry):
            z = (v1[layer, q] - mean1) * inv1
            dv = wide(pmask[q], HALF) * scale1 * (u[q] - part_a1 - z * part_b1)
            low_dv = dv.astype(BF16)
            ds[q] = low_dv
            g[q, :, CL:] = g[q, :, CL:] + dot(low_dv, w_r[layer])
            return carry

        lax.fori_loop(0, PAIRS, ds_pair, 0)
        acc_r = jnp.zeros((HALF, CG), F32)
        for q in range(PAIRS):
            a = acts[layer, 2 * q : 2 * q + 2, :, CL:].reshape(256, CG)
            acc_r = acc_r + dot_tn(ds[q], a)
        for n in range(3):
            gwl[AT_R + n * HALF : AT_R + (n + 1) * HALF, :] = acc_r[:, n * 128 : (n + 1) * 128].astype(BF16)


        stage(1, layer, 0)

        @pl.when(lax.rem(layer, 2) == 0)
        def _():
            block = lax.div(layer, 2)

            def close_row(r, carry):
                q = lax.div(r, 2)
                here = pl.ds(pl.multiple_of(lax.rem(r, 2) * 128, 128), 128)
                x = (gblk[block, r].astype(F32) + g[q, here, :]) * wide(pmask[q, here, :], 512)
                low_x = x.astype(BF16)
                gblk[1 - block, r] = low_x
                g[q, here, :] = low_x.astype(F32)

                return carry

            lax.fori_loop(0, ROWS, close_row, 0)

        return carry

    lax.fori_loop(0, LAYERS, backward, 0)

    far = pltpu.make_async_remote_copy(
        stats.at[own], stats_far, sem_st.at[0], sem_st.at[1],
        device_id=across, device_id_type=MESH,
    )
    far.start()

    def push_last(first_row, rows):
        for row in range(first_row, first_row + rows):
            start_out(g_copies(0, row))

    stage(0, 0, 4)
    stage(1, 1, QUICK_SEVEN)
    push_last(0, 1)
    stage(1, 0, 1)
    stage(1, 0, 2)
    stage(1, 1, 7)
    stage(0, 1, 6)
    stage(1, 0, 3)
    push_last(1, 2)
    stage(0, 0, QUICK_SIX)
    stage(1, 0, 4)
    push_last(3, 5)
    stage(1, 1, 8)
    stage(0, 1, 7)
    stage(1, 0, QUICK_SIX)
    stage(0, 0, QUICK_SEVEN)
    stage(1, 0, QUICK_SEVEN)
    stage(0, 1, 8)
    stage(0, 0, 7)
    stage(1, 0, 7)
    stage(0, 0, 8)
    stage(1, 0, 8)
    for block in range(2):
        def sent(row, carry, block=block):
            wait_out(y_copies(block, row))
            wait_out(g_copies(block, row))
            return carry

        lax.fori_loop(0, ROWS, sent, 0)
    for m in range(2):
        sender = member(m, d)
        from_self = (sender[0] == s) & (sender[1] == d)

        def arrived(row, carry, m=m):
            for source, target, sems in ((acts, out_y, (sem_y_s, sem_y_r)), (gblk, out_g, (sem_g_s, sem_g_r))):
                pltpu.make_async_remote_copy(
                    source.at[0, row], target.at[m, row], sems[0].at[0, row], sems[1].at[m, row],
                    device_id=partner, device_id_type=MESH,
                ).wait_recv()
            return carry

        @pl.when(jnp.logical_not(from_self))
        def _(arrived=arrived):
            lax.fori_loop(0, ROWS, arrived, 0)

    far.wait()
    for lay in range(2):
        mine = stats[2 * s + lay]
        other = stats_far[lay]
        zero_first = jnp.where(grp == 0, mine, other)
        one_next = jnp.where(grp == 0, other, mine)
        row = slice(lay, lay + 1)

        def joined(st, base):
            return jnp.concatenate(
                [st[base : base + 1, :HALF], st[base + 1 : base + 2, :FULL], st[base + 2 : base + 3]], axis=1
            )

        mean = run_m[row, :]
        var = run_v[row, :]
        for m, st in enumerate((zero_first, one_next)):
            pixels = shapes[m, 0] * shapes[m, 1]
            points = shapes[m, 0] * (lax.div(shapes[m, 1], 2) + 1)
            fix = [
                wide(jnp.full((1, 128), count.astype(F32)) * inverse(count, 1), lanes)
                for count, lanes in ((pixels, HALF), (points, FULL), (pixels, 512))
            ]
            mean = (1.0 - MOMENTUM) * mean + MOMENTUM * joined(st, 0)
            var = (1.0 - MOMENTUM) * var + MOMENTUM * joined(st, 6) * jnp.concatenate(fix, axis=1)
        out_m[row, :] = mean
        out_v[row, :] = var
        out_biases[row, :] = joined(zero_first, 9) + joined(one_next, 9)
        out_gains[row, :] = joined(zero_first, 12) + joined(one_next, 12)


def tiles_of(rows, array):
    return jnp.concatenate([array[:, n * rows : (n + 1) * rows].astype(F32) for n in range(3)], axis=-1)


def on_band(
    inputs,
    cotangent,
    shapes,
    local_to_local,
    global_to_local,
    local_to_global,
    spec_reduce,
    spec_mix,
    spec_expand,
    norm_gains,
    norm_biases,
    run_means,
    run_vars,
):
    anywhere = pl.BlockSpec(memory_space=pl.ANY)
    vmem = pl.BlockSpec(memory_space=pltpu.VMEM)
    dma = pltpu.SemaphoreType.DMA
    band = (ROWS, LONG, 512)
    out_y, out_g, out_we, out_wl, *out_norms = pl.pallas_call(
        network_kernel,
        out_shape=(
            jax.ShapeDtypeStruct((2,) + band, BF16),
            jax.ShapeDtypeStruct((2,) + band, BF16),
            jax.ShapeDtypeStruct((4, PIECES * EARLY, 128), BF16),
            jax.ShapeDtypeStruct((4, PIECES * LATE, 128), BF16),
            *[jax.ShapeDtypeStruct((2, 3 * CS + 512), F32)] * 4,
        ),
        in_specs=[anywhere, anywhere, pl.BlockSpec(memory_space=pltpu.SMEM)]
        + [anywhere] * 8
        + [vmem] * 2,
        out_specs=(anywhere,) * 4 + (vmem,) * 4,
        scratch_shapes=[
            pltpu.VMEM((LAYERS, 9, CL, 512), BF16),
            pltpu.VMEM((LAYERS, 9, CG, CL), BF16),
            pltpu.VMEM((LAYERS, CS, CG), BF16),
            pltpu.VMEM((LAYERS, FULL, FULL), BF16),
            pltpu.VMEM((LAYERS, CS, CG), BF16),
            pltpu.VMEM((2, 2, 3 * CS + 512), F32),
            pltpu.VMEM((2, 2, 3 * CS + 512), F32),
            pltpu.VMEM((LAYERS, 8, 512), F32),
            pltpu.VMEM((LAYERS + 1,) + band, BF16),
            pltpu.VMEM((ROWS + 2, LONG, 1536), BF16),
            pltpu.VMEM((2, LONG, 512), BF16),
            pltpu.VMEM((LAYERS, PAIRS, 256, CS), F32),
            pltpu.VMEM((PAIRS, 256, CS), F32),
            pltpu.VMEM((LAYERS, SLOTS, FULL), BF16),
            pltpu.VMEM((LAYERS, SLOTS, FULL), F32),
            pltpu.VMEM((LAYERS, PAIRS, 256, CS), BF16),
            pltpu.VMEM((LAYERS, PAIRS, 256, 512), F32),
            pltpu.VMEM((PAIRS, 256, 128), F32),
            pltpu.VMEM((SLOTS, 128), F32),
            pltpu.VMEM((256, 256), BF16),
            pltpu.VMEM((256, 256), BF16),
            pltpu.VMEM((256, 256), BF16),
            pltpu.VMEM((256, 256), BF16),
            pltpu.VMEM((4, 256, 512), BF16),
            pltpu.VMEM((512, 1024), BF16),
            pltpu.VMEM((1024, FULL), BF16),
            pltpu.VMEM((SLOTS, FULL), F32),
            pltpu.VMEM((SLOTS, FULL), BF16),
            pltpu.VMEM((PAIRS, 256, CS), BF16),
            pltpu.VMEM((PAIRS, 256, 512), F32),
            pltpu.VMEM((2,) + band, BF16),
            pltpu.VMEM((512, ROWS * LONG), BF16),
            pltpu.VMEM((PIECES * EARLY, 128), BF16),
            pltpu.VMEM((PIECES * LATE, 128), BF16),
            pltpu.VMEM((PIECES * EARLY, 128), BF16),
            pltpu.VMEM((PIECES * LATE, 128), BF16),
            pltpu.VMEM((EARLY, 128), BF16),
            pltpu.VMEM((LATE, 128), BF16),
            pltpu.VMEM((4, 8, 128), F32),
            pltpu.VMEM((4, MEMBERS, 8, 128), F32),
            pltpu.VMEM((2, MEMBERS, 32, FULL), BF16),
            pltpu.VMEM((2, MEMBERS, 32, FULL), BF16),
            pltpu.VMEM((LAYERS, 16, 512), F32),
            pltpu.VMEM((2, 16, 512), F32),
            dma((3, 8)),
            dma((2, 2)),
            dma((ROWS, 2)),
            dma((2,)),
            dma((2,)),
            dma((4, MEMBERS)),
            dma((4, MEMBERS)),
            dma((2, MEMBERS)),
            dma((2, MEMBERS)),
            dma((2, ROWS)),
            dma((2, ROWS)),
            dma((2, ROWS)),
            dma((2, ROWS)),
            dma((2, 2, 8, 4)),
            dma((2, 2, 8, 4)),
            dma((2,)),
        ],
        compiler_params=pltpu.CompilerParams(
            collective_id=0, has_side_effects=True, vmem_limit_bytes=63 << 20
        ),
        name="network",
    )(
        inputs[:, 0],
        cotangent[:, 0],
        shapes,
        local_to_local[0],
        global_to_local[0],
        local_to_global[0],
        jnp.swapaxes(spec_reduce[0], 1, 2),
        spec_mix[0],
        spec_expand[0],
        norm_gains[0],
        norm_biases[0],
        run_means[0],
        run_vars[0],
    )
    grad_ll = out_we[2:, AT_LL:AT_GL].astype(F32).reshape(2, 9, CL, CL)
    grad_gl = out_we[2:, AT_GL:AT_KG].astype(F32).reshape(2, 9, CG, CL)
    grad_lift = tiles_of(9 * CL, out_we[2:, AT_KG:AT_E]).reshape(2, 9, CL, CG)
    grad_expand = tiles_of(CS, out_we[2:, AT_E:])
    grad_mix = tiles_of(FULL, out_wl[2:, AT_M:])
    grad_reduce = jnp.swapaxes(tiles_of(CS, out_wl[2:, AT_R:]), 1, 2)
    out_gains, out_biases, out_means, out_vars = out_norms
    return (
        out_y[None, :, None],
        out_g.astype(F32)[None, :, None],
        grad_ll[None],
        grad_gl[None],
        grad_lift[None],
        grad_reduce[None],
        grad_mix[None],
        grad_expand[None],
        out_gains[None],
        out_biases[None],
        out_means[None],
        out_vars[None],
    )


def solution(mesh):
    in_specs = (
        P(None, None, "dp", None, None),
        P(None, None, "dp", None, None),
        P(),
        P("section", None, None, None, None),
        P("section", None, None, None, None),
        P("section", None, None, None, None),
        P("section", None, None, None),
        P("section", None, None, None),
        P("section", None, None, None),
        P("section", None, None),
        P("section", None, None),
        P("section", None, None),
        P("section", None, None),
    )
    out_specs = (
        P("section", None, None, "dp", None, None),
        P("section", None, None, "dp", None, None),
        P("section", None, None, None, None),
        P("section", None, None, None, None),
        P("section", None, None, None, None),
        P("section", None, None, None),
        P("section", None, None, None),
        P("section", None, None, None),
        P("section", None, None),
        P("section", None, None),
        P("section", None, None),
        P("section", None, None),
    )
    dp_size = mesh.shape["dp"]
    banded = dp_size == MEMBERS and LONG == dp_size * ROWS
    return jax.shard_map(
        on_band if banded else on_device, mesh=mesh, in_specs=in_specs, out_specs=out_specs, check_vma=False
    )
```
